32 devices in a mesh: dp: 2 (over x), expert: 16 (over z, y, core).
Axes of the slice: x: 2, y: 2, z: 4, core: 2. Of those that a mesh axis runs over, the one named last changes fastest.
Arguments:
- tokens: bfloat16 [4096, 2048], P(('dp', 'expert')), may hold values from -6 to 6
- cotangent: bfloat16 [4096, 2048], P(('dp', 'expert')), may hold values from -6 to 6
- expert_ids: int32 [4096, 4], P(('dp', 'expert')), may hold values from 0 to 15, all different within a row; in each aligned block of 128 rows (0 to 127, 128 to 255, ...) at most 48 rows name the same one
- combine: float32 [4096, 4], P(('dp', 'expert')), may hold values from 0.1 to 1
- placement: int32 [16], replicated, may hold values from 0 to 15, each once
- moves: int32 [16], replicated, may hold values from 0 to 1, as said below
- w_gate: bfloat16 [16, 2048, 768], P('expert'), may hold values from -0.125 to 0.125
- w_up: bfloat16 [16, 2048, 768], P('expert'), may hold values from -0.125 to 0.125
- w_down: bfloat16 [16, 768, 2048], P('expert'), may hold values from -0.21875 to 0.21875
Outputs:
- mixed: bfloat16 [4096, 2048], P(('dp', 'expert'))
- input_grad: bfloat16 [4096, 2048], P(('dp', 'expert'))
- grad_gate: float32 [16, 2048, 768], P('expert', 'dp')
- grad_up: float32 [16, 2048, 768], P('expert', 'dp')
- grad_down: float32 [16, 768, 2048], P('expert', 'dp')
The draws below stay inside these ranges and needn't reach their ends.
Inputs may be any that keep to these rules, and one draw needn't show every extreme that they name: `expert_ids`: each row names 4 different experts. In the rows of one device no expert is named more than 48 times, a bound that some block reaches. `placement`: A permutation of the experts. moves[d] = moves[(d + 8) mod 16]; at least one pair exchanges and at least one does not.
All inputs are finite; a program needn't handle non-finite values.
Results may differ from the reference program's by a relative error of at most 0.0064.
Values may be sent and summed in bfloat16 or wider, within the bound.
No kernel may reach another device: no remote copies, remote signals or barrier semaphores. Data moves between devices by JAX's collectives and lax.ppermute only.
A program may use at most 192 MiB of HBM per device.

```python
import math
import jax
import jax.numpy as jnp
import numpy as np
from jax import lax

D = 2048
FF = 768
TOPK = 4
TOK_DEV = 128
EXPERTS = 16
CAP = 48
TOKENS = 4096
N_DP = 2


def draw_moves(key, part):
    half_count = EXPERTS // 2
    pair_bits = jax.random.randint(jax.random.fold_in(key, 11), (half_count,), 0, 2).astype(jnp.int32)
    pair_bits = pair_bits.at[0].set(1).at[1].set(0).at[half_count - 1].set(1)
    return jnp.concatenate([pair_bits, pair_bits]).astype(jnp.int32)


def block_levels(stream_key, shape, split, least, high):
    level = 1.0
    for dim, shards_of in split:
        draws = jax.random.uniform(jax.random.fold_in(jax.random.fold_in(stream_key, 6), dim), (shards_of,), jnp.float32, least / len(split), high / len(split))
        level = level * jnp.repeat(jnp.exp(draws), shape[dim] // shards_of).reshape((-1,) + (1,) * (len(shape) - 1 - dim))
    return level


def deal_out(key, own, number, rows, count, top, limit, skew):
    ranking = jax.random.permutation(key, count)
    crowded, ordinary = load_shares(count, rows * top, limit, skew, True), load_shares(count, rows * top, limit, skew, False)
    places = jnp.arange(count)

    def named(lengths, turn):
        used = int((lengths > 0).sum())
        fixed = max(1, used // 4)
        passed = fixed + (places - fixed + turn * (used - fixed)) % max(1, count - fixed)
        return jnp.zeros((count,), jnp.int32).at[ranking[jnp.where(places < fixed, places, passed)]].set(jnp.asarray(lengths, jnp.int32))

    lengths = jnp.where(number % 4 == 0, named(crowded, number // 4), named(ordinary, number - number // 4 - 1))
    mixed = jax.random.permutation(jax.random.fold_in(own, 3), count)
    giver, taker = mixed[0:count // 2 * 2:2], mixed[1:count // 2 * 2:2]
    room = jnp.minimum(lengths[giver] - 1, limit - lengths[taker]) // 2
    room = jnp.where((giver == ranking[0]) | (taker == ranking[0]) | (lengths[taker] == 0), 0, jnp.maximum(room, 0))
    passed = jax.random.randint(jax.random.fold_in(own, 4), (count // 2,), 0, 1 << 20) % (room + 1)
    lengths = lengths.at[giver].add(-passed).at[taker].add(passed)
    items = jnp.searchsorted(jnp.cumsum(lengths), jnp.arange(rows * top), side="right").astype(jnp.int32)
    listing = items.reshape(top, rows).T
    listing = listing[jax.random.permutation(jax.random.fold_in(own, 1), rows)]
    turn = jax.random.randint(jax.random.fold_in(own, 2), (rows, 1), 0, top)
    return jnp.take_along_axis(listing, (jnp.arange(top)[None, :] + turn) % top, axis=1)


def load_shares(count, total, most, slope, full):
    loads = [(1 << 20) // math.isqrt(grade ** slope) + 1 for grade in range(1, count + 1)]
    largest = most if full else min(most, max(-(-total // count), total * loads[0] // sum(loads)))
    least = 1 if total - largest >= count - 1 else 0
    holding, surplus = [largest] + [least] * (count - 1), total - largest - least * (count - 1)
    while surplus > 0:
        movable = [i for i in range(1, count) if holding[i] < largest] or [i for i in range(1, count) if holding[i] < most]
        mass, left = sum([loads[i] for i in movable]), surplus
        for i in movable:
            more = min(most - holding[i], max(1, left * loads[i] // mass), surplus)
            holding[i] = holding[i] + more
            surplus = surplus - more
    return np.array(holding)


def noise(rng, extent, deviation, limit, pieces=(), held_as=jnp.bfloat16):
    result = jax.random.normal(rng, extent, jnp.float32) * deviation
    if len(pieces) > 0:
        result = block_levels(rng, extent, pieces, -0.22, 0.18) * result
    return jnp.clip(result, min=-limit, max=limit).astype(held_as)


def setup_inputs(seed: int = 0) -> dict:
    splits = jax.random.split(jax.random.key(seed), 10)
    tokens = noise(splits[0], (TOKENS, D), 1.0, 6.0, ((0, 32),))
    cotangent = noise(splits[1], (TOKENS, D), 1.0, 6.0, ((0, 32),))
    expert_ids_keys = jax.random.split(jax.random.fold_in(splits[2], 1), TOKENS // TOK_DEV)
    expert_ids_turns = jax.random.permutation(jax.random.fold_in(splits[2], 3), TOKENS // TOK_DEV)
    expert_ids = jax.vmap(lambda own, number: deal_out(jax.random.fold_in(splits[2], 2), own, number, TOK_DEV, EXPERTS, TOPK, CAP, 2))(expert_ids_keys, expert_ids_turns).reshape((TOKENS, TOPK))
    combine = jnp.clip(jnp.exp(math.log(1.0) - 2.3025851 * jax.random.uniform(splits[3], (TOKENS, TOPK), jnp.float32) ** block_levels(splits[3], (TOKENS, TOPK), ((0, 32),), -0.2, 0.2)), 0.1, 1.0)
    placement = jax.random.permutation(splits[4], EXPERTS).astype(jnp.int32)
    moves = draw_moves(jax.random.fold_in(splits[9], 71), 0)
    w_gate = noise(splits[6], (EXPERTS, D, FF), D ** -0.5, 0.125, ((0, 16),))
    w_up = noise(splits[7], (EXPERTS, D, FF), D ** -0.5, 0.125, ((0, 16),))
    w_down = noise(splits[8], (EXPERTS, FF, D), FF ** -0.5, 0.21875, ((0, 16),))
    return {"tokens": tokens, "cotangent": cotangent, "expert_ids": expert_ids, "combine": combine, "placement": placement, "moves": moves, "w_gate": w_gate, "w_up": w_up, "w_down": w_down}


def reference(tokens, cotangent, expert_ids, combine, placement, moves, w_gate, w_up, w_down):
    slot_ids = jnp.arange(EXPERTS, dtype=jnp.int32)
    held_expert = jnp.where(moves == 1, jnp.roll(placement, EXPERTS // 2), placement)
    home_slots = jnp.zeros((EXPERTS,), jnp.int32).at[placement].set(slot_ids)
    flat_ids = expert_ids.reshape(-1)
    flat_weights = combine.reshape(-1)
    token_of = (jnp.arange(TOKENS * TOPK, dtype=jnp.int32) // TOPK).astype(jnp.int32)
    max_rows = CAP * (TOKENS // TOK_DEV)
    contract_rows = (((0,), (0,)), ((), ()))
    contract_last = (((1,), (1,)), ((), ()))

    def per_expert(carry, expert):
        mixed_acc, grad_acc = carry
        chosen = flat_ids == expert
        hits = jnp.nonzero(chosen, size=max_rows, fill_value=0)[0].astype(jnp.int32)
        live_rows = (jnp.arange(max_rows, dtype=jnp.int32) < jnp.sum(chosen.astype(jnp.int32))).astype(jnp.float32)
        row_index = token_of[hits]
        row_inputs = tokens[row_index]
        row_weights = flat_weights[hits] * live_rows
        out_grad = (row_weights[:, None] * cotangent[row_index].astype(jnp.float32)).astype(jnp.bfloat16)
        home_slot = home_slots[expert]
        gate_weight = w_gate[home_slot]
        up_weight = w_up[home_slot]
        down_weight = w_down[home_slot]
        gate_pre = jnp.dot(row_inputs, gate_weight, preferred_element_type=jnp.float32)
        up_pre = jnp.dot(row_inputs, up_weight, preferred_element_type=jnp.float32)
        sigma = jax.nn.sigmoid(gate_pre)
        hidden = (gate_pre * sigma * up_pre).astype(jnp.bfloat16)
        expert_out = jnp.dot(hidden, down_weight, preferred_element_type=jnp.float32).astype(jnp.bfloat16)
        mixed_acc = mixed_acc.at[row_index].add(row_weights[:, None] * expert_out.astype(jnp.float32))
        hidden_grad = lax.dot_general(out_grad, down_weight, contract_last, preferred_element_type=jnp.float32)
        gate_grad = (hidden_grad * up_pre * sigma * (1.0 + gate_pre * (1.0 - sigma))).astype(jnp.bfloat16)
        up_grad = (hidden_grad * gate_pre * sigma).astype(jnp.bfloat16)
        row_grad = (lax.dot_general(gate_grad, gate_weight, contract_last, preferred_element_type=jnp.float32)
                    + lax.dot_general(up_grad, up_weight, contract_last, preferred_element_type=jnp.float32)).astype(jnp.bfloat16)
        grad_acc = grad_acc.at[row_index].add(live_rows[:, None] * row_grad.astype(jnp.float32))
        g_gate = lax.dot_general(row_inputs, gate_grad, contract_rows, preferred_element_type=jnp.float32)
        g_up = lax.dot_general(row_inputs, up_grad, contract_rows, preferred_element_type=jnp.float32)
        g_down = lax.dot_general(hidden, out_grad, contract_rows, preferred_element_type=jnp.float32)
        return (mixed_acc, grad_acc), (g_gate, g_up, g_down)

    start = (jnp.zeros((TOKENS, D), jnp.float32), jnp.zeros((TOKENS, D), jnp.float32))
    (mixed_acc, grad_acc), (all_gate, all_up, all_down) = lax.scan(per_expert, start, slot_ids)
    scale = 1.0 / N_DP
    grad_gate = jnp.take(all_gate, held_expert, axis=0) * scale
    grad_up = jnp.take(all_up, held_expert, axis=0) * scale
    grad_down = jnp.take(all_down, held_expert, axis=0) * scale
    return (mixed_acc.astype(jnp.bfloat16), grad_acc.astype(jnp.bfloat16), grad_gate, grad_up, grad_down)
```

```python
import jax
import jax.numpy as jnp
from jax import lax
from jax.sharding import PartitionSpec as P

CONTRACT_ROWS = (((0,), (0,)), ((), ()))
CONTRACT_LAST = (((1,), (1,)), ((), ()))


def dot_f32(a, b, dims=(((1,), (0,)), ((), ()))):
    return lax.dot_general(a, b, dims, preferred_element_type=jnp.float32)


def selector(ids, weights, expert, row_count):
    match = ids == expert.astype(ids.dtype)
    hit = jnp.any(match, axis=1)
    weight = jnp.sum(jnp.where(match, weights, 0.0), axis=1)
    rank = jnp.where(hit, jnp.cumsum(hit.astype(jnp.int32)) - 1, -1)
    chosen = rank[None, :] == jnp.arange(row_count, dtype=jnp.int32)[:, None]
    row_weight = jnp.sum(jnp.where(chosen, weight[None, :], 0.0), axis=1)
    return chosen.astype(jnp.bfloat16), row_weight[:, None]


def body(tokens, cotangent, expert_ids, combine, placement, moves, w_gate, w_up, w_down):
    owner_count = lax.axis_size("expert")
    dp_count = lax.axis_size("dp")
    my_index = lax.axis_index("expert")
    my_dp = lax.axis_index("dp")
    tok_rows, width = tokens.shape
    choose_count = expert_ids.shape[1]
    ff = w_gate.shape[2]
    row_count = 3 * tok_rows * choose_count // 2
    pair = owner_count // 2
    swap_pair = [(i, i ^ pair) for i in range(owner_count)]
    swap_dp = [(i, i ^ 1) for i in range(dp_count)]

    slot_ids = jnp.arange(owner_count, dtype=jnp.int32)
    mine = slot_ids == my_index
    home_expert = jnp.sum(jnp.where(mine, placement, 0))
    held = jnp.where(moves == 1, jnp.roll(placement, pair), placement)
    held_expert = jnp.sum(jnp.where(mine, held, 0))
    moved = jnp.sum(jnp.where(mine, moves, 0)) == 1

    routing = jnp.concatenate([expert_ids.astype(jnp.float32), combine], axis=1)
    routing = lax.all_gather(routing, "expert", axis=0, tiled=True)
    ids, weights = routing[:, :choose_count], routing[:, choose_count:]
    all_tokens = lax.all_gather(tokens, "expert", axis=0, tiled=True)
    all_cots = lax.all_gather(cotangent, "expert", axis=0, tiled=True)

    def pick(expert):
        chosen, row_weight = selector(ids, weights, expert, row_count)
        rows = dot_f32(chosen, all_tokens).astype(jnp.bfloat16)
        cots = dot_f32(chosen, all_cots)
        out_grad = (row_weight * cots).astype(jnp.bfloat16)
        return chosen, row_weight, rows, out_grad

    chosen, row_weight, rows, out_grad = pick(home_expert)
    gate_pre = dot_f32(rows, w_gate[0])
    up_pre = dot_f32(rows, w_up[0])
    sigma = jax.nn.sigmoid(gate_pre)
    hidden = (gate_pre * sigma * up_pre).astype(jnp.bfloat16)
    moved_hidden = lax.ppermute(hidden, "expert", swap_pair)
    expert_out = dot_f32(hidden, w_down[0])
    hidden_grad = dot_f32(out_grad, w_down[0], CONTRACT_LAST)
    gate_grad = (hidden_grad * up_pre * sigma * (1.0 + gate_pre * (1.0 - sigma))).astype(
        jnp.bfloat16
    )
    up_grad = (hidden_grad * gate_pre * sigma).astype(jnp.bfloat16)
    moved_gate = lax.ppermute(gate_grad, "expert", swap_pair)
    moved_up = lax.ppermute(up_grad, "expert", swap_pair)
    row_grad = dot_f32(gate_grad, w_gate[0], CONTRACT_LAST) + dot_f32(
        up_grad, w_up[0], CONTRACT_LAST
    )

    def give_back(values):
        spread = dot_f32(chosen, values.astype(jnp.bfloat16), CONTRACT_ROWS).astype(jnp.bfloat16)
        return lax.psum_scatter(spread, "expert", scatter_dimension=0, tiled=True)

    mixed = give_back(row_weight * expert_out)
    input_grad = give_back(row_grad)

    _, _, held_rows, held_out_grad = pick(held_expert)
    hidden = jnp.where(moved, moved_hidden, hidden)
    gate_grad = jnp.where(moved, moved_gate, gate_grad)
    up_grad = jnp.where(moved, moved_up, up_grad)

    def weight_grad(left, right):
        share = left.shape[1] // dp_count
        halves = [
            lax.dynamic_slice_in_dim(left, part * share, share, axis=1)
            for part in ((my_dp + 1) % dp_count, my_dp)
        ]
        sent = dot_f32(halves[0], right, CONTRACT_ROWS).astype(jnp.bfloat16)
        got = lax.ppermute(sent, "dp", swap_dp)
        kept = dot_f32(halves[1], right, CONTRACT_ROWS)
        return ((kept + got.astype(jnp.float32)) * (1.0 / dp_count))[None]

    return (
        mixed,
        input_grad,
        weight_grad(held_rows, gate_grad),
        weight_grad(held_rows, up_grad),
        weight_grad(hidden, held_out_grad),
    )


def solution(mesh):
    tokens = P(("dp", "expert"), None)
    slots = P("expert", None, None)
    grads = P("expert", "dp", None)
    return jax.shard_map(
        body,
        mesh=mesh,
        in_specs=(tokens, tokens, tokens, tokens, P(), P(), slots, slots, slots),
        out_specs=(tokens, tokens, grads, grads, grads),
        check_vma=False,
    )
```

```python
import jax
import jax.numpy as jnp
from jax import lax
from jax.sharding import PartitionSpec as P

CONTRACT_ROWS = (((0,), (0,)), ((), ()))
CONTRACT_LAST = (((1,), (1,)), ((), ()))
PLANE = 4


def dot_f32(a, b, dims=(((1,), (0,)), ((), ()))):
    return lax.dot_general(a, b, dims, preferred_element_type=jnp.float32)


def crossed(array, axis, flip):
    return lax.ppermute(array, axis, [(i, i ^ flip) for i in range(lax.axis_size(axis))])


def layer_gather(block, layers):
    return [block] + [crossed(block, "expert", j * PLANE) for j in range(1, layers)]


def plane_swap(pieces):
    return jnp.concatenate([pieces[0]] + [crossed(pieces[k], "expert", k) for k in range(1, PLANE)])


def selector(ids, weights, experts, own_layer, layers, row_count):
    match = ids[None] == experts[:, None, None].astype(ids.dtype)
    hit = jnp.any(match, axis=2)
    weight = jnp.sum(jnp.where(match, weights[None], 0.0), axis=2)
    count = hit.astype(jnp.int32).reshape(PLANE, layers, -1)
    within = jnp.cumsum(count, axis=2) - count
    layer = jnp.arange(layers, dtype=jnp.int32) ^ own_layer
    ahead = layer[:, None] < layer[None, :]
    before = jnp.sum(jnp.where(ahead[None], jnp.sum(count, axis=2)[:, :, None], 0), axis=1)
    rank = (within + before[:, :, None]).reshape(PLANE, 1, -1)
    rank = jnp.where(hit[:, None, :], rank, -1)
    chosen = rank == jnp.arange(row_count, dtype=jnp.int32)[None, :, None]
    row_weight = jnp.sum(jnp.where(chosen, weight[:, None, :], 0.0), axis=2)
    rows = PLANE * row_count
    return chosen.astype(jnp.bfloat16).reshape(rows, -1), row_weight.reshape(rows, 1)


def body(tokens, cotangent, expert_ids, combine, placement, moves, w_gate, w_up, w_down):
    owner_count = lax.axis_size("expert")
    dp_count = lax.axis_size("dp")
    my_index = lax.axis_index("expert")
    my_dp = lax.axis_index("dp")
    tok_rows, width = tokens.shape
    choose_count = expert_ids.shape[1]
    layers = owner_count // PLANE
    row_count = 3 * tok_rows * choose_count // (2 * PLANE)
    pair = owner_count // 2

    slot_ids = jnp.arange(owner_count, dtype=jnp.int32)
    near = slot_ids[None, :] == (my_index ^ jnp.arange(PLANE, dtype=jnp.int32))[:, None]
    held = jnp.where(moves == 1, jnp.roll(placement, pair), placement)
    home_experts = jnp.sum(jnp.where(near, placement[None], 0), axis=1)
    held_experts = jnp.sum(jnp.where(near, held[None], 0), axis=1)
    moved = jnp.sum(jnp.where(near[0], moves, 0)) == 1

    routing = jnp.concatenate([expert_ids.astype(jnp.float32), combine], axis=1)
    routing = jnp.concatenate(layer_gather(routing, layers))
    ids, weights = routing[:, :choose_count], routing[:, choose_count:]
    near_tokens = jnp.concatenate(layer_gather(tokens, layers))
    near_cots = jnp.concatenate(layer_gather(cotangent, layers))

    def pick(experts):
        return selector(ids, weights, experts, my_index // PLANE, layers, row_count)

    def pieces(array):
        return [array[k * row_count : (k + 1) * row_count] for k in range(PLANE)]

    def send_rows(chosen):
        return plane_swap(pieces(dot_f32(chosen, near_tokens).astype(jnp.bfloat16)))

    def send_grads(chosen, row_weight):
        return plane_swap(pieces((row_weight * dot_f32(chosen, near_cots)).astype(jnp.bfloat16)))

    chosen, row_weight = pick(home_experts)
    rows = send_rows(chosen)
    out_grad = send_grads(chosen, row_weight)
    held_chosen, held_weight = pick(held_experts)
    held_rows = send_rows(held_chosen)
    held_out_grad = send_grads(held_chosen, held_weight)

    gate_pre = dot_f32(rows, w_gate[0])
    up_pre = dot_f32(rows, w_up[0])
    sigma = jax.nn.sigmoid(gate_pre)
    hidden = (gate_pre * sigma * up_pre).astype(jnp.bfloat16)
    moved_hidden = crossed(hidden, "expert", pair)
    expert_out = dot_f32(hidden, w_down[0])
    hidden_grad = dot_f32(out_grad, w_down[0], CONTRACT_LAST)
    gate_grad = (hidden_grad * up_pre * sigma * (1.0 + gate_pre * (1.0 - sigma))).astype(
        jnp.bfloat16
    )
    up_grad = (hidden_grad * gate_pre * sigma).astype(jnp.bfloat16)
    moved_gate = crossed(gate_grad, "expert", pair)
    moved_up = crossed(up_grad, "expert", pair)
    row_grad = dot_f32(gate_grad, w_gate[0], CONTRACT_LAST) + dot_f32(
        up_grad, w_up[0], CONTRACT_LAST
    )

    def give_back(values, scale):
        back = plane_swap(pieces(values.astype(jnp.bfloat16)))
        if scale is not None:
            back = (scale * back.astype(jnp.float32)).astype(jnp.bfloat16)
        spread = dot_f32(chosen, back, CONTRACT_ROWS).astype(jnp.bfloat16)
        total = spread[:tok_rows].astype(jnp.float32)
        for j in range(1, layers):
            block = crossed(spread[j * tok_rows : (j + 1) * tok_rows], "expert", j * PLANE)
            total = total + block.astype(jnp.float32)
        return total.astype(jnp.bfloat16)

    mixed = give_back(expert_out, row_weight)
    input_grad = give_back(row_grad, None)

    hidden = jnp.where(moved, moved_hidden, hidden)
    gate_grad = jnp.where(moved, moved_gate, gate_grad)
    up_grad = jnp.where(moved, moved_up, up_grad)

    def weight_grad(left, right):
        share = left.shape[1] // dp_count
        halves = [
            lax.dynamic_slice_in_dim(left, part * share, share, axis=1)
            for part in ((my_dp + 1) % dp_count, my_dp)
        ]
        sent = dot_f32(halves[0], right, CONTRACT_ROWS).astype(jnp.bfloat16)
        got = crossed(sent, "dp", 1)
        kept = dot_f32(halves[1], right, CONTRACT_ROWS)
        return ((kept + got.astype(jnp.float32)) * (1.0 / dp_count))[None]

    return (
        mixed,
        input_grad,
        weight_grad(held_rows, gate_grad),
        weight_grad(held_rows, up_grad),
        weight_grad(hidden, held_out_grad),
    )


def solution(mesh):
    tokens = P(("dp", "expert"), None)
    slots = P("expert", None, None)
    grads = P("expert", "dp", None)
    return jax.shard_map(
        body,
        mesh=mesh,
        in_specs=(tokens, tokens, tokens, tokens, P(), P(), slots, slots, slots),
        out_specs=(tokens, tokens, grads, grads, grads),
        check_vma=False,
    )
```

```python
import jax
import jax.numpy as jnp
from jax import lax
from jax.sharding import PartitionSpec as P

CONTRACT_ROWS = (((0,), (0,)), ((), ()))
CONTRACT_LAST = (((1,), (1,)), ((), ()))
PLANE = 4


def dot_f32(a, b, dims=(((1,), (0,)), ((), ()))):
    return lax.dot_general(a, b, dims, preferred_element_type=jnp.float32)


def crossed(array, axis, flip):
    return lax.ppermute(array, axis, [(i, i ^ flip) for i in range(lax.axis_size(axis))])


def after(array, *earlier):
    return lax.optimization_barrier((array,) + earlier)[0]


def along(array, pairs):
    return lax.ppermute(array, "expert", pairs)


def line_pairs(owner_count):
    inner = [i for i in range(owner_count) if i // PLANE in (1, 2)]
    middle = [(i, i ^ 3 * PLANE) for i in inner]
    outward = [(i, i ^ PLANE) for i in inner]
    inward = [(i ^ PLANE, i) for i in inner]
    return middle, outward, inward


def layer_order(own_layer, layers):
    if layers != 4:
        return own_layer ^ jnp.arange(layers, dtype=jnp.int32)
    low = own_layer < 2
    return jnp.stack([own_layer, own_layer ^ 1, jnp.where(low, 2, 1), jnp.where(low, 3, 0)])


def layer_gather(block, own_layer, layers):
    if layers != 4:
        got = [block] + [crossed(block, "expert", j * PLANE) for j in range(1, layers)]
        return jnp.concatenate(got), got[-1]
    middle, outward, _ = line_pairs(layers * PLANE)
    inner = (own_layer == 1) | (own_layer == 2)
    near = crossed(block, "expert", PLANE)
    far = [along(block, middle), along(near, middle)]
    relayed = [along(array, outward) for array in far]
    far_blocks = [jnp.where(inner, a, b) for a, b in zip(far, relayed)]
    return jnp.concatenate([block, near] + far_blocks), far[1]


def layer_reduce(spread, own_layer, layers, earlier):
    rows = spread.shape[0] // layers
    total = spread[:rows].astype(jnp.float32)
    if layers != 4:
        for j in range(1, layers):
            block = crossed(spread[j * rows : (j + 1) * rows], "expert", j * PLANE)
            total = total + block.astype(jnp.float32)
        return total.astype(jnp.bfloat16)
    middle, outward, inward = line_pairs(layers * PLANE)
    far = spread[2 * rows :]
    far_sum = (far.astype(jnp.float32) + along(far, inward).astype(jnp.float32)).astype(far.dtype)
    near = spread[rows : 2 * rows]
    near_in = along(near, inward)
    got = along(after(far_sum, *earlier), middle)
    near_sum = (near.astype(jnp.float32) + got[rows:].astype(jnp.float32)).astype(far.dtype)
    near_out = along(near_sum, outward)
    for block in (near_in, got[:rows], near_out):
        total = total + block.astype(jnp.float32)
    return total.astype(jnp.bfloat16)


def plane_swap(pieces):
    return jnp.concatenate([pieces[0]] + [crossed(pieces[k], "expert", k) for k in range(1, PLANE)])


def selector(ids, weights, experts, layer, row_count):
    layers = layer.shape[0]
    match = ids[None] == experts[:, None, None].astype(ids.dtype)
    hit = jnp.any(match, axis=2)
    weight = jnp.sum(jnp.where(match, weights[None], 0.0), axis=2)
    count = hit.astype(jnp.int32).reshape(PLANE, layers, -1)
    within = jnp.cumsum(count, axis=2) - count
    ahead = layer[:, None] < layer[None, :]
    before = jnp.sum(jnp.where(ahead[None], jnp.sum(count, axis=2)[:, :, None], 0), axis=1)
    rank = (within + before[:, :, None]).reshape(PLANE, 1, -1)
    rank = jnp.where(hit[:, None, :], rank, -1)
    chosen = rank == jnp.arange(row_count, dtype=jnp.int32)[None, :, None]
    row_weight = jnp.sum(jnp.where(chosen, weight[:, None, :], 0.0), axis=2)
    rows = PLANE * row_count
    return chosen.astype(jnp.bfloat16).reshape(rows, -1), row_weight.reshape(rows, 1)


def body(tokens, cotangent, expert_ids, combine, placement, moves, w_gate, w_up, w_down):
    owner_count = lax.axis_size("expert")
    dp_count = lax.axis_size("dp")
    my_index = lax.axis_index("expert")
    my_dp = lax.axis_index("dp")
    tok_rows, width = tokens.shape
    choose_count = expert_ids.shape[1]
    layers = owner_count // PLANE
    row_count = 3 * tok_rows * choose_count // (2 * PLANE)
    pair = owner_count // 2

    slot_ids = jnp.arange(owner_count, dtype=jnp.int32)
    near = slot_ids[None, :] == (my_index ^ jnp.arange(PLANE, dtype=jnp.int32))[:, None]
    held = jnp.where(moves == 1, jnp.roll(placement, pair), placement)
    home_experts = jnp.sum(jnp.where(near, placement[None], 0), axis=1)
    held_experts = jnp.sum(jnp.where(near, held[None], 0), axis=1)
    moved = jnp.sum(jnp.where(near[0], moves, 0)) == 1

    routing = jnp.concatenate([expert_ids.astype(jnp.float32), combine], axis=1)
    own_layer = my_index // PLANE
    order = layer_order(own_layer, layers)
    routing = [routing] + [crossed(routing, "expert", j * PLANE) for j in range(1, layers)]
    routing = jnp.stack(routing)[order ^ own_layer].reshape(layers * tok_rows, -1)
    ids, weights = routing[:, :choose_count], routing[:, choose_count:]
    near_tokens, sign = layer_gather(tokens, own_layer, layers)
    near_cots, _ = layer_gather(after(cotangent, sign), own_layer, layers)

    def pick(experts):
        return selector(ids, weights, experts, order, row_count)

    def pieces(array):
        return [array[k * row_count : (k + 1) * row_count] for k in range(PLANE)]

    def send_rows(chosen):
        return plane_swap(pieces(dot_f32(chosen, near_tokens).astype(jnp.bfloat16)))

    def send_grads(chosen, row_weight):
        return plane_swap(pieces((row_weight * dot_f32(chosen, near_cots)).astype(jnp.bfloat16)))

    chosen, row_weight = pick(home_experts)
    rows = send_rows(chosen)
    out_grad = send_grads(chosen, row_weight)
    held_chosen, held_weight = pick(held_experts)
    held_out_grad = send_grads(after(held_chosen, out_grad), held_weight)
    held_rows = send_rows(after(held_chosen, held_out_grad))

    gate_pre = dot_f32(rows, w_gate[0])
    up_pre = dot_f32(rows, w_up[0])
    sigma = jax.nn.sigmoid(gate_pre)
    hidden = (gate_pre * sigma * up_pre).astype(jnp.bfloat16)
    moved_hidden = crossed(hidden, "expert", pair)
    expert_out = dot_f32(hidden, w_down[0])
    hidden_grad = dot_f32(out_grad, w_down[0], CONTRACT_LAST)
    gate_grad = (hidden_grad * up_pre * sigma * (1.0 + gate_pre * (1.0 - sigma))).astype(
        jnp.bfloat16
    )
    up_grad = (hidden_grad * gate_pre * sigma).astype(jnp.bfloat16)
    moved_gate = crossed(gate_grad, "expert", pair)
    moved_up = crossed(up_grad, "expert", pair)
    row_grad = dot_f32(gate_grad, w_gate[0], CONTRACT_LAST) + dot_f32(
        up_grad, w_up[0], CONTRACT_LAST
    )

    def give_back(values, scale):
        back = plane_swap(pieces(values.astype(jnp.bfloat16)))
        if scale is not None:
            back = (scale * back.astype(jnp.float32)).astype(jnp.bfloat16)
        spread = dot_f32(chosen, back, CONTRACT_ROWS).astype(jnp.bfloat16)
        return layer_reduce(spread, own_layer, layers, (moved_gate, moved_up))

    mixed = give_back(expert_out, row_weight)
    input_grad = give_back(row_grad, None)

    hidden = jnp.where(moved, moved_hidden, hidden)
    gate_grad = jnp.where(moved, moved_gate, gate_grad)
    up_grad = jnp.where(moved, moved_up, up_grad)

    def weight_grad(left, right):
        share = left.shape[1] // dp_count
        halves = [
            lax.dynamic_slice_in_dim(left, part * share, share, axis=1)
            for part in ((my_dp + 1) % dp_count, my_dp)
        ]
        sent = dot_f32(halves[0], right, CONTRACT_ROWS).astype(jnp.bfloat16)
        got = crossed(sent, "dp", 1)
        kept = dot_f32(halves[1], right, CONTRACT_ROWS)
        return ((kept + got.astype(jnp.float32)) * (1.0 / dp_count))[None]

    return (
        mixed,
        input_grad,
        weight_grad(held_rows, gate_grad),
        weight_grad(held_rows, up_grad),
        weight_grad(hidden, held_out_grad),
    )


def solution(mesh):
    tokens = P(("dp", "expert"), None)
    slots = P("expert", None, None)
    grads = P("expert", "dp", None)
    return jax.shard_map(
        body,
        mesh=mesh,
        in_specs=(tokens, tokens, tokens, tokens, P(), P(), slots, slots, slots),
        out_specs=(tokens, tokens, grads, grads, grads),
        check_vma=False,
    )
```

```python
import jax
import jax.numpy as jnp
from jax import lax
from jax.experimental import pallas as pl
from jax.experimental.pallas import tpu as pltpu
from jax.sharding import PartitionSpec as P

CONTRACT_ROWS = (((0,), (0,)), ((), ()))
CONTRACT_LAST = (((1,), (1,)), ((), ()))
PLANE = 4
FF_TILE = 256
VMEM_BYTES = 40 * 1024 * 1024


def dot_f32(a, b, dims=(((1,), (0,)), ((), ()))):
    return lax.dot_general(a, b, dims, preferred_element_type=jnp.float32)


def crossed(array, axis, flip):
    return lax.ppermute(array, axis, [(i, i ^ flip) for i in range(lax.axis_size(axis))])


def along(array, pairs):
    return lax.ppermute(array, "expert", pairs)


def line_pairs(owner_count):
    inner = [i for i in range(owner_count) if i // PLANE in (1, 2)]
    middle = [(i, i ^ 3 * PLANE) for i in inner]
    outward = [(i, i ^ PLANE) for i in inner]
    inward = [(i ^ PLANE, i) for i in inner]
    return middle, outward, inward


def layer_gather(block, inner, layers):
    if layers != 4:
        got = [block] + [crossed(block, "expert", j * PLANE) for j in range(1, layers)]
        return jnp.concatenate(got[: layers // 2]), jnp.concatenate(got[layers // 2 :])
    middle, outward, _ = line_pairs(layers * PLANE)
    near = crossed(block, "expert", PLANE)
    far = [along(block, middle), along(near, middle)]
    relayed = [along(array, outward) for array in far]
    far_half = jnp.where(inner, jnp.concatenate(far), jnp.concatenate(relayed))
    return jnp.concatenate([block, near]), far_half


def plane_gather(half):
    mine = jnp.stack([half, crossed(half, "expert", 2)])
    return mine, crossed(mine, "expert", 1)


def layer_reduce(own, far, tok_rows, layers):
    total = own[:tok_rows].astype(jnp.float32)
    if layers != 4:
        spread = jnp.concatenate([own, far])
        for j in range(1, layers):
            block = crossed(spread[j * tok_rows : (j + 1) * tok_rows], "expert", j * PLANE)
            total = total + block.astype(jnp.float32)
        return total.astype(jnp.bfloat16)
    middle, outward, inward = line_pairs(layers * PLANE)
    far_sum = (far.astype(jnp.float32) + along(far, inward).astype(jnp.float32)).astype(far.dtype)
    near = own[tok_rows:]
    near_in = along(near, inward)
    got = along(far_sum, middle)
    near_sum = (near.astype(jnp.float32) + got[tok_rows:].astype(jnp.float32)).astype(far.dtype)
    near_out = along(near_sum, outward)
    for block in (near_in, got[:tok_rows], near_out):
        total = total + block.astype(jnp.float32)
    return total.astype(jnp.bfloat16)


def rank_rows(hit, order, layers):
    half = layers // 2
    tok_rows = hit.shape[2]
    earlier = jnp.arange(tok_rows)[:, None] < jnp.arange(tok_rows)[None, :]
    within = jnp.einsum(
        "slt,tu->slu",
        hit.astype(jnp.bfloat16),
        earlier.astype(jnp.bfloat16),
        preferred_element_type=jnp.float32,
    ).astype(jnp.int32)
    count = jnp.sum(hit.astype(jnp.int32), axis=2)
    side = jnp.arange(layers) // half
    ahead = (order[:, None] < order[None, :]) & (side[:, None] == side[None, :])
    before = jnp.sum(jnp.where(ahead[None], count[:, :, None], 0), axis=1)
    return jnp.where(hit, within + before[:, :, None], -1)


def pick_rows(rank, source, row_count):
    place = lax.broadcasted_iota(jnp.int32, (row_count, rank.shape[1]), 0)
    chosen = place == rank
    one_hot = jnp.where(chosen, 1.0, 0.0).astype(jnp.bfloat16)
    return chosen, dot_f32(one_hot, source)


def pick_step(step, slot, rank_ref, weight_ref, mine_ref, other_ref, store, row_count):
    def stored(source_ref):
        chosen, rows = pick_rows(rank_ref[0], source_ref[0], row_count)
        if weight_ref is not None:
            picked = jnp.where(chosen, weight_ref[0], 0.0)
            rows = rows * jnp.sum(picked, axis=1, keepdims=True)
        store(slot, rows.astype(jnp.bfloat16))

    @pl.when(step < 2)
    def _():
        stored(mine_ref)

    @pl.when((step >= 2) & (step < PLANE))
    def _():
        stored(other_ref)


def source_xor(step):
    return (step // 2) + 2 * (step % 2)


def slot_of(step, place_ref):
    return place_ref[0] ^ source_xor(jnp.minimum(step, PLANE - 1))


def source_specs(tokens, width, weighted):
    line = pl.BlockSpec((1, 1, tokens), lambda i, p: (source_xor(jnp.minimum(i, PLANE - 1)), 0, 0))
    mine = pl.BlockSpec((1, tokens, width), lambda i, p: (jnp.minimum(i, 1), 0, 0))
    other = pl.BlockSpec((1, tokens, width), lambda i, p: (jnp.clip(i - 2, 0, 1), 0, 0))
    return [line] * (2 if weighted else 1) + [mine, other]


def run(kernel, grid, in_specs, out_specs, out_shape, scratch, flops, args):
    moved = sum(a.size * a.dtype.itemsize for a in args)
    return pl.pallas_call(
        kernel,
        grid_spec=pltpu.PrefetchScalarGridSpec(
            num_scalar_prefetch=1,
            grid=(grid,),
            in_specs=in_specs,
            out_specs=out_specs,
            scratch_shapes=scratch,
        ),
        out_shape=out_shape,
        compiler_params=pltpu.CompilerParams(vmem_limit_bytes=VMEM_BYTES),
        cost_estimate=pl.CostEstimate(flops=flops, bytes_accessed=moved, transcendentals=0),
    )(*args)


def pick(place, rank, weight, mine, other, row_count):
    _, tokens, width = mine.shape
    weighted = weight is not None

    def kernel(place_ref, rank_ref, *refs):
        weight_ref = refs[0] if weighted else None
        mine_ref, other_ref, rows_ref = refs[-3:]

        def store(slot, rows):
            rows_ref[...] = rows

        pick_step(pl.program_id(0), None, rank_ref, weight_ref, mine_ref, other_ref, store, row_count)

    return run(
        kernel,
        PLANE,
        source_specs(tokens, width, weighted),
        pl.BlockSpec((row_count, width), lambda i, p: (slot_of(i, p), 0)),
        jax.ShapeDtypeStruct((PLANE * row_count, width), jnp.bfloat16),
        [],
        2 * PLANE * row_count * tokens * width,
        [place, rank] + ([weight] if weighted else []) + [mine, other],
    )


def tile_at(step):
    return jnp.maximum(step - PLANE, 0)


def forward(place, rank, mine, other, w_gate, w_up, row_count):
    _, tokens, width = mine.shape
    ff = w_gate.shape[2]
    rows = PLANE * row_count

    def kernel(place_ref, rank_ref, mine_ref, other_ref, gate_ref, up_ref, *refs):
        hidden_ref, gate_pre_ref, up_pre_ref, rows_ref = refs
        step = pl.program_id(0)

        def store(slot, values):
            rows_ref[pl.ds(pl.multiple_of(slot * row_count, row_count), row_count), :] = values

        slot = slot_of(step, place_ref)
        pick_step(step, slot, rank_ref, None, mine_ref, other_ref, store, row_count)

        @pl.when(step >= PLANE)
        def _():
            gate_pre = dot_f32(rows_ref[...], gate_ref[0])
            up_pre = dot_f32(rows_ref[...], up_ref[0])
            gate_pre_ref[...] = gate_pre
            up_pre_ref[...] = up_pre
            hidden_ref[...] = (gate_pre * jax.nn.sigmoid(gate_pre) * up_pre).astype(jnp.bfloat16)

    weight_spec = pl.BlockSpec((1, width, FF_TILE), lambda i, p: (0, 0, tile_at(i)))
    out_spec = pl.BlockSpec((rows, FF_TILE), lambda i, p: (0, tile_at(i)))
    return run(
        kernel,
        PLANE + ff // FF_TILE,
        source_specs(tokens, width, False) + [weight_spec] * 2,
        [out_spec] * 3,
        [jax.ShapeDtypeStruct((rows, ff), t) for t in (jnp.bfloat16, jnp.float32, jnp.float32)],
        [pltpu.VMEM((rows, width), jnp.bfloat16)],
        4 * rows * width * ff,
        [place, rank, mine, other, w_gate, w_up],
    )


def backward(place, rank, weight, mine, other, w_down, gate_pre, up_pre, row_count):
    _, tokens, width = mine.shape
    ff = w_down.shape[1]
    rows = PLANE * row_count

    def kernel(place_ref, rank_ref, weight_ref, mine_ref, other_ref, down_ref, gate_pre_ref, *refs):
        up_pre_ref, gate_grad_ref, up_grad_ref, rows_ref = refs
        step = pl.program_id(0)

        def store(slot, values):
            rows_ref[pl.ds(pl.multiple_of(slot * row_count, row_count), row_count), :] = values

        slot = slot_of(step, place_ref)
        pick_step(step, slot, rank_ref, weight_ref, mine_ref, other_ref, store, row_count)

        @pl.when(step >= PLANE)
        def _():
            hidden_grad = dot_f32(rows_ref[...], down_ref[0], CONTRACT_LAST)
            gate_pre = gate_pre_ref[...]
            sigma = jax.nn.sigmoid(gate_pre)
            slope = sigma * (1.0 + gate_pre * (1.0 - sigma))
            gate_grad_ref[...] = (hidden_grad * up_pre_ref[...] * slope).astype(jnp.bfloat16)
            up_grad_ref[...] = (hidden_grad * gate_pre * sigma).astype(jnp.bfloat16)

    down_spec = pl.BlockSpec((1, FF_TILE, width), lambda i, p: (0, tile_at(i), 0))
    tile_spec = pl.BlockSpec((rows, FF_TILE), lambda i, p: (0, tile_at(i)))
    return run(
        kernel,
        PLANE + ff // FF_TILE,
        source_specs(tokens, width, True) + [down_spec] + [tile_spec] * 2,
        [tile_spec] * 2,
        [jax.ShapeDtypeStruct((rows, ff), jnp.bfloat16)] * 2,
        [pltpu.VMEM((rows, width), jnp.bfloat16)],
        2 * rows * width * ff,
        [place, rank, weight, mine, other, w_down, gate_pre, up_pre],
    )


def body(tokens, cotangent, expert_ids, combine, placement, moves, w_gate, w_up, w_down):
    owner_count = lax.axis_size("expert")
    dp_count = lax.axis_size("dp")
    my_index = lax.axis_index("expert")
    my_dp = lax.axis_index("dp")
    tok_rows, width = tokens.shape
    choose_count = expert_ids.shape[1]
    layers = owner_count // PLANE
    half = layers // 2
    row_count = 3 * tok_rows * choose_count // (4 * PLANE)
    pair = owner_count // 2
    own_layer, my_place = my_index // PLANE, my_index % PLANE
    place = my_place.astype(jnp.int32).reshape(1)
    inner = (own_layer == 1) | (own_layer == 2)

    near_tokens, far_tokens = layer_gather(tokens, inner, layers)
    near_cots, far_cots = layer_gather(cotangent, inner, layers)

    order = own_layer ^ jnp.arange(layers, dtype=jnp.int32)
    if layers == 4:
        order = jnp.where(inner, jnp.stack([order[j] for j in (0, 1, 3, 2)]), order)
    routing = jnp.concatenate([expert_ids.astype(jnp.float32), combine], axis=1)
    lines = [routing] + [crossed(routing, "expert", j * PLANE) for j in range(1, layers)]
    if layers == 4:
        lines = lines[:2] + [jnp.where(inner, lines[3], lines[2]), jnp.where(inner, lines[2], lines[3])]
    routing = jnp.stack(lines).transpose(2, 0, 1)
    routing = jnp.stack([routing] + [crossed(routing, "expert", k) for k in range(1, PLANE)])
    ids, weights = routing[:, :choose_count], routing[:, choose_count:]

    slot_ids = jnp.arange(owner_count, dtype=jnp.int32)
    held = jnp.where(moves == 1, jnp.roll(placement, pair), placement)
    mine = slot_ids == my_index
    home_expert = jnp.sum(jnp.where(mine, placement, 0))
    held_expert = jnp.sum(jnp.where(mine, held, 0))
    moved = jnp.sum(jnp.where(mine, moves, 0)) == 1
    plane_slots = own_layer * PLANE + jnp.arange(PLANE, dtype=jnp.int32)
    near = slot_ids[None, :] == plane_slots[:, None]
    plane_experts = jnp.sum(jnp.where(near, placement[None], 0), axis=1)

    def named(expert, source_ids, source_weights):
        match = source_ids == expert.astype(jnp.float32)
        return jnp.any(match, axis=1), jnp.sum(jnp.where(match, source_weights, 0.0), axis=1)

    sets = [
        named(home_expert, ids, weights),
        named(held_expert, ids, weights),
        named(plane_experts[:, None, None, None], ids[:1], weights[:1]),
    ]
    rank = rank_rows(jnp.concatenate([s[0] for s in sets]), order, layers)

    def halves(array):
        array = array.reshape(PLANE, 2, 1, half * tok_rows)
        return array[:, 0], array[:, 1]

    home_rank, held_rank, back_rank = [
        halves(rank[i * PLANE : (i + 1) * PLANE]) for i in range(3)
    ]
    home_weight, held_weight, back_weight = [halves(s[1]) for s in sets]

    groups = [[i * PLANE + j for j in range(PLANE)] for i in range(layers)]

    def sent_back(rows):
        return lax.all_to_all(
            rows.reshape(PLANE, row_count, width),
            "expert",
            split_axis=0,
            concat_axis=0,
            axis_index_groups=groups,
            tiled=True,
        ).reshape(PLANE * row_count, width)

    def spread(side, rows, weighted):
        chosen = back_rank[side] == jnp.arange(row_count, dtype=jnp.int32)[None, :, None]
        if weighted:
            scale = jnp.sum(jnp.where(chosen, back_weight[side], 0.0), axis=2)
            rows = (scale.reshape(-1, 1) * rows.astype(jnp.float32)).astype(jnp.bfloat16)
        one_hot = chosen.astype(jnp.bfloat16).reshape(PLANE * row_count, -1)
        return dot_f32(one_hot, rows, CONTRACT_ROWS).astype(jnp.bfloat16)

    hidden, gate_grad, up_grad, out_back, grad_back = [], [], [], [], []
    token_sides, cot_sides = [], []
    for side, (near_half, cot_half) in enumerate(
        ((near_tokens, near_cots), (far_tokens, far_cots))
    ):
        token_side = plane_gather(near_half)
        rows = forward(place, home_rank[side], *token_side, w_gate, w_up, row_count)
        cot_side = plane_gather(cot_half)
        grads = backward(
            place, home_rank[side], home_weight[side], *cot_side, w_down, *rows[1:], row_count
        )
        token_sides.append(token_side)
        cot_sides.append(cot_side)
        hidden.append(rows[0])
        gate_grad.append(grads[0])
        up_grad.append(grads[1])
        out_rows = dot_f32(rows[0], w_down[0]).astype(jnp.bfloat16)
        grad_rows = dot_f32(grads[0], w_gate[0], CONTRACT_LAST) + dot_f32(
            grads[1], w_up[0], CONTRACT_LAST
        )
        out_back.append(spread(side, sent_back(out_rows), True))
        grad_back.append(spread(side, sent_back(grad_rows.astype(jnp.bfloat16)), False))

    mixed = layer_reduce(*out_back, tok_rows, layers)
    input_grad = layer_reduce(*grad_back, tok_rows, layers)

    def relocated(sides):
        got = [crossed(array, "expert", pair) for array in sides]
        return [jnp.where(moved, got[1 - side], sides[side]) for side in range(2)]

    hidden, gate_grad, up_grad = relocated(hidden), relocated(gate_grad), relocated(up_grad)
    held_rows = [
        pick(place, held_rank[side], None, *token_sides[side], row_count) for side in range(2)
    ]
    held_grads = [
        pick(place, held_rank[side], held_weight[side], *cot_sides[side], row_count)
        for side in range(2)
    ]

    def weight_grad(left, right):
        share = left[0].shape[1] // dp_count

        def product(part):
            total = 0.0
            for a, b in zip(left, right):
                columns = lax.dynamic_slice_in_dim(a, part * share, share, axis=1)
                total = total + dot_f32(columns, b, CONTRACT_ROWS)
            return total

        sent = product((my_dp + 1) % dp_count).astype(jnp.bfloat16)
        got = crossed(sent, "dp", 1)
        return ((product(my_dp) + got.astype(jnp.float32)) * (1.0 / dp_count))[None]

    return (
        mixed,
        input_grad,
        weight_grad(held_rows, gate_grad),
        weight_grad(held_rows, up_grad),
        weight_grad(hidden, held_grads),
    )


def solution(mesh):
    tokens = P(("dp", "expert"), None)
    slots = P("expert", None, None)
    grads = P("expert", "dp", None)
    return jax.shard_map(
        body,
        mesh=mesh,
        in_specs=(tokens, tokens, tokens, tokens, P(), P(), slots, slots, slots),
        out_specs=(tokens, tokens, grads, grads, grads),
        check_vma=False,
    )
```

```python
import jax
import jax.numpy as jnp
from jax import lax
from jax.experimental import pallas as pl
from jax.experimental.pallas import tpu as pltpu
from jax.sharding import PartitionSpec as P

CONTRACT_ROWS = (((0,), (0,)), ((), ()))
CONTRACT_LAST = (((1,), (1,)), ((), ()))
PLANE = 4
FF_TILE = 256
VMEM_BYTES = 40 * 1024 * 1024


def dot_f32(a, b, dims=(((1,), (0,)), ((), ()))):
    return lax.dot_general(a, b, dims, preferred_element_type=jnp.float32)


def crossed(array, axis, flip):
    return lax.ppermute(array, axis, [(i, i ^ flip) for i in range(lax.axis_size(axis))])


def along(array, pairs):
    return lax.ppermute(array, "expert", pairs)


def line_pairs(owner_count):
    inner = [i for i in range(owner_count) if i // PLANE in (1, 2)]
    middle = [(i, i ^ 3 * PLANE) for i in inner]
    outward = [(i, i ^ PLANE) for i in inner]
    inward = [(i ^ PLANE, i) for i in inner]
    return middle, outward, inward


def there(flag, *arrays):
    for array in arrays:
        first = array[(0,) * array.ndim]
        flag = flag & (first == first)
    return flag


def layer_gather(block, layers):
    if layers != 4:
        got = [block] + [crossed(block, "expert", j * PLANE) for j in range(1, layers)]
        far = jnp.concatenate(got[layers // 2 :])
        return got[: layers // 2], far, far
    middle, outward, _ = line_pairs(layers * PLANE)
    near = crossed(block, "expert", PLANE)
    far = [along(block, middle), along(near, middle)]
    relayed = [along(array, outward) for array in far]
    return [block, near], jnp.concatenate(far), jnp.concatenate(relayed)


def plane_gather(blocks):
    crossing = [crossed(block, "expert", 2) for block in blocks]
    mine = jnp.stack([jnp.concatenate(blocks), jnp.concatenate(crossing)])
    return mine, crossed(mine, "expert", 1)


def layer_reduce(own, far, tok_rows, layers):
    total = own[:tok_rows].astype(jnp.float32)
    if layers != 4:
        spread = jnp.concatenate([own, far])
        for j in range(1, layers):
            block = crossed(spread[j * tok_rows : (j + 1) * tok_rows], "expert", j * PLANE)
            total = total + block.astype(jnp.float32)
        return total.astype(jnp.bfloat16)
    middle, outward, inward = line_pairs(layers * PLANE)
    far_sum = (far.astype(jnp.float32) + along(far, inward).astype(jnp.float32)).astype(far.dtype)
    near = own[tok_rows:]
    near_in = along(near, inward)
    got = along(far_sum, middle)
    near_sum = (near.astype(jnp.float32) + got[tok_rows:].astype(jnp.float32)).astype(far.dtype)
    near_out = along(near_sum, outward)
    for block in (near_in, got[:tok_rows], near_out):
        total = total + block.astype(jnp.float32)
    return total.astype(jnp.bfloat16)


def rank_rows(hit, order, layers):
    half = layers // 2
    tok_rows = hit.shape[2]
    earlier = jnp.arange(tok_rows)[:, None] < jnp.arange(tok_rows)[None, :]
    within = jnp.einsum(
        "slt,tu->slu",
        hit.astype(jnp.bfloat16),
        earlier.astype(jnp.bfloat16),
        preferred_element_type=jnp.float32,
    ).astype(jnp.int32)
    count = jnp.sum(hit.astype(jnp.int32), axis=2)
    side = jnp.arange(layers) // half
    ahead = (order[:, None] < order[None, :]) & (side[:, None] == side[None, :])
    before = jnp.sum(jnp.where(ahead[None], count[:, :, None], 0), axis=1)
    return jnp.where(hit, within + before[:, :, None], -1)


def pick_rows(rank, source, row_count):
    place = lax.broadcasted_iota(jnp.int32, (row_count, rank.shape[1]), 0)
    chosen = place == rank
    one_hot = jnp.where(chosen, 1.0, 0.0).astype(jnp.bfloat16)
    return chosen, dot_f32(one_hot, source)


def pick_step(step, slot, rank_ref, weight_ref, mine_ref, other_ref, store, row_count):
    def stored(source_ref):
        chosen, rows = pick_rows(rank_ref[0], source_ref[0], row_count)
        if weight_ref is not None:
            picked = jnp.where(chosen, weight_ref[0], 0.0)
            rows = rows * jnp.sum(picked, axis=1, keepdims=True)
        store(slot, rows.astype(jnp.bfloat16))

    @pl.when(step < 2)
    def _():
        stored(mine_ref)

    @pl.when((step >= 2) & (step < PLANE))
    def _():
        stored(other_ref)


def source_xor(step):
    return (step // 2) + 2 * (step % 2)


def slot_of(step, place_ref):
    return place_ref[0] ^ source_xor(jnp.minimum(step, PLANE - 1))


def source_specs(tokens, width, weighted):
    line = pl.BlockSpec((1, 1, tokens), lambda i, p: (source_xor(jnp.minimum(i, PLANE - 1)), 0, 0))
    mine = pl.BlockSpec((1, tokens, width), lambda i, p: (jnp.minimum(i, 1), 0, 0))
    other = pl.BlockSpec((1, tokens, width), lambda i, p: (jnp.clip(i - 2, 0, 1), 0, 0))
    return [line] * (2 if weighted else 1) + [mine, other]


def run(kernel, grid, in_specs, out_specs, out_shape, scratch, flops, args, earlier=()):
    moved = sum(a.size * a.dtype.itemsize for a in args)
    count = len(in_specs) + 1
    in_specs = in_specs + [pl.BlockSpec(memory_space=pl.ANY)] * len(earlier)
    if earlier:
        inner_kernel = kernel

        def kernel(*refs):
            inner_kernel(*refs[:count], *refs[count + len(earlier) :])

    return pl.pallas_call(
        kernel,
        grid_spec=pltpu.PrefetchScalarGridSpec(
            num_scalar_prefetch=1,
            grid=(grid,),
            in_specs=in_specs,
            out_specs=out_specs,
            scratch_shapes=scratch,
        ),
        out_shape=out_shape,
        compiler_params=pltpu.CompilerParams(vmem_limit_bytes=VMEM_BYTES),
        cost_estimate=pl.CostEstimate(flops=flops, bytes_accessed=moved, transcendentals=0),
    )(*args, *earlier)


def pick(place, rank, weight, mine, other, row_count):
    _, tokens, width = mine.shape
    weighted = weight is not None

    def kernel(place_ref, rank_ref, *refs):
        weight_ref = refs[0] if weighted else None
        mine_ref, other_ref, rows_ref = refs[-3:]

        def store(slot, rows):
            rows_ref[...] = rows

        pick_step(pl.program_id(0), None, rank_ref, weight_ref, mine_ref, other_ref, store, row_count)

    return run(
        kernel,
        PLANE,
        source_specs(tokens, width, weighted),
        pl.BlockSpec((row_count, width), lambda i, p: (slot_of(i, p), 0)),
        jax.ShapeDtypeStruct((PLANE * row_count, width), jnp.bfloat16),
        [],
        2 * PLANE * row_count * tokens * width,
        [place, rank] + ([weight] if weighted else []) + [mine, other],
    )


def tile_at(step):
    return jnp.maximum(step - PLANE, 0)


def forward(place, rank, mine, other, w_gate, w_up, row_count):
    _, tokens, width = mine.shape
    ff = w_gate.shape[2]
    rows = PLANE * row_count

    def kernel(place_ref, rank_ref, mine_ref, other_ref, gate_ref, up_ref, *refs):
        hidden_ref, gate_pre_ref, up_pre_ref, rows_ref = refs
        step = pl.program_id(0)

        def store(slot, values):
            rows_ref[pl.ds(pl.multiple_of(slot * row_count, row_count), row_count), :] = values

        slot = slot_of(step, place_ref)
        pick_step(step, slot, rank_ref, None, mine_ref, other_ref, store, row_count)

        @pl.when(step >= PLANE)
        def _():
            gate_pre = dot_f32(rows_ref[...], gate_ref[0])
            up_pre = dot_f32(rows_ref[...], up_ref[0])
            gate_pre_ref[...] = gate_pre
            up_pre_ref[...] = up_pre
            hidden_ref[...] = (gate_pre * jax.nn.sigmoid(gate_pre) * up_pre).astype(jnp.bfloat16)

    weight_spec = pl.BlockSpec((1, width, FF_TILE), lambda i, p: (0, 0, tile_at(i)))
    out_spec = pl.BlockSpec((rows, FF_TILE), lambda i, p: (0, tile_at(i)))
    return run(
        kernel,
        PLANE + ff // FF_TILE,
        source_specs(tokens, width, False) + [weight_spec] * 2,
        [out_spec] * 3,
        [jax.ShapeDtypeStruct((rows, ff), t) for t in (jnp.bfloat16, jnp.float32, jnp.float32)],
        [pltpu.VMEM((rows, width), jnp.bfloat16)],
        4 * rows * width * ff,
        [place, rank, mine, other, w_gate, w_up],
    )


def backward(place, rank, weight, mine, other, w_down, gate_pre, up_pre, row_count, earlier):
    _, tokens, width = mine.shape
    ff = w_down.shape[1]
    rows = PLANE * row_count

    def kernel(place_ref, rank_ref, weight_ref, mine_ref, other_ref, down_ref, gate_pre_ref, *refs):
        up_pre_ref, grad_ref, rows_ref = refs
        step = pl.program_id(0)

        def store(slot, values):
            rows_ref[pl.ds(pl.multiple_of(slot * row_count, row_count), row_count), :] = values

        slot = slot_of(step, place_ref)
        pick_step(step, slot, rank_ref, weight_ref, mine_ref, other_ref, store, row_count)

        @pl.when(step >= PLANE)
        def _():
            hidden_grad = dot_f32(rows_ref[...], down_ref[0], CONTRACT_LAST)
            gate_pre = gate_pre_ref[...]
            sigma = jax.nn.sigmoid(gate_pre)
            slope = sigma * (1.0 + gate_pre * (1.0 - sigma))
            grad_ref[0] = (hidden_grad * up_pre_ref[...] * slope).astype(jnp.bfloat16)
            grad_ref[1] = (hidden_grad * gate_pre * sigma).astype(jnp.bfloat16)

    down_spec = pl.BlockSpec((1, FF_TILE, width), lambda i, p: (0, tile_at(i), 0))
    tile_spec = pl.BlockSpec((rows, FF_TILE), lambda i, p: (0, tile_at(i)))
    return run(
        kernel,
        PLANE + ff // FF_TILE,
        source_specs(tokens, width, True) + [down_spec] + [tile_spec] * 2,
        pl.BlockSpec((2, rows, FF_TILE), lambda i, p: (0, 0, tile_at(i))),
        jax.ShapeDtypeStruct((2, rows, ff), jnp.bfloat16),
        [pltpu.VMEM((rows, width), jnp.bfloat16)],
        2 * rows * width * ff,
        [place, rank, weight, mine, other, w_down, gate_pre, up_pre],
        earlier,
    )


def body(tokens, cotangent, expert_ids, combine, placement, moves, w_gate, w_up, w_down):
    owner_count = lax.axis_size("expert")
    dp_count = lax.axis_size("dp")
    my_index = lax.axis_index("expert")
    my_dp = lax.axis_index("dp")
    tok_rows, width = tokens.shape
    choose_count = expert_ids.shape[1]
    layers = owner_count // PLANE
    half = layers // 2
    row_count = 3 * tok_rows * choose_count // (4 * PLANE)
    pair = owner_count // 2
    own_layer, my_place = my_index // PLANE, my_index % PLANE
    place = my_place.astype(jnp.int32).reshape(1)
    inner = (own_layer == 1) | (own_layer == 2)

    near_tokens, *far_tokens = layer_gather(tokens, layers)
    near_cots, *far_cots = layer_gather(cotangent, layers)

    order = own_layer ^ jnp.arange(layers, dtype=jnp.int32)
    if layers == 4:
        order = jnp.where(inner, jnp.stack([order[j] for j in (0, 1, 3, 2)]), order)
    routing = jnp.concatenate([expert_ids.astype(jnp.float32), combine], axis=1)
    lines = [routing] + [crossed(routing, "expert", j * PLANE) for j in range(1, layers)]
    if layers == 4:
        lines = lines[:2] + [jnp.where(inner, lines[3], lines[2]), jnp.where(inner, lines[2], lines[3])]
    routing = jnp.stack(lines).transpose(2, 0, 1)
    routing = jnp.stack([routing] + [crossed(routing, "expert", k) for k in range(1, PLANE)])
    ids, weights = routing[:, :choose_count], routing[:, choose_count:]

    slot_ids = jnp.arange(owner_count, dtype=jnp.int32)
    held = jnp.where(moves == 1, jnp.roll(placement, pair), placement)
    mine = slot_ids == my_index
    home_expert = jnp.sum(jnp.where(mine, placement, 0))
    held_expert = jnp.sum(jnp.where(mine, held, 0))
    moved = jnp.sum(jnp.where(mine, moves, 0)) == 1
    plane_slots = own_layer * PLANE + jnp.arange(PLANE, dtype=jnp.int32)
    near = slot_ids[None, :] == plane_slots[:, None]
    plane_experts = jnp.sum(jnp.where(near, placement[None], 0), axis=1)

    def named(expert, source_ids, source_weights):
        match = source_ids == expert.astype(jnp.float32)
        return jnp.any(match, axis=1), jnp.sum(jnp.where(match, source_weights, 0.0), axis=1)

    sets = [
        named(home_expert, ids, weights),
        named(held_expert, ids, weights),
        named(plane_experts[:, None, None, None], ids[:1], weights[:1]),
    ]
    rank = rank_rows(jnp.concatenate([s[0] for s in sets]), order, layers)

    def halves(array):
        array = array.reshape(PLANE, 2, 1, half * tok_rows)
        return array[:, 0], array[:, 1]

    home_rank, held_rank, back_rank = [
        halves(rank[i * PLANE : (i + 1) * PLANE]) for i in range(3)
    ]
    home_weight, held_weight, back_weight = [halves(s[1]) for s in sets]

    groups = [[i * PLANE + j for j in range(PLANE)] for i in range(layers)]

    def joined(own, far):
        sides = [array.reshape(PLANE, row_count, -1) for array in (own, far)]
        return jnp.concatenate(sides, axis=1).reshape(2 * PLANE * row_count, -1)

    def sent_back(rows):
        rows = rows.astype(jnp.bfloat16).reshape(PLANE, 2 * row_count, width)
        return lax.all_to_all(
            rows, "expert", split_axis=0, concat_axis=0, axis_index_groups=groups, tiled=True
        )

    def spread(back, weighted):
        sides = []
        for side in range(2):
            rows = back[:, side * row_count : (side + 1) * row_count]
            chosen = back_rank[side] == jnp.arange(row_count, dtype=jnp.int32)[None, :, None]
            if weighted:
                scale = jnp.sum(jnp.where(chosen, back_weight[side], 0.0), axis=2, keepdims=True)
                rows = (scale * rows.astype(jnp.float32)).astype(jnp.bfloat16)
            one_hot = chosen.astype(jnp.bfloat16).reshape(PLANE * row_count, -1)
            rows = rows.reshape(PLANE * row_count, width)
            sides.append(dot_f32(one_hot, rows, CONTRACT_ROWS).astype(jnp.bfloat16))
        return sides

    def halves_forward(side, token_side):
        return forward(place, home_rank[side], *token_side, w_gate, w_up, row_count)

    def halves_backward(side, cot_side, pre, earlier):
        rank, weight = home_rank[side], home_weight[side]
        return backward(place, rank, weight, *cot_side, w_down, *pre, row_count, earlier)

    token_sides, cot_sides = [plane_gather(near_tokens)], [plane_gather(near_cots)]
    own_hidden, *own_pre = halves_forward(0, token_sides[0])
    own_grads = halves_backward(0, cot_sides[0], own_pre, [])
    token_sides.append(plane_gather([jnp.where(there(inner, own_hidden), *far_tokens)]))
    cot_sides.append(plane_gather([jnp.where(there(inner, own_grads), *far_cots)]))
    far_hidden, *far_pre = halves_forward(1, token_sides[1])
    out_rows = dot_f32(joined(own_hidden, far_hidden), w_down[0]).astype(jnp.bfloat16)
    out_back = sent_back(out_rows)
    far_grads = halves_backward(1, cot_sides[1], far_pre, [out_rows])
    grad_rows = dot_f32(joined(own_grads[0], far_grads[0]), w_gate[0], CONTRACT_LAST) + dot_f32(
        joined(own_grads[1], far_grads[1]), w_up[0], CONTRACT_LAST
    )
    grad_back = sent_back(grad_rows)

    mixed = layer_reduce(*spread(out_back, True), tok_rows, layers)
    input_grad = layer_reduce(*spread(grad_back, False), tok_rows, layers)

    got_hidden = [crossed(array, "expert", pair) for array in (own_hidden, far_hidden)]
    got_own_grads = crossed(own_grads, "expert", pair)
    got_far_grads = [crossed(far_grads[i], "expert", pair) for i in range(2)]
    after_out, after_grad = there(moved, out_back), there(moved, grad_back)

    def relocated(flag, own, far, got_own, got_far):
        return [jnp.where(flag, got_far, own), jnp.where(flag, got_own, far)]

    hidden = relocated(after_out, own_hidden, far_hidden, *got_hidden)
    gate_grad, up_grad = [
        relocated(after_grad, own_grads[i], far_grads[i], got_own_grads[i], got_far_grads[i])
        for i in range(2)
    ]
    held_rows = [
        pick(place, held_rank[side], None, *token_sides[side], row_count) for side in range(2)
    ]
    held_grads = [
        pick(place, held_rank[side], held_weight[side], *cot_sides[side], row_count)
        for side in range(2)
    ]

    def weight_grad(left, right):
        share = left[0].shape[1] // dp_count

        def product(part):
            total = 0.0
            for a, b in zip(left, right):
                columns = lax.dynamic_slice_in_dim(a, part * share, share, axis=1)
                total = total + dot_f32(columns, b, CONTRACT_ROWS)
            return total

        sent = product((my_dp + 1) % dp_count).astype(jnp.bfloat16)
        got = crossed(sent, "dp", 1)
        return ((product(my_dp) + got.astype(jnp.float32)) * (1.0 / dp_count))[None]

    return (
        mixed,
        input_grad,
        weight_grad(held_rows, gate_grad),
        weight_grad(held_rows, up_grad),
        weight_grad(hidden, held_grads),
    )


def solution(mesh):
    tokens = P(("dp", "expert"), None)
    slots = P("expert", None, None)
    grads = P("expert", "dp", None)
    return jax.shard_map(
        body,
        mesh=mesh,
        in_specs=(tokens, tokens, tokens, tokens, P(), P(), slots, slots, slots),
        out_specs=(tokens, tokens, grads, grads, grads),
        check_vma=False,
    )
```

```python
import jax
import jax.numpy as jnp
from jax import lax
from jax.experimental import pallas as pl
from jax.experimental.pallas import tpu as pltpu
from jax.sharding import PartitionSpec as P

CONTRACT_ROWS = (((0,), (0,)), ((), ()))
CONTRACT_LAST = (((1,), (1,)), ((), ()))
PLANE = 4
FF_TILE = 256
VMEM_BYTES = 40 * 1024 * 1024


def dot_f32(a, b, dims=(((1,), (0,)), ((), ()))):
    return lax.dot_general(a, b, dims, preferred_element_type=jnp.float32)


def crossed(array, axis, flip):
    return lax.ppermute(array, axis, [(i, i ^ flip) for i in range(lax.axis_size(axis))])


def along(array, pairs):
    return lax.ppermute(array, "expert", pairs)


def line_pairs(owner_count):
    inner = [i for i in range(owner_count) if i // PLANE in (1, 2)]
    middle = [(i, i ^ 3 * PLANE) for i in inner]
    outward = [(i, i ^ PLANE) for i in inner]
    inward = [(i ^ PLANE, i) for i in inner]
    return middle, outward, inward


def there(flag, *arrays):
    for array in arrays:
        corner = array[tuple(slice(0, 1) for _ in array.shape)].reshape(())
        flag = flag & (corner == corner)
    return flag


def when(flag, array):
    return jnp.where(flag, array, jnp.zeros((), array.dtype))


def layer_gather(block, layers):
    if layers != 4:
        got = [block] + [crossed(block, "expert", j * PLANE) for j in range(1, layers)]
        far = jnp.concatenate(got[layers // 2 :])
        return got[: layers // 2], far, far, got[1:2]
    middle, outward, _ = line_pairs(layers * PLANE)
    near = crossed(block, "expert", PLANE)
    far = [along(block, middle), along(near, middle)]
    relayed = [along(array, outward) for array in far]
    return [block, near], jnp.concatenate(far), jnp.concatenate(relayed), [near, far[0]]


def plane_gather(blocks):
    crossing = [crossed(block, "expert", 2) for block in blocks]
    mine = jnp.stack([jnp.concatenate(blocks), jnp.concatenate(crossing)])
    return mine, crossed(mine, "expert", 1)


def layer_reduce(own, far, tok_rows, layers, far_flag, near_flag):
    total = own[:tok_rows].astype(jnp.float32)
    if layers != 4:
        spread = jnp.concatenate([own, far])
        for j in range(1, layers):
            block = crossed(spread[j * tok_rows : (j + 1) * tok_rows], "expert", j * PLANE)
            total = total + block.astype(jnp.float32)
        return total.astype(jnp.bfloat16)
    middle, outward, inward = line_pairs(layers * PLANE)
    far_sum = (far.astype(jnp.float32) + along(far, inward).astype(jnp.float32)).astype(far.dtype)
    far_sum = when(far_flag, far_sum)
    near = own[tok_rows:]
    near_in = along(near, inward)
    got = along(far_sum, middle)
    near_sum = (near.astype(jnp.float32) + got[tok_rows:].astype(jnp.float32)).astype(far.dtype)
    near_sum = when(near_flag, near_sum)
    near_out = along(near_sum, outward)
    for block in (near_in, got[:tok_rows], near_out):
        total = total + block.astype(jnp.float32)
    return total.astype(jnp.bfloat16)


def rank_rows(hit, order, layers):
    half = layers // 2
    tok_rows = hit.shape[2]
    earlier = jnp.arange(tok_rows)[:, None] < jnp.arange(tok_rows)[None, :]
    within = jnp.einsum(
        "slt,tu->slu",
        hit.astype(jnp.bfloat16),
        earlier.astype(jnp.bfloat16),
        preferred_element_type=jnp.float32,
    ).astype(jnp.int32)
    count = jnp.sum(hit.astype(jnp.int32), axis=2)
    side = jnp.arange(layers) // half
    ahead = (order[:, None] < order[None, :]) & (side[:, None] == side[None, :])
    before = jnp.sum(jnp.where(ahead[None], count[:, :, None], 0), axis=1)
    return jnp.where(hit, within + before[:, :, None], -1)


def pick_rows(rank, source, row_count):
    place = lax.broadcasted_iota(jnp.int32, (row_count, rank.shape[1]), 0)
    chosen = place == rank
    one_hot = jnp.where(chosen, 1.0, 0.0).astype(jnp.bfloat16)
    return chosen, dot_f32(one_hot, source)


def pick_step(step, slot, rank_ref, weight_ref, mine_ref, other_ref, store, row_count):
    def stored(source_ref):
        chosen, rows = pick_rows(rank_ref[0], source_ref[0], row_count)
        if weight_ref is not None:
            picked = jnp.where(chosen, weight_ref[0], 0.0)
            rows = rows * jnp.sum(picked, axis=1, keepdims=True)
        store(slot, rows.astype(jnp.bfloat16))

    @pl.when(step < 2)
    def _():
        stored(mine_ref)

    @pl.when((step >= 2) & (step < PLANE))
    def _():
        stored(other_ref)


def source_xor(step):
    return (step // 2) + 2 * (step % 2)


def slot_of(step, place_ref):
    return place_ref[0] ^ source_xor(jnp.minimum(step, PLANE - 1))


def source_specs(tokens, width, weighted):
    line = pl.BlockSpec((1, 1, tokens), lambda i, p: (source_xor(jnp.minimum(i, PLANE - 1)), 0, 0))
    mine = pl.BlockSpec((1, tokens, width), lambda i, p: (jnp.minimum(i, 1), 0, 0))
    other = pl.BlockSpec((1, tokens, width), lambda i, p: (jnp.clip(i - 2, 0, 1), 0, 0))
    return [line] * (2 if weighted else 1) + [mine, other]


def run(kernel, grid, in_specs, out_specs, out_shape, scratch, flops, args, earlier=()):
    moved = sum(a.size * a.dtype.itemsize for a in args)
    count = len(in_specs) + 1
    in_specs = in_specs + [pl.BlockSpec(memory_space=pl.ANY)] * len(earlier)
    if earlier:
        inner_kernel = kernel

        def kernel(*refs):
            inner_kernel(*refs[:count], *refs[count + len(earlier) :])

    return pl.pallas_call(
        kernel,
        grid_spec=pltpu.PrefetchScalarGridSpec(
            num_scalar_prefetch=1,
            grid=(grid,),
            in_specs=in_specs,
            out_specs=out_specs,
            scratch_shapes=scratch,
        ),
        out_shape=out_shape,
        compiler_params=pltpu.CompilerParams(vmem_limit_bytes=VMEM_BYTES),
        cost_estimate=pl.CostEstimate(flops=flops, bytes_accessed=moved, transcendentals=0),
    )(*args, *earlier)


def pick(place, rank, weight, mine, other, row_count):
    _, tokens, width = mine.shape
    weighted = weight is not None

    def kernel(place_ref, rank_ref, *refs):
        weight_ref = refs[0] if weighted else None
        mine_ref, other_ref, rows_ref = refs[-3:]

        def store(slot, rows):
            rows_ref[...] = rows

        pick_step(pl.program_id(0), None, rank_ref, weight_ref, mine_ref, other_ref, store, row_count)

    return run(
        kernel,
        PLANE,
        source_specs(tokens, width, weighted),
        pl.BlockSpec((row_count, width), lambda i, p: (slot_of(i, p), 0)),
        jax.ShapeDtypeStruct((PLANE * row_count, width), jnp.bfloat16),
        [],
        2 * PLANE * row_count * tokens * width,
        [place, rank] + ([weight] if weighted else []) + [mine, other],
    )


def tile_at(step):
    return jnp.maximum(step - PLANE, 0)


def forward(place, rank, mine, other, w_gate, w_up, row_count, earlier):
    _, tokens, width = mine.shape
    ff = w_gate.shape[2]
    rows = PLANE * row_count

    def kernel(place_ref, rank_ref, mine_ref, other_ref, gate_ref, up_ref, *refs):
        hidden_ref, gate_pre_ref, up_pre_ref, rows_ref = refs
        step = pl.program_id(0)

        def store(slot, values):
            rows_ref[pl.ds(pl.multiple_of(slot * row_count, row_count), row_count), :] = values

        slot = slot_of(step, place_ref)
        pick_step(step, slot, rank_ref, None, mine_ref, other_ref, store, row_count)

        @pl.when(step >= PLANE)
        def _():
            gate_pre = dot_f32(rows_ref[...], gate_ref[0])
            up_pre = dot_f32(rows_ref[...], up_ref[0])
            gate_pre_ref[...] = gate_pre
            up_pre_ref[...] = up_pre
            hidden_ref[...] = (gate_pre * jax.nn.sigmoid(gate_pre) * up_pre).astype(jnp.bfloat16)

    weight_spec = pl.BlockSpec((1, width, FF_TILE), lambda i, p: (0, 0, tile_at(i)))
    out_spec = pl.BlockSpec((rows, FF_TILE), lambda i, p: (0, tile_at(i)))
    return run(
        kernel,
        PLANE + ff // FF_TILE,
        source_specs(tokens, width, False) + [weight_spec] * 2,
        [out_spec] * 3,
        [jax.ShapeDtypeStruct((rows, ff), t) for t in (jnp.bfloat16, jnp.float32, jnp.float32)],
        [pltpu.VMEM((rows, width), jnp.bfloat16)],
        4 * rows * width * ff,
        [place, rank, mine, other, w_gate, w_up],
        earlier,
    )


def backward(place, rank, weight, mine, other, w_down, gate_pre, up_pre, row_count, earlier):
    _, tokens, width = mine.shape
    ff = w_down.shape[1]
    rows = PLANE * row_count

    def kernel(place_ref, rank_ref, weight_ref, mine_ref, other_ref, down_ref, gate_pre_ref, *refs):
        up_pre_ref, grad_ref, rows_ref = refs
        step = pl.program_id(0)

        def store(slot, values):
            rows_ref[pl.ds(pl.multiple_of(slot * row_count, row_count), row_count), :] = values

        slot = slot_of(step, place_ref)
        pick_step(step, slot, rank_ref, weight_ref, mine_ref, other_ref, store, row_count)

        @pl.when(step >= PLANE)
        def _():
            hidden_grad = dot_f32(rows_ref[...], down_ref[0], CONTRACT_LAST)
            gate_pre = gate_pre_ref[...]
            sigma = jax.nn.sigmoid(gate_pre)
            slope = sigma * (1.0 + gate_pre * (1.0 - sigma))
            grad_ref[0] = (hidden_grad * up_pre_ref[...] * slope).astype(jnp.bfloat16)
            grad_ref[1] = (hidden_grad * gate_pre * sigma).astype(jnp.bfloat16)

    down_spec = pl.BlockSpec((1, FF_TILE, width), lambda i, p: (0, tile_at(i), 0))
    tile_spec = pl.BlockSpec((rows, FF_TILE), lambda i, p: (0, tile_at(i)))
    return run(
        kernel,
        PLANE + ff // FF_TILE,
        source_specs(tokens, width, True) + [down_spec] + [tile_spec] * 2,
        pl.BlockSpec((2, rows, FF_TILE), lambda i, p: (0, 0, tile_at(i))),
        jax.ShapeDtypeStruct((2, rows, ff), jnp.bfloat16),
        [pltpu.VMEM((rows, width), jnp.bfloat16)],
        2 * rows * width * ff,
        [place, rank, weight, mine, other, w_down, gate_pre, up_pre],
        earlier,
    )


def body(tokens, cotangent, expert_ids, combine, placement, moves, w_gate, w_up, w_down):
    owner_count = lax.axis_size("expert")
    dp_count = lax.axis_size("dp")
    my_index = lax.axis_index("expert")
    my_dp = lax.axis_index("dp")
    tok_rows, width = tokens.shape
    choose_count = expert_ids.shape[1]
    layers = owner_count // PLANE
    half = layers // 2
    row_count = 3 * tok_rows * choose_count // (4 * PLANE)
    pair = owner_count // 2
    own_layer, my_place = my_index // PLANE, my_index % PLANE
    place = my_place.astype(jnp.int32).reshape(1)
    inner = (own_layer == 1) | (own_layer == 2)

    near_tokens, *far_tokens, first_hops = layer_gather(tokens, layers)

    order = own_layer ^ jnp.arange(layers, dtype=jnp.int32)
    if layers == 4:
        order = jnp.where(inner, jnp.stack([order[j] for j in (0, 1, 3, 2)]), order)
    routing = jnp.concatenate([expert_ids.astype(jnp.float32), combine], axis=1)
    lines = [routing] + [crossed(routing, "expert", j * PLANE) for j in range(1, layers)]
    if layers == 4:
        lines = lines[:2] + [jnp.where(inner, lines[3], lines[2]), jnp.where(inner, lines[2], lines[3])]
    routing = jnp.stack(lines).transpose(2, 0, 1)
    routing = jnp.stack([routing] + [crossed(routing, "expert", k) for k in range(1, PLANE)])
    ids, weights = routing[:, :choose_count], routing[:, choose_count:]
    cotangent = when(there(True, routing[1:], *first_hops), cotangent)
    near_cots, *far_cots, _ = layer_gather(cotangent, layers)

    slot_ids = jnp.arange(owner_count, dtype=jnp.int32)
    held = jnp.where(moves == 1, jnp.roll(placement, pair), placement)
    mine = slot_ids == my_index
    home_expert = jnp.sum(jnp.where(mine, placement, 0))
    held_expert = jnp.sum(jnp.where(mine, held, 0))
    moved = jnp.sum(jnp.where(mine, moves, 0)) == 1
    plane_slots = own_layer * PLANE + jnp.arange(PLANE, dtype=jnp.int32)
    near = slot_ids[None, :] == plane_slots[:, None]
    plane_experts = jnp.sum(jnp.where(near, placement[None], 0), axis=1)

    def named(expert, source_ids, source_weights):
        match = source_ids == expert.astype(jnp.float32)
        return jnp.any(match, axis=1), jnp.sum(jnp.where(match, source_weights, 0.0), axis=1)

    sets = [
        named(home_expert, ids, weights),
        named(held_expert, ids, weights),
        named(plane_experts[:, None, None, None], ids[:1], weights[:1]),
    ]
    rank = rank_rows(jnp.concatenate([s[0] for s in sets]), order, layers)

    def halves(array):
        array = array.reshape(PLANE, 2, 1, half * tok_rows)
        return array[:, 0], array[:, 1]

    home_rank, held_rank, back_rank = [
        halves(rank[i * PLANE : (i + 1) * PLANE]) for i in range(3)
    ]
    home_weight, held_weight, back_weight = [halves(s[1]) for s in sets]

    groups = [[i * PLANE + j for j in range(PLANE)] for i in range(layers)]

    def joined(own, far):
        sides = [array.reshape(PLANE, row_count, -1) for array in (own, far)]
        return jnp.concatenate(sides, axis=1).reshape(2 * PLANE * row_count, -1)

    def sent_back(rows):
        rows = rows.astype(jnp.bfloat16).reshape(PLANE, 2 * row_count, width)
        return lax.all_to_all(
            rows, "expert", split_axis=0, concat_axis=0, axis_index_groups=groups, tiled=True
        )

    def spread(back, weighted, flag):
        sides = []
        for side in range(2):
            rows = back[:, side * row_count : (side + 1) * row_count]
            chosen = back_rank[side] == jnp.arange(row_count, dtype=jnp.int32)[None, :, None]
            chosen = chosen & flag
            if weighted:
                scale = jnp.sum(jnp.where(chosen, back_weight[side], 0.0), axis=2, keepdims=True)
                rows = (scale * rows.astype(jnp.float32)).astype(jnp.bfloat16)
            one_hot = chosen.astype(jnp.bfloat16).reshape(PLANE * row_count, -1)
            rows = rows.reshape(PLANE * row_count, width)
            sides.append(dot_f32(one_hot, rows, CONTRACT_ROWS).astype(jnp.bfloat16))
        return sides

    def halves_forward(side, token_side, earlier):
        return forward(place, home_rank[side], *token_side, w_gate, w_up, row_count, earlier)

    def halves_backward(side, cot_side, pre, earlier):
        rank, weight = home_rank[side], home_weight[side]
        return backward(place, rank, weight, *cot_side, w_down, *pre, row_count, earlier)

    token_sides, cot_sides = [plane_gather(near_tokens)], [plane_gather(near_cots)]
    own_hidden, *own_pre = halves_forward(0, token_sides[0], [])
    own_grads = halves_backward(0, cot_sides[0], own_pre, [])
    token_sides.append(plane_gather([jnp.where(there(inner, own_hidden), *far_tokens)]))
    got_own_hidden = crossed(own_hidden, "expert", pair)
    far_flag = there(inner, own_grads, got_own_hidden)
    cot_sides.append(plane_gather([jnp.where(far_flag, *far_cots)]))
    got_own_grads = crossed(own_grads, "expert", pair)
    far_hidden, *far_pre = halves_forward(1, token_sides[1], [])
    out_rows = dot_f32(joined(own_hidden, far_hidden), w_down[0]).astype(jnp.bfloat16)
    out_back = sent_back(out_rows)
    far_grads = halves_backward(1, cot_sides[1], far_pre, [out_rows])
    own_sent = there(True, got_own_grads)
    gate_rows, up_rows = [when(own_sent, joined(own_grads[i], far_grads[i])) for i in range(2)]
    grad_rows = dot_f32(gate_rows, w_gate[0], CONTRACT_LAST) + dot_f32(
        up_rows, w_up[0], CONTRACT_LAST
    )
    grad_back = sent_back(grad_rows)

    got_far_hidden = crossed(far_hidden, "expert", pair)
    got_far_grads = [crossed(far_grads[i], "expert", pair) for i in range(2)]

    def relocated(own, far, got_own, got_far):
        return [jnp.where(moved, got_far, own), jnp.where(moved, got_own, far)]

    hidden = relocated(own_hidden, far_hidden, got_own_hidden, got_far_hidden)
    gate_grad, up_grad = [
        relocated(own_grads[i], far_grads[i], got_own_grads[i], got_far_grads[i])
        for i in range(2)
    ]
    held_rows = [
        pick(place, held_rank[side], None, *token_sides[side], row_count) for side in range(2)
    ]
    held_grads = [
        pick(place, held_rank[side], held_weight[side], *cot_sides[side], row_count)
        for side in range(2)
    ]

    def weight_grad(left, right):
        share = left[0].shape[1] // dp_count

        def product(part):
            total = 0.0
            for a, b in zip(left, right):
                columns = lax.dynamic_slice_in_dim(a, part * share, share, axis=1)
                total = total + dot_f32(columns, b, CONTRACT_ROWS)
            return total

        sent = product((my_dp + 1) % dp_count).astype(jnp.bfloat16)
        got = crossed(sent, "dp", 1)
        return got, ((product(my_dp) + got.astype(jnp.float32)) * (1.0 / dp_count))[None]

    got_down, grad_down = weight_grad(hidden, held_grads)
    got_gate, grad_gate = weight_grad(held_rows, gate_grad)
    _, grad_up = weight_grad(held_rows, up_grad)

    out_sides = spread(out_back, True, there(True, got_far_hidden))
    mixed = layer_reduce(*out_sides, tok_rows, layers, there(True, got_far_grads[0]), True)
    grad_sides = spread(grad_back, False, there(True, got_far_grads[0]))
    input_grad = layer_reduce(
        *grad_sides, tok_rows, layers, there(True, got_far_grads[1], got_down), there(True, got_gate)
    )
    return mixed, input_grad, grad_gate, grad_up, grad_down


def solution(mesh):
    tokens = P(("dp", "expert"), None)
    slots = P("expert", None, None)
    grads = P("expert", "dp", None)
    return jax.shard_map(
        body,
        mesh=mesh,
        in_specs=(tokens, tokens, tokens, tokens, P(), P(), slots, slots, slots),
        out_specs=(tokens, tokens, grads, grads, grads),
        check_vma=False,
    )
```

```python
import jax
import jax.numpy as jnp
from jax import lax
from jax.experimental import pallas as pl
from jax.experimental.pallas import tpu as pltpu
from jax.sharding import PartitionSpec as P

CONTRACT_ROWS = (((0,), (0,)), ((), ()))
CONTRACT_LAST = (((1,), (1,)), ((), ()))
PLANE = 4
FF_TILE = 256
VMEM_BYTES = 40 * 1024 * 1024


def dot_f32(a, b, dims=(((1,), (0,)), ((), ()))):
    return lax.dot_general(a, b, dims, preferred_element_type=jnp.float32)


def crossed(array, axis, flip):
    return lax.ppermute(array, axis, [(i, i ^ flip) for i in range(lax.axis_size(axis))])


def along(array, pairs):
    return lax.ppermute(array, "expert", pairs)


def line_pairs(owner_count):
    inner = [i for i in range(owner_count) if i // PLANE in (1, 2)]
    middle = [(i, i ^ 3 * PLANE) for i in inner]
    outward = [(i, i ^ PLANE) for i in inner]
    inward = [(i ^ PLANE, i) for i in inner]
    return middle, outward, inward


def there(flag, *arrays):
    for array in arrays:
        corner = array[tuple(slice(0, 1) for _ in array.shape)].reshape(())
        flag = flag & (corner == corner)
    return flag


def when(flag, array):
    return jnp.where(flag, array, jnp.zeros((), array.dtype))


def layer_gather(block, layers):
    if layers != 4:
        got = [block] + [crossed(block, "expert", j * PLANE) for j in range(1, layers)]
        far = jnp.concatenate(got[layers // 2 :])
        return got[: layers // 2], far, far, got[1:2]
    middle, outward, _ = line_pairs(layers * PLANE)
    near = crossed(block, "expert", PLANE)
    far = [along(block, middle), along(near, middle)]
    relayed = [along(array, outward) for array in far]
    return [block, near], jnp.concatenate(far), jnp.concatenate(relayed), [near, far[0]]


def plane_gather(blocks, flag):
    crossing = [crossed(block, "expert", 2) for block in blocks]
    mine = when(flag, jnp.stack([jnp.concatenate(blocks), jnp.concatenate(crossing)]))
    return mine, crossed(mine, "expert", 1)


def layer_reduce(own, far, tok_rows, layers, far_flag, near_flag):
    total = own[:tok_rows].astype(jnp.float32)
    if layers != 4:
        spread = jnp.concatenate([own, far])
        for j in range(1, layers):
            block = crossed(spread[j * tok_rows : (j + 1) * tok_rows], "expert", j * PLANE)
            total = total + block.astype(jnp.float32)
        return total.astype(jnp.bfloat16)
    middle, outward, inward = line_pairs(layers * PLANE)
    far_sum = (far.astype(jnp.float32) + along(far, inward).astype(jnp.float32)).astype(far.dtype)
    far_sum = when(far_flag, far_sum)
    near = own[tok_rows:]
    near_in = along(near, inward)
    got = along(far_sum, middle)
    near_sum = (near.astype(jnp.float32) + got[tok_rows:].astype(jnp.float32)).astype(far.dtype)
    near_sum = when(near_flag, near_sum)
    near_out = along(near_sum, outward)
    for block in (near_in, got[:tok_rows], near_out):
        total = total + block.astype(jnp.float32)
    return total.astype(jnp.bfloat16)


def rank_rows(hit, layers):
    half = layers // 2
    tok_rows = hit.shape[2]
    earlier = jnp.arange(tok_rows)[:, None] < jnp.arange(tok_rows)[None, :]
    within = jnp.einsum(
        "slt,tu->slu",
        hit.astype(jnp.bfloat16),
        earlier.astype(jnp.bfloat16),
        preferred_element_type=jnp.float32,
    ).astype(jnp.int32)
    count = jnp.sum(hit.astype(jnp.int32), axis=2)
    layer = jnp.arange(layers)
    ahead = (layer[:, None] < layer[None, :]) & (layer[:, None] // half == layer[None, :] // half)
    before = jnp.sum(jnp.where(ahead[None], count[:, :, None], 0), axis=1)
    return jnp.where(hit, within + before[:, :, None], -1)


def pick_rows(rank, source, row_count):
    place = lax.broadcasted_iota(jnp.int32, (row_count, rank.shape[1]), 0)
    chosen = place == rank
    one_hot = jnp.where(chosen, 1.0, 0.0).astype(jnp.bfloat16)
    return chosen, dot_f32(one_hot, source)


def pick_step(step, slot, rank_ref, mine_ref, other_ref, store, row_count):
    def stored(source_ref):
        rows = pick_rows(rank_ref[0], source_ref[0], row_count)[1]
        store(slot, rows.astype(jnp.bfloat16))

    @pl.when(step < 2)
    def _():
        stored(mine_ref)

    @pl.when((step >= 2) & (step < PLANE))
    def _():
        stored(other_ref)


def source_xor(step):
    return (step // 2) + 2 * (step % 2)


def slot_of(step, place_ref):
    return place_ref[0] ^ source_xor(jnp.minimum(step, PLANE - 1))


def source_specs(tokens, width):
    line = pl.BlockSpec((1, 1, tokens), lambda i, p: (source_xor(jnp.minimum(i, PLANE - 1)), 0, 0))
    mine = pl.BlockSpec((1, tokens, width), lambda i, p: (jnp.minimum(i, 1), 0, 0))
    other = pl.BlockSpec((1, tokens, width), lambda i, p: (jnp.clip(i - 2, 0, 1), 0, 0))
    return [line, mine, other]


def run(kernel, grid, in_specs, out_specs, out_shape, scratch, flops, args, earlier=()):
    moved = sum(a.size * a.dtype.itemsize for a in args)
    count = len(in_specs) + 1
    in_specs = in_specs + [pl.BlockSpec(memory_space=pl.ANY)] * len(earlier)
    if earlier:
        inner_kernel = kernel

        def kernel(*refs):
            inner_kernel(*refs[:count], *refs[count + len(earlier) :])

    return pl.pallas_call(
        kernel,
        grid_spec=pltpu.PrefetchScalarGridSpec(
            num_scalar_prefetch=1,
            grid=(grid,),
            in_specs=in_specs,
            out_specs=out_specs,
            scratch_shapes=scratch,
        ),
        out_shape=out_shape,
        compiler_params=pltpu.CompilerParams(vmem_limit_bytes=VMEM_BYTES),
        cost_estimate=pl.CostEstimate(flops=flops, bytes_accessed=moved, transcendentals=0),
    )(*args, *earlier)


def pick_tokens(place, rank, sides, row_count):
    _, tokens, width = sides[0][0].shape

    def kernel(place_ref, rank_ref, *refs):
        rows_ref = refs[-1]
        part = pl.program_id(0) // 2
        for i in range(PLANE):

            @pl.when(part == i)
            def _():
                rows = pick_rows(rank_ref[0, 0], refs[i][0], row_count)[1]
                rows_ref[...] = rows.astype(jnp.bfloat16)

    def source(first):
        return pl.BlockSpec((1, tokens, width), lambda i, p: (jnp.clip(i - first, 0, 1), 0, 0))

    def out_at(i, p):
        slot = p[0] ^ source_xor(i % PLANE)
        return ((i // PLANE) ^ p[2]) * PLANE + slot, 0

    line = pl.BlockSpec((1, 1, 1, tokens), lambda i, p: (i // PLANE, source_xor(i % PLANE), 0, 0))
    return run(
        kernel,
        2 * PLANE,
        [line] + [source(2 * i) for i in range(PLANE)],
        pl.BlockSpec((row_count, width), out_at),
        jax.ShapeDtypeStruct((2 * PLANE * row_count, width), jnp.bfloat16),
        [],
        4 * PLANE * row_count * tokens * width,
        [place, rank, *sides[0], *sides[1]],
    )


def cot_specs(cots, row_of):
    layers, _, tok_rows, width = cots.shape
    tokens = layers // 2 * tok_rows

    def line_at(i, p):
        side, source = row_of(i)
        return side, source ^ p[0], 0, 0

    def block_at(i, p):
        side, source = row_of(i)
        return side ^ p[1], source, 0, 0

    line = pl.BlockSpec((1, 1, 1, tokens), line_at)
    return [line, line, pl.BlockSpec((layers // 2, 1, tok_rows, width), block_at)]


def scaled_rows(rank_ref, weight_ref, cots_ref, row_count):
    source = cots_ref[...].reshape(-1, cots_ref.shape[-1])
    chosen, rows = pick_rows(rank_ref[0, 0], source, row_count)
    scale = jnp.sum(jnp.where(chosen, weight_ref[0, 0], 0.0), axis=1, keepdims=True)
    return (scale * rows).astype(jnp.bfloat16)


def pick_cots(place, rank, weight, cots, row_count):
    width = cots.shape[3]

    def kernel(place_ref, rank_ref, weight_ref, cots_ref, rows_ref):
        rows_ref[...] = scaled_rows(rank_ref, weight_ref, cots_ref, row_count)

    return run(
        kernel,
        2 * PLANE,
        cot_specs(cots, lambda i: (i // PLANE, i % PLANE)),
        pl.BlockSpec(
            (row_count, width), lambda i, p: (((i // PLANE) ^ p[2]) * PLANE + i % PLANE, 0)
        ),
        jax.ShapeDtypeStruct((2 * PLANE * row_count, width), jnp.bfloat16),
        [],
        2 * row_count * cots.size,
        [place, rank, weight, cots],
    )


def tile_at(step):
    return jnp.maximum(step - PLANE, 0)


def forward(place, rank, mine, other, w_gate, w_up, row_count, earlier):
    _, tokens, width = mine.shape
    ff = w_gate.shape[2]
    rows = PLANE * row_count

    def kernel(place_ref, rank_ref, mine_ref, other_ref, gate_ref, up_ref, *refs):
        hidden_ref, gate_pre_ref, up_pre_ref, rows_ref = refs
        step = pl.program_id(0)

        def store(slot, values):
            rows_ref[pl.ds(pl.multiple_of(slot * row_count, row_count), row_count), :] = values

        slot = slot_of(step, place_ref)
        pick_step(step, slot, rank_ref, mine_ref, other_ref, store, row_count)

        @pl.when(step >= PLANE)
        def _():
            gate_pre = dot_f32(rows_ref[...], gate_ref[0])
            up_pre = dot_f32(rows_ref[...], up_ref[0])
            gate_pre_ref[...] = gate_pre
            up_pre_ref[...] = up_pre
            hidden_ref[...] = (gate_pre * jax.nn.sigmoid(gate_pre) * up_pre).astype(jnp.bfloat16)

    weight_spec = pl.BlockSpec((1, width, FF_TILE), lambda i, p: (0, 0, tile_at(i)))
    out_spec = pl.BlockSpec((rows, FF_TILE), lambda i, p: (0, tile_at(i)))
    return run(
        kernel,
        PLANE + ff // FF_TILE,
        source_specs(tokens, width) + [weight_spec] * 2,
        [out_spec] * 3,
        [jax.ShapeDtypeStruct((rows, ff), t) for t in (jnp.bfloat16, jnp.float32, jnp.float32)],
        [pltpu.VMEM((rows, width), jnp.bfloat16)],
        4 * rows * width * ff,
        [place, rank, mine, other, w_gate, w_up],
        earlier,
    )


def backward(place, rank, weight, cots, w_down, own_pre, far_pre, row_count, earlier):
    width = cots.shape[3]
    ff = w_down.shape[1]
    rows = PLANE * row_count
    span = PLANE + ff // FF_TILE

    def kernel(place_ref, rank_ref, weight_ref, cots_ref, down_ref, *refs):
        own_gate_ref, own_up_ref, far_gate_ref, far_up_ref, gate_grad_ref, up_grad_ref, rows_ref = refs
        side, step = pl.program_id(0) // span, pl.program_id(0) % span

        @pl.when(step < PLANE)
        def _():
            start = pl.multiple_of(step * row_count, row_count)
            rows_ref[pl.ds(start, row_count), :] = scaled_rows(
                rank_ref, weight_ref, cots_ref, row_count
            )

        @pl.when(step >= PLANE)
        def _():
            hidden_grad = dot_f32(rows_ref[...], down_ref[0], CONTRACT_LAST)
            gate_pre = jnp.where(side == 0, own_gate_ref[...], far_gate_ref[...])
            up_pre = jnp.where(side == 0, own_up_ref[...], far_up_ref[...])
            sigma = jax.nn.sigmoid(gate_pre)
            slope = sigma * (1.0 + gate_pre * (1.0 - sigma))
            gate_grad_ref[0] = (hidden_grad * up_pre * slope).astype(jnp.bfloat16)
            up_grad_ref[0] = (hidden_grad * gate_pre * sigma).astype(jnp.bfloat16)

    def row_of(i):
        return i // span, jnp.minimum(i % span, PLANE - 1)

    def own_at(i, p):
        return 0, jnp.where(i < span, tile_at(i), ff // FF_TILE - 1)

    def far_at(i, p):
        return 0, tile_at(jnp.maximum(i - span, 0))

    own_spec, far_spec = [pl.BlockSpec((rows, FF_TILE), at) for at in (own_at, far_at)]
    down_spec = pl.BlockSpec((1, FF_TILE, width), lambda i, p: (0, tile_at(i % span), 0))
    out_spec = pl.BlockSpec((1, rows, FF_TILE), lambda i, p: (i // span, 0, tile_at(i % span)))
    return run(
        kernel,
        2 * span,
        cot_specs(cots, row_of) + [down_spec] + [own_spec] * 2 + [far_spec] * 2,
        [out_spec] * 2,
        [jax.ShapeDtypeStruct((2, rows, ff), jnp.bfloat16)] * 2,
        [pltpu.VMEM((rows, width), jnp.bfloat16)],
        4 * rows * width * ff,
        [place, rank, weight, cots, w_down, *own_pre, *far_pre],
        earlier,
    )


def body(tokens, cotangent, expert_ids, combine, placement, moves, w_gate, w_up, w_down):
    owner_count = lax.axis_size("expert")
    dp_count = lax.axis_size("dp")
    my_index = lax.axis_index("expert")
    my_dp = lax.axis_index("dp")
    tok_rows, width = tokens.shape
    choose_count = expert_ids.shape[1]
    layers = owner_count // PLANE
    half = layers // 2
    row_count = 3 * tok_rows * choose_count // (4 * PLANE)
    pair = owner_count // 2
    own_layer, my_place = my_index // PLANE, my_index % PLANE
    inner = (own_layer == 1) | (own_layer == 2)

    near_tokens, *far_tokens, _ = layer_gather(tokens, layers)
    cots = lax.all_gather(cotangent, "expert", axis=0, tiled=True)
    cots = cots.reshape(layers, PLANE, tok_rows, width)

    layer_ids = jnp.arange(layers, dtype=jnp.int32)
    order = own_layer ^ layer_ids
    if layers == 4:
        order = jnp.where(inner, jnp.stack([order[j] for j in (0, 1, 3, 2)]), order)
    routing = jnp.concatenate([expert_ids.astype(jnp.float32), combine], axis=1)
    lines = [routing] + [crossed(routing, "expert", j * PLANE) for j in range(1, layers)]
    routing = jnp.stack(lines).transpose(2, 0, 1)[:, layer_ids ^ own_layer]
    routing = jnp.stack([routing] + [crossed(routing, "expert", k) for k in range(1, PLANE)])
    ids, weights = routing[:, :choose_count], routing[:, choose_count:]

    slot_ids = jnp.arange(owner_count, dtype=jnp.int32)
    held = jnp.where(moves == 1, jnp.roll(placement, pair), placement)
    mine = slot_ids == my_index
    home_expert = jnp.sum(jnp.where(mine, placement, 0))
    held_expert = jnp.sum(jnp.where(mine, held, 0))
    my_move = jnp.sum(jnp.where(mine, moves, 0))
    moved = my_move == 1
    place = jnp.stack([my_place, own_layer // half, my_move]).astype(jnp.int32)
    plane_slots = own_layer * PLANE + jnp.arange(PLANE, dtype=jnp.int32)
    near = slot_ids[None, :] == plane_slots[:, None]
    plane_experts = jnp.sum(jnp.where(near, placement[None], 0), axis=1)

    def named(expert, source_ids, source_weights):
        match = source_ids == expert.astype(jnp.float32)
        return jnp.any(match, axis=1), jnp.sum(jnp.where(match, source_weights, 0.0), axis=1)

    sets = [
        named(home_expert, ids, weights),
        named(held_expert, ids, weights),
        named(plane_experts[:, None, None, None], ids[:1], weights[:1]),
    ]
    rank = rank_rows(jnp.concatenate([s[0] for s in sets]), layers)
    home_rank, held_rank, back_rank = [rank[i * PLANE : (i + 1) * PLANE] for i in range(3)]

    def in_order(array):
        array = array[:, order].reshape(PLANE, 2, 1, half * tok_rows)
        return array.transpose(1, 0, 2, 3)

    def in_layers(array):
        array = array.reshape(PLANE, 2, 1, half * tok_rows).transpose(1, 0, 2, 3)
        return jnp.where(place[1] == 0, array, array[::-1])

    token_rank, back_rank, back_weight = [in_order(a) for a in (home_rank, back_rank, sets[2][1])]
    held_token_rank = in_order(held_rank)

    groups = [[i * PLANE + j for j in range(PLANE)] for i in range(layers)]

    def joined(own, far):
        sides = [array.reshape(PLANE, row_count, -1) for array in (own, far)]
        return jnp.concatenate(sides, axis=1).reshape(2 * PLANE * row_count, -1)

    def sent_back(rows):
        rows = rows.astype(jnp.bfloat16).reshape(PLANE, 2 * row_count, width)
        return lax.all_to_all(
            rows, "expert", split_axis=0, concat_axis=0, axis_index_groups=groups, tiled=True
        )

    def spread(back, weighted, flag):
        sides = []
        for side in range(2):
            rows = back[:, side * row_count : (side + 1) * row_count]
            chosen = back_rank[side] == jnp.arange(row_count, dtype=jnp.int32)[None, :, None]
            chosen = chosen & flag
            if weighted:
                scale = jnp.sum(jnp.where(chosen, back_weight[side], 0.0), axis=2, keepdims=True)
                rows = (scale * rows.astype(jnp.float32)).astype(jnp.bfloat16)
            one_hot = chosen.astype(jnp.bfloat16).reshape(PLANE * row_count, -1)
            rows = rows.reshape(PLANE * row_count, width)
            sides.append(dot_f32(one_hot, rows, CONTRACT_ROWS).astype(jnp.bfloat16))
        return sides

    token_sides = [plane_gather(near_tokens, True)]
    own_hidden, *own_pre = forward(
        place, token_rank[0], *token_sides[0], w_gate, w_up, row_count, []
    )
    got_own_hidden = crossed(own_hidden, "expert", pair)
    far_half = jnp.where(there(inner, own_hidden), *far_tokens)
    token_sides.append(plane_gather([far_half], there(True, got_own_hidden)))
    far_hidden, *far_pre = forward(
        place, token_rank[1], *token_sides[1], w_gate, w_up, row_count, []
    )
    got_far_hidden = crossed(far_hidden, "expert", pair)
    out_rows = dot_f32(joined(own_hidden, far_hidden), w_down[0]).astype(jnp.bfloat16)
    out_back = sent_back(out_rows)
    home_rows = in_layers(home_rank), in_layers(sets[0][1])
    gate_grad, up_grad = backward(
        place, *home_rows, cots, w_down, own_pre, far_pre, row_count, [out_rows]
    )
    got_gate_grad = crossed(gate_grad, "expert", pair)
    got_up_grad = crossed(up_grad, "expert", pair)
    grad_rows = dot_f32(joined(*gate_grad), w_gate[0], CONTRACT_LAST) + dot_f32(
        joined(*up_grad), w_up[0], CONTRACT_LAST
    )
    grad_back = sent_back(grad_rows)

    def relocated(own, got):
        return jnp.where(moved, got, own).reshape(2 * PLANE * row_count, -1)

    hidden = relocated(
        jnp.stack([own_hidden, far_hidden]), jnp.stack([got_own_hidden, got_far_hidden])
    )
    held_rows = pick_tokens(place, held_token_rank, token_sides, row_count)
    held_grads = pick_cots(
        place, in_layers(held_rank), in_layers(sets[1][1]), cots, row_count
    )

    def weight_grad(left, right):
        share = left.shape[1] // dp_count

        def product(part):
            columns = lax.dynamic_slice_in_dim(left, part * share, share, axis=1)
            return dot_f32(columns, right, CONTRACT_ROWS)

        sent = product((my_dp + 1) % dp_count).astype(jnp.bfloat16)
        got = crossed(sent, "dp", 1)
        return got, ((product(my_dp) + got.astype(jnp.float32)) * (1.0 / dp_count))[None]

    got_down, grad_down = weight_grad(hidden, held_grads)
    got_gate, grad_gate = weight_grad(held_rows, relocated(gate_grad, got_gate_grad))
    _, grad_up = weight_grad(held_rows, relocated(up_grad, got_up_grad))

    out_sides = spread(out_back, True, there(True, got_far_hidden))
    mixed = layer_reduce(*out_sides, tok_rows, layers, there(True, got_down), True)
    grad_sides = spread(grad_back, False, there(True, got_gate_grad))
    input_grad = layer_reduce(
        *grad_sides, tok_rows, layers, there(True, got_up_grad), there(True, got_gate)
    )
    return mixed, input_grad, grad_gate, grad_up, grad_down


def solution(mesh):
    tokens = P(("dp", "expert"), None)
    slots = P("expert", None, None)
    grads = P("expert", "dp", None)
    return jax.shard_map(
        body,
        mesh=mesh,
        in_specs=(tokens, tokens, tokens, tokens, P(), P(), slots, slots, slots),
        out_specs=(tokens, tokens, grads, grads, grads),
        check_vma=False,
    )
```

```python
import jax
import jax.numpy as jnp
from jax import lax
from jax.experimental import pallas as pl
from jax.experimental.pallas import tpu as pltpu
from jax.sharding import PartitionSpec as P

CONTRACT_ROWS = (((0,), (0,)), ((), ()))
CONTRACT_LAST = (((1,), (1,)), ((), ()))
PLANE = 4
FF_TILE = 256
VMEM_BYTES = 48 * 1024 * 1024


def dot_f32(a, b, dims=(((1,), (0,)), ((), ()))):
    return lax.dot_general(a, b, dims, preferred_element_type=jnp.float32)


def crossed(array, axis, flip):
    return lax.ppermute(array, axis, [(i, i ^ flip) for i in range(lax.axis_size(axis))])


def along(array, pairs):
    return lax.ppermute(array, "expert", pairs)


def line_pairs(owner_count):
    inner = [i for i in range(owner_count) if i // PLANE in (1, 2)]
    middle = [(i, i ^ 3 * PLANE) for i in inner]
    outward = [(i, i ^ PLANE) for i in inner]
    inward = [(i ^ PLANE, i) for i in inner]
    return middle, outward, inward


def there(flag, *arrays):
    for array in arrays:
        corner = array[tuple(slice(0, 1) for _ in array.shape)].reshape(())
        flag = flag & (corner == corner)
    return flag


def when(flag, array):
    return jnp.where(flag, array, jnp.zeros((), array.dtype))


def layer_gather(block, layers, earlier):
    near = [block] + [crossed(block, "expert", j * PLANE) for j in range(1, layers // 2)]
    sent = when(there(True, *earlier), block)
    return near, [crossed(sent, "expert", j * PLANE) for j in range(layers // 2, layers)]


def plane_gather(blocks):
    crossing = [crossed(block, "expert", 2) for block in blocks]
    mine = jnp.stack([jnp.concatenate(blocks), jnp.concatenate(crossing)])
    return mine, crossed(mine, "expert", 1)


def layer_reduce(own, far, tok_rows, own_layer, layers, far_flag, near_flag):
    total = own[:tok_rows].astype(jnp.float32)
    if layers != 4:
        spread = jnp.concatenate([own, far])
        for j in range(1, layers):
            block = crossed(spread[j * tok_rows : (j + 1) * tok_rows], "expert", j * PLANE)
            total = total + block.astype(jnp.float32)
        return total.astype(jnp.bfloat16)
    middle, outward, inward = line_pairs(layers * PLANE)
    got = along(far, inward)
    swapped = jnp.concatenate([got[tok_rows:], got[:tok_rows]])
    far_sum = (far.astype(jnp.float32) + swapped.astype(jnp.float32)).astype(far.dtype)
    near = own[tok_rows:]
    near_in = along(near, inward)
    got = along(when(far_flag, far_sum), middle)
    near_sum = (near.astype(jnp.float32) + got[:tok_rows].astype(jnp.float32)).astype(far.dtype)
    near_out = along(when(near_flag, near_sum), outward)
    for block in (near_in, got[tok_rows:], near_out):
        total = total + block.astype(jnp.float32)
    return total.astype(jnp.bfloat16)


def rank_rows(hit, order):
    half = order.shape[0] // 2
    tok_rows = hit.shape[2]
    earlier = jnp.arange(tok_rows)[:, None] < jnp.arange(tok_rows)[None, :]
    within = jnp.einsum(
        "slt,tu->slu",
        hit.astype(jnp.bfloat16),
        earlier.astype(jnp.bfloat16),
        preferred_element_type=jnp.float32,
    ).astype(jnp.int32)
    count = jnp.sum(hit.astype(jnp.int32), axis=2)
    ahead = (order[:, None] < order[None, :]) & (order[:, None] // half == order[None, :] // half)
    before = jnp.sum(jnp.where(ahead[None], count[:, :, None], 0), axis=1)
    return jnp.where(hit, within + before[:, :, None], -1)


def pick_rows(rank, source, row_count):
    place = lax.broadcasted_iota(jnp.int32, (row_count, rank.shape[1]), 0)
    chosen = place == rank
    one_hot = jnp.where(chosen, 1.0, 0.0).astype(jnp.bfloat16)
    return chosen, dot_f32(one_hot, source)


def source_xor(step):
    return (step % PLANE) // 2 + 2 * (step % 2)


def run(kernel, grid, in_specs, out_specs, out_shape, scratch, flops, args, earlier=()):
    moved = sum(a.size * a.dtype.itemsize for a in args)
    count = len(in_specs) + 1
    in_specs = in_specs + [pl.BlockSpec(memory_space=pl.ANY)] * len(earlier)
    if earlier:
        inner_kernel = kernel

        def kernel(*refs):
            inner_kernel(*refs[:count], *refs[count + len(earlier) :])

    return pl.pallas_call(
        kernel,
        grid_spec=pltpu.PrefetchScalarGridSpec(
            num_scalar_prefetch=1,
            grid=(grid,),
            in_specs=in_specs,
            out_specs=out_specs,
            scratch_shapes=scratch,
        ),
        out_shape=out_shape,
        compiler_params=pltpu.CompilerParams(vmem_limit_bytes=VMEM_BYTES),
        cost_estimate=pl.CostEstimate(flops=flops, bytes_accessed=moved, transcendentals=0),
    )(*args, *earlier)


def row_block(side, source):
    return source * 2 + side


def token_specs(sides):
    _, tokens, width = sides[0][0].shape

    def line_at(i, p):
        i = jnp.minimum(i, 2 * PLANE - 1)
        return i // PLANE, source_xor(i), 0, 0

    def source(first):
        return pl.BlockSpec((1, tokens, width), lambda i, p: (jnp.clip(i - first, 0, 1), 0, 0))

    return [pl.BlockSpec((1, 1, 1, tokens), line_at)] + [source(2 * i) for i in range(PLANE)]


def each_source(step, rank_ref, source_refs, store, row_count):
    for i, source_ref in enumerate(source_refs):

        @pl.when(step // 2 == i)
        def _():
            store(pick_rows(rank_ref[0, 0], source_ref[0], row_count)[1].astype(jnp.bfloat16))


def pick_tokens(place, rank, sides, row_count, earlier):
    _, tokens, width = sides[0][0].shape

    def kernel(place_ref, rank_ref, *refs):
        def store(rows):
            refs[PLANE][...] = rows

        each_source(pl.program_id(0), rank_ref, refs[:PLANE], store, row_count)

    def out_at(i, p):
        return row_block((i // PLANE) ^ p[2], p[0] ^ source_xor(i)), 0

    return run(
        kernel,
        2 * PLANE,
        token_specs(sides),
        pl.BlockSpec((row_count, width), out_at),
        jax.ShapeDtypeStruct((2 * PLANE * row_count, width), jnp.bfloat16),
        [],
        4 * PLANE * row_count * tokens * width,
        [place, rank, *sides[0], *sides[1]],
        earlier,
    )


def scaled_each(step, rank_ref, weight_ref, source_refs, store, row_count):
    for i, source_ref in enumerate(source_refs):

        @pl.when(step // 2 == i)
        def _():
            chosen, rows = pick_rows(rank_ref[0, 0], source_ref[0], row_count)
            scale = jnp.sum(jnp.where(chosen, weight_ref[0, 0], 0.0), axis=1, keepdims=True)
            store((scale * rows).astype(jnp.bfloat16))


def pick_cots(place, rank, weight, sides, row_count, earlier):
    _, tokens, width = sides[0][0].shape

    def kernel(place_ref, rank_ref, weight_ref, *refs):
        def store(rows):
            refs[PLANE][...] = rows

        scaled_each(pl.program_id(0), rank_ref, weight_ref, refs[:PLANE], store, row_count)

    def out_at(i, p):
        return row_block((i // PLANE) ^ p[2], p[0] ^ source_xor(i)), 0

    specs = token_specs(sides)
    return run(
        kernel,
        2 * PLANE,
        specs[:1] + specs,
        pl.BlockSpec((row_count, width), out_at),
        jax.ShapeDtypeStruct((2 * PLANE * row_count, width), jnp.bfloat16),
        [],
        4 * PLANE * row_count * tokens * width,
        [place, rank, weight, *sides[0], *sides[1]],
        earlier,
    )


def tile_at(step):
    return jnp.maximum(step - 2 * PLANE, 0)


def row_store(step, place_ref, rows_ref, row_count):
    block = row_block(step // PLANE, place_ref[0] ^ source_xor(step))

    def store(rows):
        rows_ref[pl.ds(pl.multiple_of(block * row_count, row_count), row_count), :] = rows

    return store


def forward(place, rank, sides, w_gate, w_up, row_count):
    _, tokens, width = sides[0][0].shape
    ff = w_gate.shape[2]
    rows = 2 * PLANE * row_count

    def kernel(place_ref, rank_ref, *refs):
        gate_ref, up_ref, hidden_ref, gate_pre_ref, up_pre_ref, rows_ref = refs[PLANE:]
        step = pl.program_id(0)

        @pl.when(step < 2 * PLANE)
        def _():
            store = row_store(step, place_ref, rows_ref, row_count)
            each_source(step, rank_ref, refs[:PLANE], store, row_count)

        @pl.when(step >= 2 * PLANE)
        def _():
            gate_pre = dot_f32(rows_ref[...], gate_ref[0])
            up_pre = dot_f32(rows_ref[...], up_ref[0])
            gate_pre_ref[...] = gate_pre
            up_pre_ref[...] = up_pre
            hidden_ref[...] = (gate_pre * jax.nn.sigmoid(gate_pre) * up_pre).astype(jnp.bfloat16)

    weight_spec = pl.BlockSpec((1, width, FF_TILE), lambda i, p: (0, 0, tile_at(i)))
    out_spec = pl.BlockSpec((rows, FF_TILE), lambda i, p: (0, tile_at(i)))
    return run(
        kernel,
        2 * PLANE + ff // FF_TILE,
        token_specs(sides) + [weight_spec] * 2,
        [out_spec] * 3,
        [jax.ShapeDtypeStruct((rows, ff), t) for t in (jnp.bfloat16, jnp.float32, jnp.float32)],
        [pltpu.VMEM((rows, width), jnp.bfloat16)],
        4 * rows * width * ff,
        [place, rank, *sides[0], *sides[1], w_gate, w_up],
    )


def backward(place, rank, weight, sides, w_down, gate_pre, up_pre, row_count, earlier):
    _, tokens, width = sides[0][0].shape
    ff = w_down.shape[1]
    rows = 2 * PLANE * row_count

    def kernel(place_ref, rank_ref, weight_ref, *refs):
        down_ref, gate_pre_ref, up_pre_ref, gate_grad_ref, up_grad_ref, rows_ref = refs[PLANE:]
        step = pl.program_id(0)

        @pl.when(step < 2 * PLANE)
        def _():
            store = row_store(step, place_ref, rows_ref, row_count)
            scaled_each(step, rank_ref, weight_ref, refs[:PLANE], store, row_count)

        @pl.when(step >= 2 * PLANE)
        def _():
            hidden_grad = dot_f32(rows_ref[...], down_ref[0], CONTRACT_LAST)
            gate_pre = gate_pre_ref[...]
            sigma = jax.nn.sigmoid(gate_pre)
            slope = sigma * (1.0 + gate_pre * (1.0 - sigma))
            gate_grad_ref[...] = (hidden_grad * up_pre_ref[...] * slope).astype(jnp.bfloat16)
            up_grad_ref[...] = (hidden_grad * gate_pre * sigma).astype(jnp.bfloat16)

    specs = token_specs(sides)
    down_spec = pl.BlockSpec((1, FF_TILE, width), lambda i, p: (0, tile_at(i), 0))
    tile_spec = pl.BlockSpec((rows, FF_TILE), lambda i, p: (0, tile_at(i)))
    return run(
        kernel,
        2 * PLANE + ff // FF_TILE,
        specs[:1] + specs + [down_spec] + [tile_spec] * 2,
        [tile_spec] * 2,
        [jax.ShapeDtypeStruct((rows, ff), jnp.bfloat16)] * 2,
        [pltpu.VMEM((rows, width), jnp.bfloat16)],
        2 * rows * width * ff,
        [place, rank, weight, *sides[0], *sides[1], w_down, gate_pre, up_pre],
        earlier,
    )


def body(tokens, cotangent, expert_ids, combine, placement, moves, w_gate, w_up, w_down):
    owner_count = lax.axis_size("expert")
    dp_count = lax.axis_size("dp")
    my_index = lax.axis_index("expert")
    my_dp = lax.axis_index("dp")
    tok_rows, width = tokens.shape
    choose_count = expert_ids.shape[1]
    layers = owner_count // PLANE
    half = layers // 2
    row_count = 3 * tok_rows * choose_count // (4 * PLANE)
    pair = owner_count // 2
    own_layer, my_place = my_index // PLANE, my_index % PLANE
    near_tokens, far_tokens = layer_gather(tokens, layers, [])
    near_cots, far_cots = layer_gather(cotangent, layers, far_tokens)

    layer_ids = jnp.arange(layers, dtype=jnp.int32)
    order = own_layer ^ layer_ids
    routing = jnp.concatenate([expert_ids.astype(jnp.float32), combine], axis=1)
    routing = when(there(True, near_tokens[1]), routing)
    lines = [routing] + [crossed(routing, "expert", j * PLANE) for j in range(1, layers)]
    routing = jnp.stack(lines).transpose(2, 0, 1)
    routing = jnp.stack([routing] + [crossed(routing, "expert", k) for k in range(1, PLANE)])
    ids, weights = routing[:, :choose_count], routing[:, choose_count:]

    slot_ids = jnp.arange(owner_count, dtype=jnp.int32)
    held = jnp.where(moves == 1, jnp.roll(placement, pair), placement)
    mine = slot_ids == my_index
    home_expert = jnp.sum(jnp.where(mine, placement, 0))
    held_expert = jnp.sum(jnp.where(mine, held, 0))
    my_move = jnp.sum(jnp.where(mine, moves, 0))
    moved = my_move == 1
    place = jnp.stack([my_place, own_layer, my_move]).astype(jnp.int32)
    plane_slots = own_layer * PLANE + jnp.arange(PLANE, dtype=jnp.int32)
    near = slot_ids[None, :] == plane_slots[:, None]
    plane_experts = jnp.sum(jnp.where(near, placement[None], 0), axis=1)

    def named(expert, source_ids, source_weights):
        match = source_ids == expert.astype(jnp.float32)
        return jnp.any(match, axis=1), jnp.sum(jnp.where(match, source_weights, 0.0), axis=1)

    sets = [
        named(home_expert, ids, weights),
        named(held_expert, ids, weights),
        named(plane_experts[:, None, None, None], ids[:1], weights[:1]),
    ]
    rank = rank_rows(jnp.concatenate([s[0] for s in sets]), order)
    weight = jnp.concatenate([jnp.broadcast_to(s[1], (PLANE,) + s[1].shape[1:]) for s in sets])

    def halves(array):
        array = array.reshape(len(sets), PLANE, 2, 1, half * tok_rows)
        return array.transpose(0, 2, 1, 3, 4)

    home_rank, held_rank, back_rank = halves(rank)
    home_weight, held_weight, back_weight = halves(weight)

    groups = [[i * PLANE + j for j in range(PLANE)] for i in range(layers)]

    def sent_back(rows):
        rows = rows.reshape(PLANE, 2 * row_count, width)
        return lax.all_to_all(
            rows, "expert", split_axis=0, concat_axis=0, axis_index_groups=groups, tiled=True
        )

    def spread(back, weighted, flag):
        sides = []
        for side in range(2):
            rows = back[:, side * row_count : (side + 1) * row_count]
            chosen = back_rank[side] == jnp.arange(row_count, dtype=jnp.int32)[None, :, None]
            chosen = chosen & flag
            if weighted:
                scale = jnp.sum(jnp.where(chosen, back_weight[side], 0.0), axis=2, keepdims=True)
                rows = (scale * rows.astype(jnp.float32)).astype(jnp.bfloat16)
            one_hot = chosen.astype(jnp.bfloat16).reshape(PLANE * row_count, -1)
            rows = rows.reshape(PLANE * row_count, width)
            sides.append(dot_f32(one_hot, rows, CONTRACT_ROWS).astype(jnp.bfloat16))
        return sides

    token_sides = [plane_gather(near_tokens), plane_gather(far_tokens)]
    cot_sides = [plane_gather(near_cots), plane_gather(far_cots)]
    hidden, *pre = forward(place, home_rank, token_sides, w_gate, w_up, row_count)
    got_hidden = crossed(hidden, "expert", pair)
    out_rows = dot_f32(hidden, w_down[0]).astype(jnp.bfloat16)
    out_back = sent_back(out_rows)
    gate_grad, up_grad = backward(
        place, home_rank, home_weight, cot_sides, w_down, *pre, row_count, [out_rows]
    )
    got_gate_grad = crossed(gate_grad, "expert", pair)
    got_up_grad = crossed(up_grad, "expert", pair)
    grad_rows = (
        dot_f32(gate_grad, w_gate[0], CONTRACT_LAST) + dot_f32(up_grad, w_up[0], CONTRACT_LAST)
    ).astype(jnp.bfloat16)
    grad_back = sent_back(grad_rows)
    held_grads = pick_cots(place, held_rank, held_weight, cot_sides, row_count, [grad_rows])
    held_rows = pick_tokens(place, held_rank, token_sides, row_count, [held_grads])

    def relocated(own, got):
        return jnp.where(moved, got, own)

    def weight_grad(left, right):
        share = left.shape[1] // dp_count

        def product(part):
            columns = lax.dynamic_slice_in_dim(left, part * share, share, axis=1)
            return dot_f32(columns, right, CONTRACT_ROWS)

        sent = product((my_dp + 1) % dp_count).astype(jnp.bfloat16)
        got = crossed(sent, "dp", 1)
        return got, ((product(my_dp) + got.astype(jnp.float32)) * (1.0 / dp_count))[None]

    got_down, grad_down = weight_grad(relocated(hidden, got_hidden), held_grads)
    got_gate, grad_gate = weight_grad(held_rows, relocated(gate_grad, got_gate_grad))
    _, grad_up = weight_grad(held_rows, relocated(up_grad, got_up_grad))

    out_sides = spread(out_back, True, there(True, grad_rows))
    mixed = layer_reduce(*out_sides, tok_rows, own_layer, layers, there(True, got_down), True)
    grad_sides = spread(grad_back, False, there(True, got_gate_grad))
    input_grad = layer_reduce(
        *grad_sides, tok_rows, own_layer, layers, there(True, got_up_grad), there(True, got_gate)
    )
    return mixed, input_grad, grad_gate, grad_up, grad_down


def solution(mesh):
    tokens = P(("dp", "expert"), None)
    slots = P("expert", None, None)
    grads = P("expert", "dp", None)
    return jax.shard_map(
        body,
        mesh=mesh,
        in_specs=(tokens, tokens, tokens, tokens, P(), P(), slots, slots, slots),
        out_specs=(tokens, tokens, grads, grads, grads),
        check_vma=False,
    )
```

```python
import jax
import jax.numpy as jnp
from jax import lax
from jax.experimental import pallas as pl
from jax.experimental.pallas import tpu as pltpu
from jax.sharding import PartitionSpec as P

CONTRACT_ROWS = (((0,), (0,)), ((), ()))
CONTRACT_LAST = (((1,), (1,)), ((), ()))
PLANE = 4
FF_TILE = 256
VMEM_BYTES = 48 * 1024 * 1024


def dot_f32(a, b, dims=(((1,), (0,)), ((), ()))):
    return lax.dot_general(a, b, dims, preferred_element_type=jnp.float32)


def crossed(array, axis, flip):
    return lax.ppermute(array, axis, [(i, i ^ flip) for i in range(lax.axis_size(axis))])


def along(array, pairs):
    return lax.ppermute(array, "expert", pairs)


def line_pairs(owner_count):
    inner = [i for i in range(owner_count) if i // PLANE in (1, 2)]
    middle = [(i, i ^ 3 * PLANE) for i in inner]
    outward = [(i, i ^ PLANE) for i in inner]
    inward = [(i ^ PLANE, i) for i in inner]
    return middle, outward, inward


def there(flag, *arrays):
    for array in arrays:
        corner = array[tuple(slice(0, 1) for _ in array.shape)].reshape(())
        flag = flag & (corner == corner)
    return flag


def when(flag, array):
    return jnp.where(flag, array, jnp.zeros((), array.dtype))


def layer_gather(block, layers):
    return [block] + [crossed(block, "expert", j * PLANE) for j in range(1, layers)]


def plane_gather(blocks):
    crossing = [crossed(block, "expert", 2) for block in blocks]
    mine = jnp.stack([jnp.concatenate(blocks), jnp.concatenate(crossing)])
    return mine, crossed(mine, "expert", 1)


def layer_reduce(spread, tok_rows, layers, flag):
    blocks = [spread[j * tok_rows : (j + 1) * tok_rows] for j in range(layers)]
    if layers != 4:
        parts = [blocks[0]] + [crossed(blocks[j], "expert", j * PLANE) for j in range(1, layers)]
        return sum(part.astype(jnp.float32) for part in parts).astype(jnp.bfloat16)
    middle, outward, inward = line_pairs(layers * PLANE)

    def added(a, b):
        return (a.astype(jnp.float32) + b.astype(jnp.float32)).astype(jnp.bfloat16)

    got = along(spread[tok_rows:], inward)
    near_in, far_in = got[:tok_rows], got[tok_rows:]
    far_in = jnp.concatenate([far_in[tok_rows:], far_in[:tok_rows]])
    far_sum = added(spread[2 * tok_rows :], far_in)
    got = along(when(flag, far_sum), middle)
    near_out = along(added(blocks[1], got[:tok_rows]), outward)
    parts = [blocks[0], near_in, got[tok_rows:], near_out]
    return sum(part.astype(jnp.float32) for part in parts).astype(jnp.bfloat16)


def rank_rows(hit, order):
    half = order.shape[0] // 2
    tok_rows = hit.shape[2]
    earlier = jnp.arange(tok_rows)[:, None] < jnp.arange(tok_rows)[None, :]
    within = jnp.einsum(
        "slt,tu->slu",
        hit.astype(jnp.bfloat16),
        earlier.astype(jnp.bfloat16),
        preferred_element_type=jnp.float32,
    ).astype(jnp.int32)
    count = jnp.sum(hit.astype(jnp.int32), axis=2)
    ahead = (order[:, None] < order[None, :]) & (order[:, None] // half == order[None, :] // half)
    before = jnp.sum(jnp.where(ahead[None], count[:, :, None], 0), axis=1)
    return jnp.where(hit, within + before[:, :, None], -1)


def pick_rows(rank, source, row_count):
    place = lax.broadcasted_iota(jnp.int32, (row_count, rank.shape[1]), 0)
    chosen = place == rank
    one_hot = jnp.where(chosen, 1.0, 0.0).astype(jnp.bfloat16)
    return chosen, dot_f32(one_hot, source)


def source_xor(step):
    return (step % PLANE) // 2 + 2 * (step % 2)


def run(kernel, grid, in_specs, out_specs, out_shape, scratch, flops, args, earlier=()):
    moved = sum(a.size * a.dtype.itemsize for a in args)
    count = len(in_specs) + 1
    in_specs = in_specs + [pl.BlockSpec(memory_space=pl.ANY)] * len(earlier)
    if earlier:
        inner_kernel = kernel

        def kernel(*refs):
            inner_kernel(*refs[:count], *refs[count + len(earlier) :])

    return pl.pallas_call(
        kernel,
        grid_spec=pltpu.PrefetchScalarGridSpec(
            num_scalar_prefetch=1,
            grid=(grid,),
            in_specs=in_specs,
            out_specs=out_specs,
            scratch_shapes=scratch,
        ),
        out_shape=out_shape,
        compiler_params=pltpu.CompilerParams(vmem_limit_bytes=VMEM_BYTES),
        cost_estimate=pl.CostEstimate(flops=flops, bytes_accessed=moved, transcendentals=0),
    )(*args, *earlier)


def row_block(side, source):
    return source * 2 + side


def token_specs(sides):
    _, tokens, width = sides[0][0].shape

    def line_at(i, p):
        i = jnp.minimum(i, 2 * PLANE - 1)
        return i // PLANE, source_xor(i), 0, 0

    def source(first):
        return pl.BlockSpec((1, tokens, width), lambda i, p: (jnp.clip(i - first, 0, 1), 0, 0))

    return [pl.BlockSpec((1, 1, 1, tokens), line_at)] + [source(2 * i) for i in range(PLANE)]


def each_source(step, rank_ref, source_refs, store, row_count):
    for i, source_ref in enumerate(source_refs):

        @pl.when(step // 2 == i)
        def _():
            store(pick_rows(rank_ref[0, 0], source_ref[0], row_count)[1].astype(jnp.bfloat16))


def pick_tokens(place, rank, sides, row_count, earlier):
    _, tokens, width = sides[0][0].shape

    def kernel(place_ref, rank_ref, *refs):
        def store(rows):
            refs[PLANE][...] = rows

        each_source(pl.program_id(0), rank_ref, refs[:PLANE], store, row_count)

    def out_at(i, p):
        return row_block((i // PLANE) ^ p[2], p[0] ^ source_xor(i)), 0

    return run(
        kernel,
        2 * PLANE,
        token_specs(sides),
        pl.BlockSpec((row_count, width), out_at),
        jax.ShapeDtypeStruct((2 * PLANE * row_count, width), jnp.bfloat16),
        [],
        4 * PLANE * row_count * tokens * width,
        [place, rank, *sides[0], *sides[1]],
        earlier,
    )


def cot_specs(cots):
    layers, _, tok_rows, width = cots.shape
    tokens = layers // 2 * tok_rows

    def line_at(i, p):
        i = jnp.minimum(i, 2 * PLANE - 1)
        return i // PLANE, (i % PLANE) ^ p[0], 0, 0

    def block_at(i, p):
        i = jnp.minimum(i, 2 * PLANE - 1)
        return (i // PLANE) ^ p[1], i % PLANE, 0, 0

    line = pl.BlockSpec((1, 1, 1, tokens), line_at)
    return [line, line, pl.BlockSpec((layers // 2, 1, tok_rows, width), block_at)]


def scaled_rows(rank_ref, weight_ref, cots_ref, row_count):
    source = cots_ref[...].reshape(-1, cots_ref.shape[-1])
    chosen, rows = pick_rows(rank_ref[0, 0], source, row_count)
    scale = jnp.sum(jnp.where(chosen, weight_ref[0, 0], 0.0), axis=1, keepdims=True)
    return (scale * rows).astype(jnp.bfloat16)


def pick_cots(place, rank, weight, cots, row_count, earlier):
    width = cots.shape[3]

    def kernel(place_ref, rank_ref, weight_ref, cots_ref, rows_ref):
        rows_ref[...] = scaled_rows(rank_ref, weight_ref, cots_ref, row_count)

    def out_at(i, p):
        return row_block((i // PLANE) ^ p[2], i % PLANE), 0

    return run(
        kernel,
        2 * PLANE,
        cot_specs(cots),
        pl.BlockSpec((row_count, width), out_at),
        jax.ShapeDtypeStruct((2 * PLANE * row_count, width), jnp.bfloat16),
        [],
        2 * row_count * cots.size,
        [place, rank, weight, cots],
        earlier,
    )


def tile_at(step):
    return jnp.maximum(step - 2 * PLANE, 0)


def store_rows(block, rows, rows_ref, row_count):
    rows_ref[pl.ds(pl.multiple_of(block * row_count, row_count), row_count), :] = rows


def forward(place, rank, sides, w_gate, w_up, row_count):
    _, tokens, width = sides[0][0].shape
    ff = w_gate.shape[2]
    rows = 2 * PLANE * row_count

    def kernel(place_ref, rank_ref, *refs):
        gate_ref, up_ref, hidden_ref, gate_pre_ref, up_pre_ref, rows_ref = refs[PLANE:]
        step = pl.program_id(0)

        @pl.when(step < 2 * PLANE)
        def _():
            def store(rows):
                block = row_block(step // PLANE, place_ref[0] ^ source_xor(step))
                store_rows(block, rows, rows_ref, row_count)

            each_source(step, rank_ref, refs[:PLANE], store, row_count)

        @pl.when(step >= 2 * PLANE)
        def _():
            gate_pre = dot_f32(rows_ref[...], gate_ref[0])
            up_pre = dot_f32(rows_ref[...], up_ref[0])
            gate_pre_ref[...] = gate_pre
            up_pre_ref[...] = up_pre
            hidden_ref[...] = (gate_pre * jax.nn.sigmoid(gate_pre) * up_pre).astype(jnp.bfloat16)

    weight_spec = pl.BlockSpec((1, width, FF_TILE), lambda i, p: (0, 0, tile_at(i)))
    out_spec = pl.BlockSpec((rows, FF_TILE), lambda i, p: (0, tile_at(i)))
    return run(
        kernel,
        2 * PLANE + ff // FF_TILE,
        token_specs(sides) + [weight_spec] * 2,
        [out_spec] * 3,
        [jax.ShapeDtypeStruct((rows, ff), t) for t in (jnp.bfloat16, jnp.float32, jnp.float32)],
        [pltpu.VMEM((rows, width), jnp.bfloat16)],
        4 * rows * width * ff,
        [place, rank, *sides[0], *sides[1], w_gate, w_up],
    )


def backward(place, rank, weight, cots, w_down, gate_pre, up_pre, row_count, earlier):
    width = cots.shape[3]
    ff = w_down.shape[1]
    rows = 2 * PLANE * row_count

    def kernel(place_ref, rank_ref, weight_ref, cots_ref, down_ref, *refs):
        gate_pre_ref, up_pre_ref, gate_grad_ref, up_grad_ref, rows_ref = refs
        step = pl.program_id(0)

        @pl.when(step < 2 * PLANE)
        def _():
            block = row_block(step // PLANE, step % PLANE)
            rows = scaled_rows(rank_ref, weight_ref, cots_ref, row_count)
            store_rows(block, rows, rows_ref, row_count)

        @pl.when(step >= 2 * PLANE)
        def _():
            hidden_grad = dot_f32(rows_ref[...], down_ref[0], CONTRACT_LAST)
            gate_pre = gate_pre_ref[...]
            sigma = jax.nn.sigmoid(gate_pre)
            slope = sigma * (1.0 + gate_pre * (1.0 - sigma))
            gate_grad_ref[...] = (hidden_grad * up_pre_ref[...] * slope).astype(jnp.bfloat16)
            up_grad_ref[...] = (hidden_grad * gate_pre * sigma).astype(jnp.bfloat16)

    down_spec = pl.BlockSpec((1, FF_TILE, width), lambda i, p: (0, tile_at(i), 0))
    tile_spec = pl.BlockSpec((rows, FF_TILE), lambda i, p: (0, tile_at(i)))
    return run(
        kernel,
        2 * PLANE + ff // FF_TILE,
        cot_specs(cots) + [down_spec] + [tile_spec] * 2,
        [tile_spec] * 2,
        [jax.ShapeDtypeStruct((rows, ff), jnp.bfloat16)] * 2,
        [pltpu.VMEM((rows, width), jnp.bfloat16)],
        2 * rows * width * ff,
        [place, rank, weight, cots, w_down, gate_pre, up_pre],
        earlier,
    )


def body(tokens, cotangent, expert_ids, combine, placement, moves, w_gate, w_up, w_down):
    owner_count = lax.axis_size("expert")
    dp_count = lax.axis_size("dp")
    my_index = lax.axis_index("expert")
    my_dp = lax.axis_index("dp")
    tok_rows, width = tokens.shape
    choose_count = expert_ids.shape[1]
    layers = owner_count // PLANE
    half = layers // 2
    row_count = 3 * tok_rows * choose_count // (4 * PLANE)
    pair = owner_count // 2
    own_layer, my_place = my_index // PLANE, my_index % PLANE
    cots = lax.all_gather(cotangent, "expert", axis=0, tiled=True)
    cots = cots.reshape(layers, PLANE, tok_rows, width)
    gathered = layer_gather(tokens, layers)

    layer_ids = jnp.arange(layers, dtype=jnp.int32)
    order = own_layer ^ layer_ids
    routing = jnp.concatenate([expert_ids.astype(jnp.float32), combine], axis=1)
    routing = jnp.stack(layer_gather(routing, layers)).transpose(2, 0, 1)
    routings = [routing] + [crossed(routing, "expert", k) for k in range(1, PLANE)]
    routing = jnp.stack(routings)
    ids, weights = routing[:, :choose_count], routing[:, choose_count:]

    slot_ids = jnp.arange(owner_count, dtype=jnp.int32)
    held = jnp.where(moves == 1, jnp.roll(placement, pair), placement)
    mine = slot_ids == my_index
    home_expert = jnp.sum(jnp.where(mine, placement, 0))
    held_expert = jnp.sum(jnp.where(mine, held, 0))
    my_move = jnp.sum(jnp.where(mine, moves, 0))
    moved = my_move == 1
    place = jnp.stack([my_place, own_layer // half, my_move]).astype(jnp.int32)
    plane_slots = own_layer * PLANE + jnp.arange(PLANE, dtype=jnp.int32)
    near = slot_ids[None, :] == plane_slots[:, None]
    plane_experts = jnp.sum(jnp.where(near, placement[None], 0), axis=1)

    def named(expert, source_ids, source_weights):
        match = source_ids == expert.astype(jnp.float32)
        return jnp.any(match, axis=1), jnp.sum(jnp.where(match, source_weights, 0.0), axis=1)

    sets = [
        named(home_expert, ids, weights),
        named(held_expert, ids, weights),
        named(plane_experts[:, None, None, None], ids[:1], weights[:1]),
    ]
    rank = rank_rows(jnp.concatenate([s[0] for s in sets]), order)
    weight = jnp.concatenate([jnp.broadcast_to(s[1], (PLANE,) + s[1].shape[1:]) for s in sets])

    def halves(array):
        array = array.reshape(len(sets), PLANE, 2, 1, half * tok_rows)
        return array.transpose(0, 2, 1, 3, 4)

    home_rank, held_rank, back_rank = halves(rank)
    back_weight = halves(weight)[2]

    def by_layer(array):
        array = array.reshape(len(sets), PLANE, 2, half, tok_rows)
        return halves(array[:, :, :, layer_ids[:half] ^ (own_layer % half)])

    cot_rank, cot_weight = by_layer(rank), by_layer(weight)

    groups = [[i * PLANE + j for j in range(PLANE)] for i in range(layers)]

    def sent_back(rows):
        rows = rows.reshape(PLANE, 2 * row_count, width)
        return lax.all_to_all(
            rows, "expert", split_axis=0, concat_axis=0, axis_index_groups=groups, tiled=True
        )

    def spread(back, weighted, flag):
        numbers = jnp.arange(row_count, dtype=jnp.int32)[None, None, :, None]
        chosen = (back_rank.transpose(1, 0, 2, 3) == numbers) & flag
        rows = back.reshape(PLANE, 2, row_count, width)
        if weighted:
            weights = back_weight.transpose(1, 0, 2, 3)
            scale = jnp.sum(jnp.where(chosen, weights, 0.0), axis=3, keepdims=True)
            rows = (scale * rows.astype(jnp.float32)).astype(jnp.bfloat16)
        same = jnp.eye(2, dtype=bool)[None, :, None, :, None]
        one_hot = (chosen[:, :, :, None, :] & same).astype(jnp.bfloat16)
        one_hot = one_hot.reshape(2 * PLANE * row_count, layers * tok_rows)
        rows = rows.reshape(2 * PLANE * row_count, width)
        return dot_f32(one_hot, rows, CONTRACT_ROWS).astype(jnp.bfloat16)

    far_tokens = [when(there(True, *routings), block) for block in gathered[half:]]
    token_sides = [plane_gather(gathered[:half]), plane_gather(far_tokens)]
    hidden, *pre = forward(place, home_rank, token_sides, w_gate, w_up, row_count)
    got_hidden = crossed(hidden, "expert", pair)
    out_rows = dot_f32(hidden, w_down[0]).astype(jnp.bfloat16)
    out_back = sent_back(out_rows)
    gate_grad, up_grad = backward(
        place, cot_rank[0], cot_weight[0], cots, w_down, *pre, row_count, [out_rows]
    )
    got_gate_grad = crossed(gate_grad, "expert", pair)
    got_up_grad = crossed(up_grad, "expert", pair)
    grad_rows = (
        dot_f32(gate_grad, w_gate[0], CONTRACT_LAST) + dot_f32(up_grad, w_up[0], CONTRACT_LAST)
    ).astype(jnp.bfloat16)
    grad_back = sent_back(grad_rows)
    held_grads = pick_cots(place, cot_rank[1], cot_weight[1], cots, row_count, [grad_rows])
    held_rows = pick_tokens(place, held_rank, token_sides, row_count, [held_grads])

    out_spread = spread(out_back, True, there(True, grad_rows))
    grad_spread = spread(grad_back, False, there(True, got_gate_grad))
    after_up = there(True, got_up_grad)
    mixed = layer_reduce(out_spread, tok_rows, layers, after_up)
    input_grad = layer_reduce(grad_spread, tok_rows, layers, after_up)

    def weight_grad(left, own, got, transposed, earlier):
        right = jnp.where(moved & there(True, *earlier), got, own)
        if transposed:
            left, right = right, left
        share = left.shape[1] // dp_count

        def product(part):
            columns = lax.dynamic_slice_in_dim(left, part * share, share, axis=1)
            return dot_f32(columns, right, CONTRACT_ROWS)

        sent = product((my_dp + 1) % dp_count).astype(jnp.bfloat16)
        got = crossed(sent, "dp", 1)
        return got, ((product(my_dp) + got.astype(jnp.float32)) * (1.0 / dp_count))[None]

    got_down, grad_down = weight_grad(held_grads, hidden, got_hidden, True, [out_spread])
    got_gate, grad_gate = weight_grad(
        held_rows, gate_grad, got_gate_grad, False, [grad_spread, got_down]
    )
    _, grad_up = weight_grad(held_rows, up_grad, got_up_grad, False, [got_gate])
    return mixed, input_grad, grad_gate, grad_up, grad_down


def solution(mesh):
    tokens = P(("dp", "expert"), None)
    slots = P("expert", None, None)
    grads = P("expert", "dp", None)
    return jax.shard_map(
        body,
        mesh=mesh,
        in_specs=(tokens, tokens, tokens, tokens, P(), P(), slots, slots, slots),
        out_specs=(tokens, tokens, grads, grads, grads),
        check_vma=False,
    )
```

```python
import jax
import jax.numpy as jnp
from jax import lax
from jax.experimental import pallas as pl
from jax.experimental.pallas import tpu as pltpu
from jax.sharding import PartitionSpec as P

CONTRACT_ROWS = (((0,), (0,)), ((), ()))
CONTRACT_LAST = (((1,), (1,)), ((), ()))
PLANE = 4
FF_TILE = 256
VMEM_BYTES = 48 * 1024 * 1024


def dot_f32(a, b, dims=(((1,), (0,)), ((), ()))):
    return lax.dot_general(a, b, dims, preferred_element_type=jnp.float32)


def crossed(array, axis, flip):
    return lax.ppermute(array, axis, [(i, i ^ flip) for i in range(lax.axis_size(axis))])


def along(array, pairs):
    return lax.ppermute(array, "expert", pairs)


def line_pairs(owner_count):
    inner = [i for i in range(owner_count) if i // PLANE in (1, 2)]
    middle = [(i, i ^ 3 * PLANE) for i in inner]
    outward = [(i, i ^ PLANE) for i in inner]
    inward = [(i ^ PLANE, i) for i in inner]
    return middle, outward, inward


def there(flag, *arrays):
    for array in arrays:
        corner = array[tuple(slice(0, 1) for _ in array.shape)].reshape(())
        flag = flag & (corner == corner)
    return flag


def when(flag, array):
    return jnp.where(flag, array, jnp.zeros((), array.dtype))


def layer_gather(block, layers):
    return [block] + [crossed(block, "expert", j * PLANE) for j in range(1, layers)]


def plane_gather(blocks):
    crossing = [crossed(block, "expert", 2) for block in blocks]
    mine = jnp.stack([jnp.concatenate(blocks), jnp.concatenate(crossing)])
    return mine, crossed(mine, "expert", 1)


def layer_send(spread, tok_rows, layers):
    if layers != 4:
        blocks = [spread[j * tok_rows : (j + 1) * tok_rows] for j in range(1, layers)]
        return [crossed(block, "expert", j * PLANE) for j, block in enumerate(blocks, 1)]
    return [along(spread[tok_rows:], line_pairs(layers * PLANE)[2])]


def layer_reduce(spread, got, tok_rows, layers, flag):
    def total(parts):
        return sum(part.astype(jnp.float32) for part in parts).astype(jnp.bfloat16)

    if layers != 4:
        return total([spread[:tok_rows]] + got)
    middle, outward, _ = line_pairs(layers * PLANE)
    near_in, far_in = got[0][:tok_rows], got[0][tok_rows:]
    far_in = jnp.concatenate([far_in[tok_rows:], far_in[:tok_rows]])
    far_sum = total([spread[2 * tok_rows :], far_in])
    crossing = along(when(flag, far_sum), middle)
    near_sum = total([spread[tok_rows : 2 * tok_rows], crossing[:tok_rows]])
    near_out = along(near_sum, outward)
    return total([spread[:tok_rows], near_in, crossing[tok_rows:], near_out])


def rank_rows(hit, order):
    half = order.shape[0] // 2
    tok_rows = hit.shape[2]
    earlier = jnp.arange(tok_rows)[:, None] < jnp.arange(tok_rows)[None, :]
    within = jnp.einsum(
        "slt,tu->slu",
        hit.astype(jnp.bfloat16),
        earlier.astype(jnp.bfloat16),
        preferred_element_type=jnp.float32,
    ).astype(jnp.int32)
    count = jnp.sum(hit.astype(jnp.int32), axis=2)
    ahead = (order[:, None] < order[None, :]) & (order[:, None] // half == order[None, :] // half)
    before = jnp.sum(jnp.where(ahead[None], count[:, :, None], 0), axis=1)
    return jnp.where(hit, within + before[:, :, None], -1)


def pick_rows(rank, source, row_count):
    place = lax.broadcasted_iota(jnp.int32, (row_count, rank.shape[1]), 0)
    chosen = place == rank
    one_hot = jnp.where(chosen, 1.0, 0.0).astype(jnp.bfloat16)
    return chosen, dot_f32(one_hot, source)


def source_xor(step):
    return (step % PLANE) // 2 + 2 * (step % 2)


def run(kernel, grid, in_specs, out_specs, out_shape, scratch, flops, args, earlier=()):
    moved = sum(a.size * a.dtype.itemsize for a in args)
    count = len(in_specs) + 1
    in_specs = in_specs + [pl.BlockSpec(memory_space=pl.ANY)] * len(earlier)
    if earlier:
        inner_kernel = kernel

        def kernel(*refs):
            inner_kernel(*refs[:count], *refs[count + len(earlier) :])

    return pl.pallas_call(
        kernel,
        grid_spec=pltpu.PrefetchScalarGridSpec(
            num_scalar_prefetch=1,
            grid=(grid,),
            in_specs=in_specs,
            out_specs=out_specs,
            scratch_shapes=scratch,
        ),
        out_shape=out_shape,
        compiler_params=pltpu.CompilerParams(vmem_limit_bytes=VMEM_BYTES),
        cost_estimate=pl.CostEstimate(flops=flops, bytes_accessed=moved, transcendentals=0),
    )(*args, *earlier)


def row_block(side, source):
    return source * 2 + side


def token_specs(sides):
    _, tokens, width = sides[0][0].shape

    def line_at(i, p):
        i = jnp.minimum(i, 2 * PLANE - 1)
        return i // PLANE, source_xor(i), 0, 0

    def source(first):
        return pl.BlockSpec((1, tokens, width), lambda i, p: (jnp.clip(i - first, 0, 1), 0, 0))

    return [pl.BlockSpec((1, 1, 1, tokens), line_at)] + [source(2 * i) for i in range(PLANE)]


def each_source(step, rank_ref, source_refs, store, row_count):
    for i, source_ref in enumerate(source_refs):

        @pl.when(step // 2 == i)
        def _():
            store(pick_rows(rank_ref[0, 0], source_ref[0], row_count)[1].astype(jnp.bfloat16))


def pick_tokens(place, rank, sides, row_count, earlier):
    _, tokens, width = sides[0][0].shape

    def kernel(place_ref, rank_ref, *refs):
        def store(rows):
            refs[PLANE][...] = rows

        each_source(pl.program_id(0), rank_ref, refs[:PLANE], store, row_count)

    def out_at(i, p):
        return row_block((i // PLANE) ^ p[2], p[0] ^ source_xor(i)), 0

    return run(
        kernel,
        2 * PLANE,
        token_specs(sides),
        pl.BlockSpec((row_count, width), out_at),
        jax.ShapeDtypeStruct((2 * PLANE * row_count, width), jnp.bfloat16),
        [],
        4 * PLANE * row_count * tokens * width,
        [place, rank, *sides[0], *sides[1]],
        earlier,
    )


def cot_specs(cots):
    layers, _, tok_rows, width = cots.shape
    tokens = layers // 2 * tok_rows

    def line_at(i, p):
        i = jnp.minimum(i, 2 * PLANE - 1)
        return i // PLANE, (i % PLANE) ^ p[0], 0, 0

    def block_at(i, p):
        i = jnp.minimum(i, 2 * PLANE - 1)
        return (i // PLANE) ^ p[1], i % PLANE, 0, 0

    line = pl.BlockSpec((1, 1, 1, tokens), line_at)
    return [line, line, pl.BlockSpec((layers // 2, 1, tok_rows, width), block_at)]


def scaled_rows(rank_ref, weight_ref, cots_ref, row_count):
    source = cots_ref[...].reshape(-1, cots_ref.shape[-1])
    chosen, rows = pick_rows(rank_ref[0, 0], source, row_count)
    scale = jnp.sum(jnp.where(chosen, weight_ref[0, 0], 0.0), axis=1, keepdims=True)
    return (scale * rows).astype(jnp.bfloat16)


def pick_cots(place, rank, weight, cots, row_count, earlier):
    width = cots.shape[3]

    def kernel(place_ref, rank_ref, weight_ref, cots_ref, rows_ref):
        rows_ref[...] = scaled_rows(rank_ref, weight_ref, cots_ref, row_count)

    def out_at(i, p):
        return row_block((i // PLANE) ^ p[2], i % PLANE), 0

    return run(
        kernel,
        2 * PLANE,
        cot_specs(cots),
        pl.BlockSpec((row_count, width), out_at),
        jax.ShapeDtypeStruct((2 * PLANE * row_count, width), jnp.bfloat16),
        [],
        2 * row_count * cots.size,
        [place, rank, weight, cots],
        earlier,
    )


def tile_at(step):
    return jnp.maximum(step - 2 * PLANE, 0)


def store_rows(block, rows, rows_ref, row_count):
    rows_ref[pl.ds(pl.multiple_of(block * row_count, row_count), row_count), :] = rows


def forward(place, rank, sides, w_gate, w_up, row_count):
    _, tokens, width = sides[0][0].shape
    ff = w_gate.shape[2]
    rows = 2 * PLANE * row_count

    def kernel(place_ref, rank_ref, *refs):
        gate_ref, up_ref, hidden_ref, gate_pre_ref, up_pre_ref, rows_ref = refs[PLANE:]
        step = pl.program_id(0)

        @pl.when(step < 2 * PLANE)
        def _():
            def store(rows):
                block = row_block(step // PLANE, place_ref[0] ^ source_xor(step))
                store_rows(block, rows, rows_ref, row_count)

            each_source(step, rank_ref, refs[:PLANE], store, row_count)

        @pl.when(step >= 2 * PLANE)
        def _():
            gate_pre = dot_f32(rows_ref[...], gate_ref[0])
            up_pre = dot_f32(rows_ref[...], up_ref[0])
            gate_pre_ref[...] = gate_pre
            up_pre_ref[...] = up_pre
            hidden_ref[...] = (gate_pre * jax.nn.sigmoid(gate_pre) * up_pre).astype(jnp.bfloat16)

    weight_spec = pl.BlockSpec((1, width, FF_TILE), lambda i, p: (0, 0, tile_at(i)))
    out_spec = pl.BlockSpec((rows, FF_TILE), lambda i, p: (0, tile_at(i)))
    return run(
        kernel,
        2 * PLANE + ff // FF_TILE,
        token_specs(sides) + [weight_spec] * 2,
        [out_spec] * 3,
        [jax.ShapeDtypeStruct((rows, ff), t) for t in (jnp.bfloat16, jnp.float32, jnp.float32)],
        [pltpu.VMEM((rows, width), jnp.bfloat16)],
        4 * rows * width * ff,
        [place, rank, *sides[0], *sides[1], w_gate, w_up],
    )


def backward(place, rank, weight, cots, w_down, gate_pre, up_pre, row_count, earlier):
    width = cots.shape[3]
    ff = w_down.shape[1]
    rows = 2 * PLANE * row_count

    def kernel(place_ref, rank_ref, weight_ref, cots_ref, down_ref, *refs):
        gate_pre_ref, up_pre_ref, gate_grad_ref, up_grad_ref, rows_ref = refs
        step = pl.program_id(0)

        @pl.when(step < 2 * PLANE)
        def _():
            block = row_block(step // PLANE, step % PLANE)
            rows = scaled_rows(rank_ref, weight_ref, cots_ref, row_count)
            store_rows(block, rows, rows_ref, row_count)

        @pl.when(step >= 2 * PLANE)
        def _():
            hidden_grad = dot_f32(rows_ref[...], down_ref[0], CONTRACT_LAST)
            gate_pre = gate_pre_ref[...]
            sigma = jax.nn.sigmoid(gate_pre)
            slope = sigma * (1.0 + gate_pre * (1.0 - sigma))
            gate_grad_ref[...] = (hidden_grad * up_pre_ref[...] * slope).astype(jnp.bfloat16)
            up_grad_ref[...] = (hidden_grad * gate_pre * sigma).astype(jnp.bfloat16)

    down_spec = pl.BlockSpec((1, FF_TILE, width), lambda i, p: (0, tile_at(i), 0))
    tile_spec = pl.BlockSpec((rows, FF_TILE), lambda i, p: (0, tile_at(i)))
    return run(
        kernel,
        2 * PLANE + ff // FF_TILE,
        cot_specs(cots) + [down_spec] + [tile_spec] * 2,
        [tile_spec] * 2,
        [jax.ShapeDtypeStruct((rows, ff), jnp.bfloat16)] * 2,
        [pltpu.VMEM((rows, width), jnp.bfloat16)],
        2 * rows * width * ff,
        [place, rank, weight, cots, w_down, gate_pre, up_pre],
        earlier,
    )


def body(tokens, cotangent, expert_ids, combine, placement, moves, w_gate, w_up, w_down):
    owner_count = lax.axis_size("expert")
    dp_count = lax.axis_size("dp")
    my_index = lax.axis_index("expert")
    my_dp = lax.axis_index("dp")
    tok_rows, width = tokens.shape
    choose_count = expert_ids.shape[1]
    layers = owner_count // PLANE
    half = layers // 2
    row_count = 3 * tok_rows * choose_count // (4 * PLANE)
    pair = owner_count // 2
    own_layer, my_place = my_index // PLANE, my_index % PLANE
    gathered = layer_gather(tokens, layers)
    cots = when(there(True, *gathered), cotangent)
    cots = lax.all_gather(cots, "expert", axis=0, tiled=True)
    cots = cots.reshape(layers, PLANE, tok_rows, width)

    layer_ids = jnp.arange(layers, dtype=jnp.int32)
    order = own_layer ^ layer_ids
    routing = jnp.concatenate([expert_ids.astype(jnp.float32), combine], axis=1)
    routing = jnp.stack(layer_gather(routing, layers)).transpose(2, 0, 1)
    routings = [routing] + [crossed(routing, "expert", k) for k in range(1, PLANE)]
    routing = jnp.stack(routings)
    ids, weights = routing[:, :choose_count], routing[:, choose_count:]

    slot_ids = jnp.arange(owner_count, dtype=jnp.int32)
    held = jnp.where(moves == 1, jnp.roll(placement, pair), placement)
    mine = slot_ids == my_index
    home_expert = jnp.sum(jnp.where(mine, placement, 0))
    held_expert = jnp.sum(jnp.where(mine, held, 0))
    my_move = jnp.sum(jnp.where(mine, moves, 0))
    moved = my_move == 1
    place = jnp.stack([my_place, own_layer // half, my_move]).astype(jnp.int32)
    plane_slots = own_layer * PLANE + jnp.arange(PLANE, dtype=jnp.int32)
    near = slot_ids[None, :] == plane_slots[:, None]
    plane_experts = jnp.sum(jnp.where(near, placement[None], 0), axis=1)

    def named(expert, source_ids, source_weights):
        match = source_ids == expert.astype(jnp.float32)
        return jnp.any(match, axis=1), jnp.sum(jnp.where(match, source_weights, 0.0), axis=1)

    sets = [
        named(home_expert, ids, weights),
        named(held_expert, ids, weights),
        named(plane_experts[:, None, None, None], ids[:1], weights[:1]),
    ]
    rank = rank_rows(jnp.concatenate([s[0] for s in sets]), order)
    weight = jnp.concatenate([jnp.broadcast_to(s[1], (PLANE,) + s[1].shape[1:]) for s in sets])

    def halves(array):
        array = array.reshape(len(sets), PLANE, 2, 1, half * tok_rows)
        return array.transpose(0, 2, 1, 3, 4)

    home_rank, held_rank, back_rank = halves(rank)
    back_weight = halves(weight)[2]

    def by_layer(array):
        array = array.reshape(len(sets), PLANE, 2, half, tok_rows)
        return halves(array[:, :, :, layer_ids[:half] ^ (own_layer % half)])

    cot_rank, cot_weight = by_layer(rank), by_layer(weight)

    groups = [[i * PLANE + j for j in range(PLANE)] for i in range(layers)]

    def sent_back(rows):
        rows = rows.reshape(PLANE, 2 * row_count, width)
        return lax.all_to_all(
            rows, "expert", split_axis=0, concat_axis=0, axis_index_groups=groups, tiled=True
        )

    def spread(back, weighted, flag):
        numbers = jnp.arange(row_count, dtype=jnp.int32)[None, None, :, None]
        chosen = (back_rank.transpose(1, 0, 2, 3) == numbers) & flag
        rows = back.reshape(PLANE, 2, row_count, width)
        if weighted:
            weights = back_weight.transpose(1, 0, 2, 3)
            scale = jnp.sum(jnp.where(chosen, weights, 0.0), axis=3, keepdims=True)
            rows = (scale * rows.astype(jnp.float32)).astype(jnp.bfloat16)
        same = jnp.eye(2, dtype=bool)[None, :, None, :, None]
        one_hot = (chosen[:, :, :, None, :] & same).astype(jnp.bfloat16)
        one_hot = one_hot.reshape(2 * PLANE * row_count, layers * tok_rows)
        rows = rows.reshape(2 * PLANE * row_count, width)
        return dot_f32(one_hot, rows, CONTRACT_ROWS).astype(jnp.bfloat16)

    far_tokens = [when(there(True, *routings), block) for block in gathered[half:]]
    token_sides = [plane_gather(gathered[:half]), plane_gather(far_tokens)]
    hidden, *pre = forward(place, home_rank, token_sides, w_gate, w_up, row_count)
    got_hidden = crossed(hidden, "expert", pair)
    out_rows = dot_f32(hidden, w_down[0]).astype(jnp.bfloat16)
    out_back = sent_back(out_rows)
    gate_grad, up_grad = backward(
        place, cot_rank[0], cot_weight[0], cots, w_down, *pre, row_count, [out_rows, got_hidden]
    )
    got_gate_grad = crossed(gate_grad, "expert", pair)
    got_up_grad = crossed(when(there(True, got_gate_grad), up_grad), "expert", pair)
    grad_rows = (
        dot_f32(gate_grad, w_gate[0], CONTRACT_LAST) + dot_f32(up_grad, w_up[0], CONTRACT_LAST)
    ).astype(jnp.bfloat16)
    grad_back = sent_back(grad_rows)
    held_grads = pick_cots(place, cot_rank[1], cot_weight[1], cots, row_count, [grad_rows])
    held_rows = pick_tokens(place, held_rank, token_sides, row_count, [held_grads])

    out_spread = spread(out_back, True, there(True, grad_rows))
    grad_spread = spread(grad_back, False, True)
    out_in, grad_in = [layer_send(a, tok_rows, layers) for a in (out_spread, grad_spread)]
    mixed = layer_reduce(out_spread, out_in, tok_rows, layers, there(True, got_gate_grad))
    input_grad = layer_reduce(grad_spread, grad_in, tok_rows, layers, there(True, got_up_grad))

    def weight_grad(left, own, got, transposed, earlier):
        right = jnp.where(moved & there(True, *earlier), got, own)
        if transposed:
            left, right = right, left
        share = left.shape[1] // dp_count

        def product(part):
            columns = lax.dynamic_slice_in_dim(left, part * share, share, axis=1)
            return dot_f32(columns, right, CONTRACT_ROWS)

        sent = product((my_dp + 1) % dp_count).astype(jnp.bfloat16)
        got = crossed(sent, "dp", 1)
        return got, ((product(my_dp) + got.astype(jnp.float32)) * (1.0 / dp_count))[None]

    _, grad_down = weight_grad(held_grads, hidden, got_hidden, True, [])
    _, grad_gate = weight_grad(held_rows, gate_grad, got_gate_grad, False, [])
    _, grad_up = weight_grad(held_rows, up_grad, got_up_grad, False, [])
    return mixed, input_grad, grad_gate, grad_up, grad_down


def solution(mesh):
    tokens = P(("dp", "expert"), None)
    slots = P("expert", None, None)
    grads = P("expert", "dp", None)
    return jax.shard_map(
        body,
        mesh=mesh,
        in_specs=(tokens, tokens, tokens, tokens, P(), P(), slots, slots, slots),
        out_specs=(tokens, tokens, grads, grads, grads),
        check_vma=False,
    )
```

```python
import jax
import jax.numpy as jnp
from jax import lax
from jax.experimental import pallas as pl
from jax.experimental.pallas import tpu as pltpu
from jax.sharding import PartitionSpec as P

CONTRACT_ROWS = (((0,), (0,)), ((), ()))
CONTRACT_LAST = (((1,), (1,)), ((), ()))
PLANE = 4
FF_TILE = 256
VMEM_BYTES = 48 * 1024 * 1024


def dot_f32(a, b, dims=(((1,), (0,)), ((), ()))):
    return lax.dot_general(a, b, dims, preferred_element_type=jnp.float32)


def crossed(array, axis, flip):
    return lax.ppermute(array, axis, [(i, i ^ flip) for i in range(lax.axis_size(axis))])


def along(array, pairs):
    return lax.ppermute(array, "expert", pairs)


def line_pairs(owner_count):
    inner = [i for i in range(owner_count) if i // PLANE in (1, 2)]
    middle = [(i, i ^ 3 * PLANE) for i in inner]
    outward = [(i, i ^ PLANE) for i in inner]
    inward = [(i ^ PLANE, i) for i in inner]
    return middle, outward, inward


def there(flag, *arrays):
    for array in arrays:
        corner = array[tuple(slice(0, 1) for _ in array.shape)].reshape(())
        flag = flag & (corner == corner)
    return flag


def when(flag, array):
    return jnp.where(flag, array, jnp.zeros((), array.dtype))


def layer_gather(block, inner, layers):
    if layers != 4:
        got = [block] + [crossed(block, "expert", j * PLANE) for j in range(1, layers)]
        return jnp.concatenate(got[: layers // 2]), jnp.concatenate(got[layers // 2 :])
    middle, outward, _ = line_pairs(layers * PLANE)
    near = crossed(block, "expert", PLANE)
    far = [along(block, middle), along(near, middle)]
    relayed = [along(array, outward) for array in far]
    far_half = jnp.where(inner, jnp.concatenate(far), jnp.concatenate(relayed))
    return jnp.concatenate([block, near]), far_half


def plane_gather(half):
    mine = jnp.stack([half, crossed(half, "expert", 2)])
    return mine, crossed(mine, "expert", 1)


def layer_send(spread, tok_rows, layers):
    if layers != 4:
        blocks = [spread[j * tok_rows : (j + 1) * tok_rows] for j in range(1, layers)]
        return [crossed(block, "expert", j * PLANE) for j, block in enumerate(blocks, 1)]
    return [along(spread[tok_rows:], line_pairs(layers * PLANE)[2])]


def layer_reduce(spread, got, tok_rows, layers, flag):
    def total(parts):
        return sum(part.astype(jnp.float32) for part in parts).astype(jnp.bfloat16)

    if layers != 4:
        return total([spread[:tok_rows]] + got)
    middle, outward, _ = line_pairs(layers * PLANE)
    near_in, far_in = got[0][:tok_rows], got[0][tok_rows:]
    far_sum = total([spread[2 * tok_rows :], far_in])
    crossing = along(when(flag, far_sum), middle)
    near_sum = total([spread[tok_rows : 2 * tok_rows], crossing[tok_rows:]])
    near_out = along(near_sum, outward)
    return total([spread[:tok_rows], near_in, crossing[:tok_rows], near_out])


def rank_rows(hit, order):
    half = order.shape[0] // 2
    tok_rows = hit.shape[2]
    earlier = jnp.arange(tok_rows)[:, None] < jnp.arange(tok_rows)[None, :]
    within = jnp.einsum(
        "slt,tu->slu",
        hit.astype(jnp.bfloat16),
        earlier.astype(jnp.bfloat16),
        preferred_element_type=jnp.float32,
    ).astype(jnp.int32)
    count = jnp.sum(hit.astype(jnp.int32), axis=2)
    ahead = (order[:, None] < order[None, :]) & (order[:, None] // half == order[None, :] // half)
    before = jnp.sum(jnp.where(ahead[None], count[:, :, None], 0), axis=1)
    return jnp.where(hit, within + before[:, :, None], -1)


def pick_rows(rank, source, row_count):
    place = lax.broadcasted_iota(jnp.int32, (row_count, rank.shape[1]), 0)
    chosen = place == rank
    one_hot = jnp.where(chosen, 1.0, 0.0).astype(jnp.bfloat16)
    return chosen, dot_f32(one_hot, source)


def source_xor(step):
    return (step % PLANE) // 2 + 2 * (step % 2)


def run(kernel, grid, in_specs, out_specs, out_shape, scratch, flops, args, earlier=()):
    moved = sum(a.size * a.dtype.itemsize for a in args)
    count = len(in_specs) + 1
    in_specs = in_specs + [pl.BlockSpec(memory_space=pl.ANY)] * len(earlier)
    if earlier:
        inner_kernel = kernel

        def kernel(*refs):
            inner_kernel(*refs[:count], *refs[count + len(earlier) :])

    return pl.pallas_call(
        kernel,
        grid_spec=pltpu.PrefetchScalarGridSpec(
            num_scalar_prefetch=1,
            grid=(grid,),
            in_specs=in_specs,
            out_specs=out_specs,
            scratch_shapes=scratch,
        ),
        out_shape=out_shape,
        compiler_params=pltpu.CompilerParams(vmem_limit_bytes=VMEM_BYTES),
        cost_estimate=pl.CostEstimate(flops=flops, bytes_accessed=moved, transcendentals=0),
    )(*args, *earlier)


def row_block(side, source):
    return source * 2 + side


def token_specs(sides):
    _, tokens, width = sides[0][0].shape

    def line_at(i, p):
        i = jnp.minimum(i, 2 * PLANE - 1)
        return i // PLANE, source_xor(i), 0, 0

    def source(first):
        return pl.BlockSpec((1, tokens, width), lambda i, p: (jnp.clip(i - first, 0, 1), 0, 0))

    return [pl.BlockSpec((1, 1, 1, tokens), line_at)] + [source(2 * i) for i in range(PLANE)]


def each_source(step, rank_ref, source_refs, store, row_count):
    for i, source_ref in enumerate(source_refs):

        @pl.when(step // 2 == i)
        def _():
            store(pick_rows(rank_ref[0, 0], source_ref[0], row_count)[1].astype(jnp.bfloat16))


def pick_tokens(place, rank, sides, row_count, earlier):
    _, tokens, width = sides[0][0].shape

    def kernel(place_ref, rank_ref, *refs):
        def store(rows):
            refs[PLANE][...] = rows

        each_source(pl.program_id(0), rank_ref, refs[:PLANE], store, row_count)

    def out_at(i, p):
        return row_block((i // PLANE) ^ p[2], p[0] ^ source_xor(i)), 0

    return run(
        kernel,
        2 * PLANE,
        token_specs(sides),
        pl.BlockSpec((row_count, width), out_at),
        jax.ShapeDtypeStruct((2 * PLANE * row_count, width), jnp.bfloat16),
        [],
        4 * PLANE * row_count * tokens * width,
        [place, rank, *sides[0], *sides[1]],
        earlier,
    )


def scaled_each(step, rank_ref, weight_ref, source_refs, store, row_count):
    for i, source_ref in enumerate(source_refs):

        @pl.when(step // 2 == i)
        def _():
            chosen, rows = pick_rows(rank_ref[0, 0], source_ref[0], row_count)
            scale = jnp.sum(jnp.where(chosen, weight_ref[0, 0], 0.0), axis=1, keepdims=True)
            store((scale * rows).astype(jnp.bfloat16))


def pick_cots(place, rank, weight, sides, row_count, earlier):
    _, tokens, width = sides[0][0].shape

    def kernel(place_ref, rank_ref, weight_ref, *refs):
        def store(rows):
            refs[PLANE][...] = rows

        scaled_each(pl.program_id(0), rank_ref, weight_ref, refs[:PLANE], store, row_count)

    def out_at(i, p):
        return row_block((i // PLANE) ^ p[2], p[0] ^ source_xor(i)), 0

    specs = token_specs(sides)
    return run(
        kernel,
        2 * PLANE,
        specs[:1] + specs,
        pl.BlockSpec((row_count, width), out_at),
        jax.ShapeDtypeStruct((2 * PLANE * row_count, width), jnp.bfloat16),
        [],
        4 * PLANE * row_count * tokens * width,
        [place, rank, weight, *sides[0], *sides[1]],
        earlier,
    )


def tile_at(step):
    return jnp.maximum(step - 2 * PLANE, 0)


def store_rows(block, rows, rows_ref, row_count):
    rows_ref[pl.ds(pl.multiple_of(block * row_count, row_count), row_count), :] = rows


def forward(place, rank, sides, w_gate, w_up, row_count):
    _, tokens, width = sides[0][0].shape
    ff = w_gate.shape[2]
    rows = 2 * PLANE * row_count

    def kernel(place_ref, rank_ref, *refs):
        gate_ref, up_ref, hidden_ref, gate_pre_ref, up_pre_ref, rows_ref = refs[PLANE:]
        step = pl.program_id(0)

        @pl.when(step < 2 * PLANE)
        def _():
            def store(rows):
                block = row_block(step // PLANE, place_ref[0] ^ source_xor(step))
                store_rows(block, rows, rows_ref, row_count)

            each_source(step, rank_ref, refs[:PLANE], store, row_count)

        @pl.when(step >= 2 * PLANE)
        def _():
            gate_pre = dot_f32(rows_ref[...], gate_ref[0])
            up_pre = dot_f32(rows_ref[...], up_ref[0])
            gate_pre_ref[...] = gate_pre
            up_pre_ref[...] = up_pre
            hidden_ref[...] = (gate_pre * jax.nn.sigmoid(gate_pre) * up_pre).astype(jnp.bfloat16)

    weight_spec = pl.BlockSpec((1, width, FF_TILE), lambda i, p: (0, 0, tile_at(i)))
    out_spec = pl.BlockSpec((rows, FF_TILE), lambda i, p: (0, tile_at(i)))
    return run(
        kernel,
        2 * PLANE + ff // FF_TILE,
        token_specs(sides) + [weight_spec] * 2,
        [out_spec] * 3,
        [jax.ShapeDtypeStruct((rows, ff), t) for t in (jnp.bfloat16, jnp.float32, jnp.float32)],
        [pltpu.VMEM((rows, width), jnp.bfloat16)],
        4 * rows * width * ff,
        [place, rank, *sides[0], *sides[1], w_gate, w_up],
    )


def backward(place, rank, weight, sides, w_down, gate_pre, up_pre, row_count, earlier):
    _, tokens, width = sides[0][0].shape
    ff = w_down.shape[1]
    rows = 2 * PLANE * row_count

    def kernel(place_ref, rank_ref, weight_ref, *refs):
        down_ref, gate_pre_ref, up_pre_ref, gate_grad_ref, up_grad_ref, rows_ref = refs[PLANE:]
        step = pl.program_id(0)

        @pl.when(step < 2 * PLANE)
        def _():
            def store(rows):
                block = row_block(step // PLANE, place_ref[0] ^ source_xor(step))
                store_rows(block, rows, rows_ref, row_count)

            scaled_each(step, rank_ref, weight_ref, refs[:PLANE], store, row_count)

        @pl.when(step >= 2 * PLANE)
        def _():
            hidden_grad = dot_f32(rows_ref[...], down_ref[0], CONTRACT_LAST)
            gate_pre = gate_pre_ref[...]
            sigma = jax.nn.sigmoid(gate_pre)
            slope = sigma * (1.0 + gate_pre * (1.0 - sigma))
            gate_grad_ref[...] = (hidden_grad * up_pre_ref[...] * slope).astype(jnp.bfloat16)
            up_grad_ref[...] = (hidden_grad * gate_pre * sigma).astype(jnp.bfloat16)

    specs = token_specs(sides)
    down_spec = pl.BlockSpec((1, FF_TILE, width), lambda i, p: (0, tile_at(i), 0))
    tile_spec = pl.BlockSpec((rows, FF_TILE), lambda i, p: (0, tile_at(i)))
    return run(
        kernel,
        2 * PLANE + ff // FF_TILE,
        specs[:1] + specs + [down_spec] + [tile_spec] * 2,
        [tile_spec] * 2,
        [jax.ShapeDtypeStruct((rows, ff), jnp.bfloat16)] * 2,
        [pltpu.VMEM((rows, width), jnp.bfloat16)],
        2 * rows * width * ff,
        [place, rank, weight, *sides[0], *sides[1], w_down, gate_pre, up_pre],
        earlier,
    )


def body(tokens, cotangent, expert_ids, combine, placement, moves, w_gate, w_up, w_down):
    owner_count = lax.axis_size("expert")
    dp_count = lax.axis_size("dp")
    my_index = lax.axis_index("expert")
    my_dp = lax.axis_index("dp")
    tok_rows, width = tokens.shape
    choose_count = expert_ids.shape[1]
    layers = owner_count // PLANE
    half = layers // 2
    row_count = 3 * tok_rows * choose_count // (4 * PLANE)
    pair = owner_count // 2
    own_layer, my_place = my_index // PLANE, my_index % PLANE
    inner = (own_layer == 1) | (own_layer == 2)
    token_sides = [plane_gather(side) for side in layer_gather(tokens, inner, layers)]
    cot_sides = [plane_gather(side) for side in layer_gather(cotangent, inner, layers)]

    layer_ids = jnp.arange(layers, dtype=jnp.int32)
    order = own_layer ^ layer_ids
    if layers == 4:
        order = jnp.where(inner, jnp.stack([order[j] for j in (0, 1, 3, 2)]), order)
    routing = jnp.concatenate([expert_ids.astype(jnp.float32), combine], axis=1)
    lines = [routing] + [crossed(routing, "expert", j * PLANE) for j in range(1, layers)]
    if layers == 4:
        lines = lines[:2] + [jnp.where(inner, a, b) for a, b in (lines[:1:-1], lines[2:])]
    routing = jnp.stack(lines).transpose(2, 0, 1)
    routings = [routing] + [crossed(routing, "expert", k) for k in range(1, PLANE)]
    routing = jnp.stack(routings)
    ids, weights = routing[:, :choose_count], routing[:, choose_count:]

    slot_ids = jnp.arange(owner_count, dtype=jnp.int32)
    held = jnp.where(moves == 1, jnp.roll(placement, pair), placement)
    mine = slot_ids == my_index
    home_expert = jnp.sum(jnp.where(mine, placement, 0))
    held_expert = jnp.sum(jnp.where(mine, held, 0))
    my_move = jnp.sum(jnp.where(mine, moves, 0))
    moved = my_move == 1
    place = jnp.stack([my_place, own_layer // half, my_move]).astype(jnp.int32)
    plane_slots = own_layer * PLANE + jnp.arange(PLANE, dtype=jnp.int32)
    near = slot_ids[None, :] == plane_slots[:, None]
    plane_experts = jnp.sum(jnp.where(near, placement[None], 0), axis=1)

    def named(expert, source_ids, source_weights):
        match = source_ids == expert.astype(jnp.float32)
        return jnp.any(match, axis=1), jnp.sum(jnp.where(match, source_weights, 0.0), axis=1)

    sets = [
        named(home_expert, ids, weights),
        named(held_expert, ids, weights),
        named(plane_experts[:, None, None, None], ids[:1], weights[:1]),
    ]
    rank = rank_rows(jnp.concatenate([s[0] for s in sets]), order)
    weight = jnp.concatenate([jnp.broadcast_to(s[1], (PLANE,) + s[1].shape[1:]) for s in sets])

    def halves(array):
        array = array.reshape(len(sets), PLANE, 2, 1, half * tok_rows)
        return array.transpose(0, 2, 1, 3, 4)

    home_rank, held_rank, back_rank = halves(rank)
    home_weight, held_weight, back_weight = halves(weight)

    groups = [[i * PLANE + j for j in range(PLANE)] for i in range(layers)]

    def sent_back(rows):
        rows = rows.reshape(PLANE, 2 * row_count, width)
        return lax.all_to_all(
            rows, "expert", split_axis=0, concat_axis=0, axis_index_groups=groups, tiled=True
        )

    def spread(back, weighted, flag):
        numbers = jnp.arange(row_count, dtype=jnp.int32)[None, None, :, None]
        chosen = (back_rank.transpose(1, 0, 2, 3) == numbers) & flag
        rows = back.reshape(PLANE, 2, row_count, width)
        if weighted:
            weights = back_weight.transpose(1, 0, 2, 3)
            scale = jnp.sum(jnp.where(chosen, weights, 0.0), axis=3, keepdims=True)
            rows = (scale * rows.astype(jnp.float32)).astype(jnp.bfloat16)
        same = jnp.eye(2, dtype=bool)[None, :, None, :, None]
        one_hot = (chosen[:, :, :, None, :] & same).astype(jnp.bfloat16)
        one_hot = one_hot.reshape(2 * PLANE * row_count, layers * tok_rows)
        rows = rows.reshape(2 * PLANE * row_count, width)
        return dot_f32(one_hot, rows, CONTRACT_ROWS).astype(jnp.bfloat16)

    hidden, *pre = forward(place, home_rank, token_sides, w_gate, w_up, row_count)
    got_hidden = crossed(hidden, "expert", pair)
    out_rows = dot_f32(hidden, w_down[0]).astype(jnp.bfloat16)
    out_back = sent_back(out_rows)
    gate_grad, up_grad = backward(
        place, home_rank, home_weight, cot_sides, w_down, *pre, row_count, [out_rows]
    )
    got_gate_grad = crossed(when(there(True, got_hidden), gate_grad), "expert", pair)
    got_up_grad = crossed(when(there(True, got_gate_grad), up_grad), "expert", pair)
    grad_rows = (
        dot_f32(gate_grad, w_gate[0], CONTRACT_LAST) + dot_f32(up_grad, w_up[0], CONTRACT_LAST)
    ).astype(jnp.bfloat16)
    grad_back = sent_back(grad_rows)
    held_grads = pick_cots(place, held_rank, held_weight, cot_sides, row_count, [grad_rows])
    held_rows = pick_tokens(place, held_rank, token_sides, row_count, [held_grads])

    out_spread = spread(out_back, True, there(True, grad_rows))
    grad_spread = spread(grad_back, False, True)
    out_in, grad_in = [layer_send(a, tok_rows, layers) for a in (out_spread, grad_spread)]
    mixed = layer_reduce(out_spread, out_in, tok_rows, layers, there(True, got_gate_grad))
    input_grad = layer_reduce(grad_spread, grad_in, tok_rows, layers, there(True, got_up_grad))

    def weight_grad(left, own, got, transposed, earlier):
        right = jnp.where(moved & there(True, *earlier), got, own)
        if transposed:
            left, right = right, left
        share = left.shape[1] // dp_count

        def product(part):
            columns = lax.dynamic_slice_in_dim(left, part * share, share, axis=1)
            return dot_f32(columns, right, CONTRACT_ROWS)

        sent = product((my_dp + 1) % dp_count).astype(jnp.bfloat16)
        got = crossed(sent, "dp", 1)
        return got, ((product(my_dp) + got.astype(jnp.float32)) * (1.0 / dp_count))[None]

    _, grad_down = weight_grad(held_grads, hidden, got_hidden, True, [])
    _, grad_gate = weight_grad(held_rows, gate_grad, got_gate_grad, False, [])
    _, grad_up = weight_grad(held_rows, up_grad, got_up_grad, False, [])
    return mixed, input_grad, grad_gate, grad_up, grad_down


def solution(mesh):
    tokens = P(("dp", "expert"), None)
    slots = P("expert", None, None)
    grads = P("expert", "dp", None)
    return jax.shard_map(
        body,
        mesh=mesh,
        in_specs=(tokens, tokens, tokens, tokens, P(), P(), slots, slots, slots),
        out_specs=(tokens, tokens, grads, grads, grads),
        check_vma=False,
    )
```

```python
import jax
import jax.numpy as jnp
from jax import lax
from jax.experimental import pallas as pl
from jax.experimental.pallas import tpu as pltpu
from jax.sharding import PartitionSpec as P

CONTRACT_ROWS = (((0,), (0,)), ((), ()))
CONTRACT_LAST = (((1,), (1,)), ((), ()))
PLANE = 4
FF_TILE = 256
VMEM_BYTES = 48 * 1024 * 1024


def dot_f32(a, b, dims=(((1,), (0,)), ((), ()))):
    return lax.dot_general(a, b, dims, preferred_element_type=jnp.float32)


def crossed(array, axis, flip):
    return lax.ppermute(array, axis, [(i, i ^ flip) for i in range(lax.axis_size(axis))])


def along(array, pairs):
    return lax.ppermute(array, "expert", pairs)


def line_pairs(owner_count):
    inner = [i for i in range(owner_count) if i // PLANE in (1, 2)]
    middle = [(i, i ^ 3 * PLANE) for i in inner]
    outward = [(i, i ^ PLANE) for i in inner]
    inward = [(i ^ PLANE, i) for i in inner]
    return middle, outward, inward


def there(flag, *arrays):
    for array in arrays:
        corner = array[tuple(slice(0, 1) for _ in array.shape)].reshape(())
        flag = flag & (corner == corner)
    return flag


def when(flag, array):
    return jnp.where(flag, array, jnp.zeros((), array.dtype))


def layer_gather(block, inner, layers):
    if layers != 4:
        got = [block] + [crossed(block, "expert", j * PLANE) for j in range(1, layers)]
        return jnp.concatenate(got[: layers // 2]), jnp.concatenate(got[layers // 2 :])
    middle, outward, _ = line_pairs(layers * PLANE)
    near = crossed(block, "expert", PLANE)
    far = [along(block, middle), along(near, middle)]
    relayed = [along(array, outward) for array in far]
    far_half = jnp.where(inner, jnp.concatenate(far), jnp.concatenate(relayed))
    return jnp.concatenate([block, near]), far_half


def plane_gather(half):
    mine = jnp.stack([half, crossed(half, "expert", 2)])
    return mine, crossed(mine, "expert", 1)


def layer_send(spread, tok_rows, layers):
    if layers != 4:
        blocks = [spread[j * tok_rows : (j + 1) * tok_rows] for j in range(1, layers)]
        return [crossed(block, "expert", j * PLANE) for j, block in enumerate(blocks, 1)]
    return [along(spread[tok_rows:], line_pairs(layers * PLANE)[2])]


def layer_reduce(spread, got, tok_rows, layers, flag):
    def total(parts):
        return sum(part.astype(jnp.float32) for part in parts).astype(jnp.bfloat16)

    if layers != 4:
        return total([spread[:tok_rows]] + got)
    middle, outward, _ = line_pairs(layers * PLANE)
    near_in, far_in = got[0][:tok_rows], got[0][tok_rows:]
    far_sum = total([spread[2 * tok_rows :], far_in])
    crossing = along(when(flag, far_sum), middle)
    near_sum = total([spread[tok_rows : 2 * tok_rows], crossing[tok_rows:]])
    near_out = along(near_sum, outward)
    return total([spread[:tok_rows], near_in, crossing[:tok_rows], near_out])


def rank_rows(hit, order):
    half = order.shape[0] // 2
    tok_rows = hit.shape[2]
    earlier = jnp.arange(tok_rows)[:, None] < jnp.arange(tok_rows)[None, :]
    within = jnp.einsum(
        "slt,tu->slu",
        hit.astype(jnp.bfloat16),
        earlier.astype(jnp.bfloat16),
        preferred_element_type=jnp.float32,
    ).astype(jnp.int32)
    count = jnp.sum(hit.astype(jnp.int32), axis=2)
    ahead = (order[:, None] < order[None, :]) & (order[:, None] // half == order[None, :] // half)
    before = jnp.sum(jnp.where(ahead[None], count[:, :, None], 0), axis=1)
    return jnp.where(hit, within + before[:, :, None], -1)


def pick_rows(rank, source, row_count):
    place = lax.broadcasted_iota(jnp.int32, (row_count, rank.shape[1]), 0)
    chosen = place == rank
    one_hot = jnp.where(chosen, 1.0, 0.0).astype(jnp.bfloat16)
    return chosen, dot_f32(one_hot, source)


def source_xor(step):
    return (step % PLANE) // 2 + 2 * (step % 2)


def run(kernel, grid, in_specs, out_specs, out_shape, scratch, flops, args, earlier=()):
    moved = sum(a.size * a.dtype.itemsize for a in args)
    count = len(in_specs) + 1
    in_specs = in_specs + [pl.BlockSpec(memory_space=pl.ANY)] * len(earlier)
    if earlier:
        inner_kernel = kernel

        def kernel(*refs):
            inner_kernel(*refs[:count], *refs[count + len(earlier) :])

    return pl.pallas_call(
        kernel,
        grid_spec=pltpu.PrefetchScalarGridSpec(
            num_scalar_prefetch=1,
            grid=(grid,),
            in_specs=in_specs,
            out_specs=out_specs,
            scratch_shapes=scratch,
        ),
        out_shape=out_shape,
        compiler_params=pltpu.CompilerParams(vmem_limit_bytes=VMEM_BYTES),
        cost_estimate=pl.CostEstimate(flops=flops, bytes_accessed=moved, transcendentals=0),
    )(*args, *earlier)


def row_block(side, source):
    return source * 2 + side


def token_specs(sides):
    _, tokens, width = sides[0][0].shape

    def line_at(i, p):
        i = jnp.minimum(i, 2 * PLANE - 1)
        return i // PLANE, source_xor(i), 0, 0

    def source(first):
        return pl.BlockSpec((1, tokens, width), lambda i, p: (jnp.clip(i - first, 0, 1), 0, 0))

    return [pl.BlockSpec((1, 1, 1, tokens), line_at)] + [source(2 * i) for i in range(PLANE)]


def each_source(step, rank_ref, source_refs, store, row_count):
    for i, source_ref in enumerate(source_refs):

        @pl.when(step // 2 == i)
        def _():
            store(pick_rows(rank_ref[0, 0], source_ref[0], row_count)[1].astype(jnp.bfloat16))


def pick_tokens(place, rank, sides, row_count, earlier):
    _, tokens, width = sides[0][0].shape

    def kernel(place_ref, rank_ref, *refs):
        def store(rows):
            refs[PLANE][...] = rows

        each_source(pl.program_id(0), rank_ref, refs[:PLANE], store, row_count)

    def out_at(i, p):
        return row_block((i // PLANE) ^ p[2], p[0] ^ source_xor(i)), 0

    return run(
        kernel,
        2 * PLANE,
        token_specs(sides),
        pl.BlockSpec((row_count, width), out_at),
        jax.ShapeDtypeStruct((2 * PLANE * row_count, width), jnp.bfloat16),
        [],
        4 * PLANE * row_count * tokens * width,
        [place, rank, *sides[0], *sides[1]],
        earlier,
    )


def scaled_each(step, rank_ref, weight_ref, source_refs, store, row_count):
    for i, source_ref in enumerate(source_refs):

        @pl.when(step // 2 == i)
        def _():
            chosen, rows = pick_rows(rank_ref[0, 0], source_ref[0], row_count)
            scale = jnp.sum(jnp.where(chosen, weight_ref[0, 0], 0.0), axis=1, keepdims=True)
            store((scale * rows).astype(jnp.bfloat16))


def pick_cots(place, rank, weight, sides, row_count, earlier):
    _, tokens, width = sides[0][0].shape

    def kernel(place_ref, rank_ref, weight_ref, *refs):
        def store(rows):
            refs[PLANE][...] = rows

        scaled_each(pl.program_id(0), rank_ref, weight_ref, refs[:PLANE], store, row_count)

    def out_at(i, p):
        return row_block((i // PLANE) ^ p[2], p[0] ^ source_xor(i)), 0

    specs = token_specs(sides)
    return run(
        kernel,
        2 * PLANE,
        specs[:1] + specs,
        pl.BlockSpec((row_count, width), out_at),
        jax.ShapeDtypeStruct((2 * PLANE * row_count, width), jnp.bfloat16),
        [],
        4 * PLANE * row_count * tokens * width,
        [place, rank, weight, *sides[0], *sides[1]],
        earlier,
    )


def tile_at(step):
    return jnp.maximum(step - 2 * PLANE, 0)


def store_rows(block, rows, rows_ref, row_count):
    rows_ref[pl.ds(pl.multiple_of(block * row_count, row_count), row_count), :] = rows


def forward(place, rank, sides, w_gate, w_up, row_count):
    _, tokens, width = sides[0][0].shape
    ff = w_gate.shape[2]
    rows = 2 * PLANE * row_count

    def kernel(place_ref, rank_ref, *refs):
        gate_ref, up_ref, hidden_ref, gate_pre_ref, up_pre_ref, rows_ref = refs[PLANE:]
        step = pl.program_id(0)

        @pl.when(step < 2 * PLANE)
        def _():
            def store(rows):
                block = row_block(step // PLANE, place_ref[0] ^ source_xor(step))
                store_rows(block, rows, rows_ref, row_count)

            each_source(step, rank_ref, refs[:PLANE], store, row_count)

        @pl.when(step >= 2 * PLANE)
        def _():
            gate_pre = dot_f32(rows_ref[...], gate_ref[0])
            up_pre = dot_f32(rows_ref[...], up_ref[0])
            gate_pre_ref[...] = gate_pre
            up_pre_ref[...] = up_pre
            hidden_ref[...] = (gate_pre * jax.nn.sigmoid(gate_pre) * up_pre).astype(jnp.bfloat16)

    weight_spec = pl.BlockSpec((1, width, FF_TILE), lambda i, p: (0, 0, tile_at(i)))
    out_spec = pl.BlockSpec((rows, FF_TILE), lambda i, p: (0, tile_at(i)))
    return run(
        kernel,
        2 * PLANE + ff // FF_TILE,
        token_specs(sides) + [weight_spec] * 2,
        [out_spec] * 3,
        [jax.ShapeDtypeStruct((rows, ff), t) for t in (jnp.bfloat16, jnp.float32, jnp.float32)],
        [pltpu.VMEM((rows, width), jnp.bfloat16)],
        4 * rows * width * ff,
        [place, rank, *sides[0], *sides[1], w_gate, w_up],
    )


def backward(place, rank, weight, sides, w_down, gate_pre, up_pre, row_count, earlier):
    _, tokens, width = sides[0][0].shape
    ff = w_down.shape[1]
    rows = 2 * PLANE * row_count

    def kernel(place_ref, rank_ref, weight_ref, *refs):
        down_ref, gate_pre_ref, up_pre_ref, gate_grad_ref, up_grad_ref, rows_ref = refs[PLANE:]
        step = pl.program_id(0)

        @pl.when(step < 2 * PLANE)
        def _():
            def store(rows):
                block = row_block(step // PLANE, place_ref[0] ^ source_xor(step))
                store_rows(block, rows, rows_ref, row_count)

            scaled_each(step, rank_ref, weight_ref, refs[:PLANE], store, row_count)

        @pl.when(step >= 2 * PLANE)
        def _():
            hidden_grad = dot_f32(rows_ref[...], down_ref[0], CONTRACT_LAST)
            gate_pre = gate_pre_ref[...]
            sigma = jax.nn.sigmoid(gate_pre)
            slope = sigma * (1.0 + gate_pre * (1.0 - sigma))
            gate_grad_ref[...] = (hidden_grad * up_pre_ref[...] * slope).astype(jnp.bfloat16)
            up_grad_ref[...] = (hidden_grad * gate_pre * sigma).astype(jnp.bfloat16)

    specs = token_specs(sides)
    down_spec = pl.BlockSpec((1, FF_TILE, width), lambda i, p: (0, tile_at(i), 0))
    tile_spec = pl.BlockSpec((rows, FF_TILE), lambda i, p: (0, tile_at(i)))
    return run(
        kernel,
        2 * PLANE + ff // FF_TILE,
        specs[:1] + specs + [down_spec] + [tile_spec] * 2,
        [tile_spec] * 2,
        [jax.ShapeDtypeStruct((rows, ff), jnp.bfloat16)] * 2,
        [pltpu.VMEM((rows, width), jnp.bfloat16)],
        2 * rows * width * ff,
        [place, rank, weight, *sides[0], *sides[1], w_down, gate_pre, up_pre],
        earlier,
    )


def body(tokens, cotangent, expert_ids, combine, placement, moves, w_gate, w_up, w_down):
    owner_count = lax.axis_size("expert")
    dp_count = lax.axis_size("dp")
    my_index = lax.axis_index("expert")
    my_dp = lax.axis_index("dp")
    tok_rows, width = tokens.shape
    choose_count = expert_ids.shape[1]
    layers = owner_count // PLANE
    half = layers // 2
    row_count = 3 * tok_rows * choose_count // (4 * PLANE)
    pair = owner_count // 2
    own_layer, my_place = my_index // PLANE, my_index % PLANE
    inner = (own_layer == 1) | (own_layer == 2)
    layer_ids = jnp.arange(layers, dtype=jnp.int32)
    order = own_layer ^ layer_ids
    if layers == 4:
        order = jnp.where(inner, jnp.stack([order[j] for j in (0, 1, 3, 2)]), order)
    routing = jnp.concatenate([expert_ids.astype(jnp.float32), combine], axis=1)
    lines = [routing] + [crossed(routing, "expert", j * PLANE) for j in range(1, layers)]
    if layers == 4:
        lines = lines[:2] + [jnp.where(inner, a, b) for a, b in (lines[:1:-1], lines[2:])]
    routing = jnp.stack(lines).transpose(2, 0, 1)
    routings = [routing] + [crossed(routing, "expert", k) for k in range(1, PLANE)]
    routing = jnp.stack(routings)
    routed = there(inner, *routings)
    near_tokens, far_tokens = layer_gather(tokens, routed, layers)
    near_cots, far_cots = layer_gather(cotangent, inner, layers)
    near_cots = when(there(True, far_tokens), near_cots)
    token_sides = [plane_gather(near_tokens), plane_gather(far_tokens)]
    cot_sides = [plane_gather(near_cots), plane_gather(far_cots)]
    ids, weights = routing[:, :choose_count], routing[:, choose_count:]

    slot_ids = jnp.arange(owner_count, dtype=jnp.int32)
    held = jnp.where(moves == 1, jnp.roll(placement, pair), placement)
    mine = slot_ids == my_index
    home_expert = jnp.sum(jnp.where(mine, placement, 0))
    held_expert = jnp.sum(jnp.where(mine, held, 0))
    my_move = jnp.sum(jnp.where(mine, moves, 0))
    moved = my_move == 1
    place = jnp.stack([my_place, own_layer // half, my_move]).astype(jnp.int32)
    plane_slots = own_layer * PLANE + jnp.arange(PLANE, dtype=jnp.int32)
    near = slot_ids[None, :] == plane_slots[:, None]
    plane_experts = jnp.sum(jnp.where(near, placement[None], 0), axis=1)

    def named(expert, source_ids, source_weights):
        match = source_ids == expert.astype(jnp.float32)
        return jnp.any(match, axis=1), jnp.sum(jnp.where(match, source_weights, 0.0), axis=1)

    sets = [
        named(home_expert, ids, weights),
        named(held_expert, ids, weights),
        named(plane_experts[:, None, None, None], ids[:1], weights[:1]),
    ]
    rank = rank_rows(jnp.concatenate([s[0] for s in sets]), order)
    weight = jnp.concatenate([jnp.broadcast_to(s[1], (PLANE,) + s[1].shape[1:]) for s in sets])

    def halves(array):
        array = array.reshape(len(sets), PLANE, 2, 1, half * tok_rows)
        return array.transpose(0, 2, 1, 3, 4)

    home_rank, held_rank, back_rank = halves(rank)
    home_weight, held_weight, back_weight = halves(weight)

    groups = [[i * PLANE + j for j in range(PLANE)] for i in range(layers)]

    def sent_back(rows):
        rows = rows.reshape(PLANE, 2 * row_count, width)
        return lax.all_to_all(
            rows, "expert", split_axis=0, concat_axis=0, axis_index_groups=groups, tiled=True
        )

    def spread(back, weighted, flag):
        numbers = jnp.arange(row_count, dtype=jnp.int32)[None, None, :, None]
        chosen = (back_rank.transpose(1, 0, 2, 3) == numbers) & flag
        rows = back.reshape(PLANE, 2, row_count, width)
        if weighted:
            weights = back_weight.transpose(1, 0, 2, 3)
            scale = jnp.sum(jnp.where(chosen, weights, 0.0), axis=3, keepdims=True)
            rows = (scale * rows.astype(jnp.float32)).astype(jnp.bfloat16)
        same = jnp.eye(2, dtype=bool)[None, :, None, :, None]
        one_hot = (chosen[:, :, :, None, :] & same).astype(jnp.bfloat16)
        one_hot = one_hot.reshape(2 * PLANE * row_count, layers * tok_rows)
        rows = rows.reshape(2 * PLANE * row_count, width)
        return dot_f32(one_hot, rows, CONTRACT_ROWS).astype(jnp.bfloat16)

    hidden, *pre = forward(place, home_rank, token_sides, w_gate, w_up, row_count)
    got_hidden = crossed(hidden, "expert", pair)
    out_rows = dot_f32(hidden, w_down[0]).astype(jnp.bfloat16)
    out_back = sent_back(out_rows)
    earlier = [out_rows, got_hidden]
    gate_grad, up_grad = backward(
        place, home_rank, home_weight, cot_sides, w_down, *pre, row_count, earlier
    )
    got_gate_grad = crossed(gate_grad, "expert", pair)
    got_up_grad = crossed(when(there(True, got_gate_grad), up_grad), "expert", pair)
    grad_rows = dot_f32(gate_grad, w_gate[0], CONTRACT_LAST)
    grad_rows = grad_rows + dot_f32(up_grad, w_up[0], CONTRACT_LAST)
    grad_rows = grad_rows.astype(jnp.bfloat16)
    grad_back = sent_back(grad_rows)
    held_grads = pick_cots(place, held_rank, held_weight, cot_sides, row_count, [out_rows])
    held_rows = pick_tokens(place, held_rank, token_sides, row_count, [held_grads])

    out_spread = spread(out_back, True, there(True, grad_rows))
    grad_spread = spread(grad_back, False, True)
    out_in, grad_in = [layer_send(a, tok_rows, layers) for a in (out_spread, grad_spread)]
    mixed = layer_reduce(out_spread, out_in, tok_rows, layers, there(True, got_gate_grad))
    input_grad = layer_reduce(grad_spread, grad_in, tok_rows, layers, there(True, got_up_grad))

    def weight_grad(left, own, got, transposed, earlier):
        right = jnp.where(moved & there(True, *earlier), got, own)
        if transposed:
            left, right = right, left
        share = left.shape[1] // dp_count

        def product(part):
            columns = lax.dynamic_slice_in_dim(left, part * share, share, axis=1)
            return dot_f32(columns, right, CONTRACT_ROWS)

        sent = product((my_dp + 1) % dp_count).astype(jnp.bfloat16)
        got = crossed(sent, "dp", 1)
        return got, ((product(my_dp) + got.astype(jnp.float32)) * (1.0 / dp_count))[None]

    _, grad_down = weight_grad(held_grads, hidden, got_hidden, True, [])
    _, grad_gate = weight_grad(held_rows, gate_grad, got_gate_grad, False, [])
    _, grad_up = weight_grad(held_rows, up_grad, got_up_grad, False, [])
    return mixed, input_grad, grad_gate, grad_up, grad_down


def solution(mesh):
    tokens = P(("dp", "expert"), None)
    slots = P("expert", None, None)
    grads = P("expert", "dp", None)
    return jax.shard_map(
        body,
        mesh=mesh,
        in_specs=(tokens, tokens, tokens, tokens, P(), P(), slots, slots, slots),
        out_specs=(tokens, tokens, grads, grads, grads),
        check_vma=False,
    )
```

```python
import jax
import jax.numpy as jnp
from jax import lax
from jax.experimental import pallas as pl
from jax.experimental.pallas import tpu as pltpu
from jax.sharding import PartitionSpec as P

CONTRACT_ROWS = (((0,), (0,)), ((), ()))
CONTRACT_LAST = (((1,), (1,)), ((), ()))
PLANE = 4
FF_TILE = 256
VMEM_BYTES = 48 * 1024 * 1024


def dot_f32(a, b, dims=(((1,), (0,)), ((), ()))):
    return lax.dot_general(a, b, dims, preferred_element_type=jnp.float32)


def crossed(array, axis, flip):
    return lax.ppermute(array, axis, [(i, i ^ flip) for i in range(lax.axis_size(axis))])


def along(array, pairs):
    return lax.ppermute(array, "expert", pairs)


def line_pairs(owner_count):
    inner = [i for i in range(owner_count) if i // PLANE in (1, 2)]
    middle = [(i, i ^ 3 * PLANE) for i in inner]
    outward = [(i, i ^ PLANE) for i in inner]
    inward = [(i ^ PLANE, i) for i in inner]
    return middle, outward, inward


def there(flag, *arrays):
    for array in arrays:
        corner = array[tuple(slice(0, 1) for _ in array.shape)].reshape(())
        flag = flag & (corner == corner)
    return flag


def when(flag, array):
    return jnp.where(flag, array, jnp.zeros((), array.dtype))


def layer_gather(block, inner, layers):
    if layers != 4:
        got = [block] + [crossed(block, "expert", j * PLANE) for j in range(1, layers)]
        return jnp.concatenate(got[: layers // 2]), jnp.concatenate(got[layers // 2 :])
    middle, outward, _ = line_pairs(layers * PLANE)
    near = crossed(block, "expert", PLANE)
    far = [along(block, middle), along(near, middle)]
    relayed = [along(array, outward) for array in far]
    far_half = jnp.where(inner, jnp.concatenate(far), jnp.concatenate(relayed))
    return jnp.concatenate([block, near]), far_half


def plane_gather(half, earlier=()):
    mine = when(there(True, *earlier), jnp.stack([half, crossed(half, "expert", 2)]))
    return mine, crossed(mine, "expert", 1)


def layer_send(spread, tok_rows, layers):
    if layers != 4:
        blocks = [spread[j * tok_rows : (j + 1) * tok_rows] for j in range(1, layers)]
        return [crossed(block, "expert", j * PLANE) for j, block in enumerate(blocks, 1)]
    return [along(spread[tok_rows:], line_pairs(layers * PLANE)[2])]


def layer_reduce(spread, got, tok_rows, layers, flag):
    def total(parts):
        return sum(part.astype(jnp.float32) for part in parts).astype(jnp.bfloat16)

    if layers != 4:
        return total([spread[:tok_rows]] + got)
    middle, outward, _ = line_pairs(layers * PLANE)
    near_in, far_in = got[0][:tok_rows], got[0][tok_rows:]
    far_sum = total([spread[2 * tok_rows :], far_in])
    crossing = along(when(flag, far_sum), middle)
    near_sum = total([spread[tok_rows : 2 * tok_rows], crossing[tok_rows:]])
    near_out = along(near_sum, outward)
    return total([spread[:tok_rows], near_in, crossing[:tok_rows], near_out])


def rank_rows(hit, order):
    half = order.shape[0] // 2
    tok_rows = hit.shape[2]
    earlier = jnp.arange(tok_rows)[:, None] < jnp.arange(tok_rows)[None, :]
    within = jnp.einsum(
        "slt,tu->slu",
        hit.astype(jnp.bfloat16),
        earlier.astype(jnp.bfloat16),
        preferred_element_type=jnp.float32,
    ).astype(jnp.int32)
    count = jnp.sum(hit.astype(jnp.int32), axis=2)
    ahead = (order[:, None] < order[None, :]) & (order[:, None] // half == order[None, :] // half)
    before = jnp.sum(jnp.where(ahead[None], count[:, :, None], 0), axis=1)
    return jnp.where(hit, within + before[:, :, None], -1)


def pick_rows(rank, source, row_count):
    place = lax.broadcasted_iota(jnp.int32, (row_count, rank.shape[1]), 0)
    chosen = place == rank
    one_hot = jnp.where(chosen, 1.0, 0.0).astype(jnp.bfloat16)
    return chosen, dot_f32(one_hot, source)


def source_xor(step):
    return (step % PLANE) // 2 + 2 * (step % 2)


def run(kernel, grid, in_specs, out_specs, out_shape, scratch, flops, args, earlier=()):
    moved = sum(a.size * a.dtype.itemsize for a in args)
    count = len(in_specs) + 1
    in_specs = in_specs + [pl.BlockSpec(memory_space=pl.ANY)] * len(earlier)
    if earlier:
        inner_kernel = kernel

        def kernel(*refs):
            inner_kernel(*refs[:count], *refs[count + len(earlier) :])

    return pl.pallas_call(
        kernel,
        grid_spec=pltpu.PrefetchScalarGridSpec(
            num_scalar_prefetch=1,
            grid=(grid,),
            in_specs=in_specs,
            out_specs=out_specs,
            scratch_shapes=scratch,
        ),
        out_shape=out_shape,
        compiler_params=pltpu.CompilerParams(vmem_limit_bytes=VMEM_BYTES),
        cost_estimate=pl.CostEstimate(flops=flops, bytes_accessed=moved, transcendentals=0),
    )(*args, *earlier)


def row_block(side, source):
    return source * 2 + side


def token_specs(sides):
    _, tokens, width = sides[0][0].shape

    def line_at(i, p):
        i = jnp.minimum(i, 2 * PLANE - 1)
        return i // PLANE, source_xor(i), 0, 0

    def source(first):
        return pl.BlockSpec((1, tokens, width), lambda i, p: (jnp.clip(i - first, 0, 1), 0, 0))

    return [pl.BlockSpec((1, 1, 1, tokens), line_at)] + [source(2 * i) for i in range(PLANE)]


def each_source(step, rank_ref, source_refs, store, row_count):
    for i, source_ref in enumerate(source_refs):

        @pl.when(step // 2 == i)
        def _():
            store(pick_rows(rank_ref[0, 0], source_ref[0], row_count)[1].astype(jnp.bfloat16))


def pick_tokens(place, rank, sides, row_count, earlier):
    _, tokens, width = sides[0][0].shape

    def kernel(place_ref, rank_ref, *refs):
        def store(rows):
            refs[PLANE][...] = rows

        each_source(pl.program_id(0), rank_ref, refs[:PLANE], store, row_count)

    def out_at(i, p):
        return row_block((i // PLANE) ^ p[2], p[0] ^ source_xor(i)), 0

    return run(
        kernel,
        2 * PLANE,
        token_specs(sides),
        pl.BlockSpec((row_count, width), out_at),
        jax.ShapeDtypeStruct((2 * PLANE * row_count, width), jnp.bfloat16),
        [],
        4 * PLANE * row_count * tokens * width,
        [place, rank, *sides[0], *sides[1]],
        earlier,
    )


def scaled_each(step, rank_ref, weight_ref, source_refs, store, row_count):
    for i, source_ref in enumerate(source_refs):

        @pl.when(step // 2 == i)
        def _():
            chosen, rows = pick_rows(rank_ref[0, 0], source_ref[0], row_count)
            scale = jnp.sum(jnp.where(chosen, weight_ref[0, 0], 0.0), axis=1, keepdims=True)
            store((scale * rows).astype(jnp.bfloat16))


def pick_cots(place, rank, weight, sides, row_count, earlier):
    _, tokens, width = sides[0][0].shape

    def kernel(place_ref, rank_ref, weight_ref, *refs):
        def store(rows):
            refs[PLANE][...] = rows

        scaled_each(pl.program_id(0), rank_ref, weight_ref, refs[:PLANE], store, row_count)

    def out_at(i, p):
        return row_block((i // PLANE) ^ p[2], p[0] ^ source_xor(i)), 0

    specs = token_specs(sides)
    return run(
        kernel,
        2 * PLANE,
        specs[:1] + specs,
        pl.BlockSpec((row_count, width), out_at),
        jax.ShapeDtypeStruct((2 * PLANE * row_count, width), jnp.bfloat16),
        [],
        4 * PLANE * row_count * tokens * width,
        [place, rank, weight, *sides[0], *sides[1]],
        earlier,
    )


def tile_at(step):
    return jnp.maximum(step - 2 * PLANE, 0)


def store_rows(block, rows, rows_ref, row_count):
    rows_ref[pl.ds(pl.multiple_of(block * row_count, row_count), row_count), :] = rows


def forward(place, rank, sides, w_gate, w_up, row_count):
    _, tokens, width = sides[0][0].shape
    ff = w_gate.shape[2]
    rows = 2 * PLANE * row_count

    def kernel(place_ref, rank_ref, *refs):
        gate_ref, up_ref, hidden_ref, gate_pre_ref, up_pre_ref, rows_ref = refs[PLANE:]
        step = pl.program_id(0)

        @pl.when(step < 2 * PLANE)
        def _():
            def store(rows):
                block = row_block(step // PLANE, place_ref[0] ^ source_xor(step))
                store_rows(block, rows, rows_ref, row_count)

            each_source(step, rank_ref, refs[:PLANE], store, row_count)

        @pl.when(step >= 2 * PLANE)
        def _():
            gate_pre = dot_f32(rows_ref[...], gate_ref[0])
            up_pre = dot_f32(rows_ref[...], up_ref[0])
            gate_pre_ref[...] = gate_pre
            up_pre_ref[...] = up_pre
            hidden_ref[...] = (gate_pre * jax.nn.sigmoid(gate_pre) * up_pre).astype(jnp.bfloat16)

    weight_spec = pl.BlockSpec((1, width, FF_TILE), lambda i, p: (0, 0, tile_at(i)))
    out_spec = pl.BlockSpec((rows, FF_TILE), lambda i, p: (0, tile_at(i)))
    return run(
        kernel,
        2 * PLANE + ff // FF_TILE,
        token_specs(sides) + [weight_spec] * 2,
        [out_spec] * 3,
        [jax.ShapeDtypeStruct((rows, ff), t) for t in (jnp.bfloat16, jnp.float32, jnp.float32)],
        [pltpu.VMEM((rows, width), jnp.bfloat16)],
        4 * rows * width * ff,
        [place, rank, *sides[0], *sides[1], w_gate, w_up],
    )


def backward(place, rank, weight, sides, w_down, gate_pre, up_pre, row_count, earlier):
    _, tokens, width = sides[0][0].shape
    ff = w_down.shape[1]
    rows = 2 * PLANE * row_count

    def kernel(place_ref, rank_ref, weight_ref, *refs):
        down_ref, gate_pre_ref, up_pre_ref, gate_grad_ref, up_grad_ref, rows_ref = refs[PLANE:]
        step = pl.program_id(0)

        @pl.when(step < 2 * PLANE)
        def _():
            def store(rows):
                block = row_block(step // PLANE, place_ref[0] ^ source_xor(step))
                store_rows(block, rows, rows_ref, row_count)

            scaled_each(step, rank_ref, weight_ref, refs[:PLANE], store, row_count)

        @pl.when(step >= 2 * PLANE)
        def _():
            hidden_grad = dot_f32(rows_ref[...], down_ref[0], CONTRACT_LAST)
            gate_pre = gate_pre_ref[...]
            sigma = jax.nn.sigmoid(gate_pre)
            slope = sigma * (1.0 + gate_pre * (1.0 - sigma))
            gate_grad_ref[...] = (hidden_grad * up_pre_ref[...] * slope).astype(jnp.bfloat16)
            up_grad_ref[...] = (hidden_grad * gate_pre * sigma).astype(jnp.bfloat16)

    specs = token_specs(sides)
    down_spec = pl.BlockSpec((1, FF_TILE, width), lambda i, p: (0, tile_at(i), 0))
    tile_spec = pl.BlockSpec((rows, FF_TILE), lambda i, p: (0, tile_at(i)))
    return run(
        kernel,
        2 * PLANE + ff // FF_TILE,
        specs[:1] + specs + [down_spec] + [tile_spec] * 2,
        [tile_spec] * 2,
        [jax.ShapeDtypeStruct((rows, ff), jnp.bfloat16)] * 2,
        [pltpu.VMEM((rows, width), jnp.bfloat16)],
        2 * rows * width * ff,
        [place, rank, weight, *sides[0], *sides[1], w_down, gate_pre, up_pre],
        earlier,
    )


def body(tokens, cotangent, expert_ids, combine, placement, moves, w_gate, w_up, w_down):
    owner_count = lax.axis_size("expert")
    dp_count = lax.axis_size("dp")
    my_index = lax.axis_index("expert")
    my_dp = lax.axis_index("dp")
    tok_rows, width = tokens.shape
    choose_count = expert_ids.shape[1]
    layers = owner_count // PLANE
    half = layers // 2
    row_count = 3 * tok_rows * choose_count // (4 * PLANE)
    pair = owner_count // 2
    own_layer, my_place = my_index // PLANE, my_index % PLANE
    inner = (own_layer == 1) | (own_layer == 2)
    layer_ids = jnp.arange(layers, dtype=jnp.int32)
    order = own_layer ^ layer_ids
    if layers == 4:
        order = jnp.where(inner, jnp.stack([order[j] for j in (0, 1, 3, 2)]), order)
    routing = jnp.concatenate([expert_ids.astype(jnp.float32), combine], axis=1)
    lines = [routing] + [crossed(routing, "expert", j * PLANE) for j in range(1, layers)]
    if layers == 4:
        lines = lines[:2] + [jnp.where(inner, a, b) for a, b in (lines[:1:-1], lines[2:])]
    routing = jnp.stack(lines).transpose(2, 0, 1)
    routings = [routing] + [crossed(routing, "expert", k) for k in range(1, PLANE)]
    routing = jnp.stack(routings)
    routed = there(inner, *routings)
    near_tokens, far_tokens = layer_gather(tokens, routed, layers)
    near_cots, far_cots = layer_gather(cotangent, inner, layers)
    near_cots = when(there(True, far_tokens), near_cots)
    token_sides = [plane_gather(near_tokens), plane_gather(far_tokens)]
    ids, weights = routing[:, :choose_count], routing[:, choose_count:]

    slot_ids = jnp.arange(owner_count, dtype=jnp.int32)
    held = jnp.where(moves == 1, jnp.roll(placement, pair), placement)
    mine = slot_ids == my_index
    home_expert = jnp.sum(jnp.where(mine, placement, 0))
    held_expert = jnp.sum(jnp.where(mine, held, 0))
    my_move = jnp.sum(jnp.where(mine, moves, 0))
    moved = my_move == 1
    place = jnp.stack([my_place, own_layer // half, my_move]).astype(jnp.int32)
    plane_slots = own_layer * PLANE + jnp.arange(PLANE, dtype=jnp.int32)
    near = slot_ids[None, :] == plane_slots[:, None]
    plane_experts = jnp.sum(jnp.where(near, placement[None], 0), axis=1)

    def named(expert, source_ids, source_weights):
        match = source_ids == expert.astype(jnp.float32)
        return jnp.any(match, axis=1), jnp.sum(jnp.where(match, source_weights, 0.0), axis=1)

    sets = [
        named(home_expert, ids, weights),
        named(held_expert, ids, weights),
        named(plane_experts[:, None, None, None], ids[:1], weights[:1]),
    ]
    rank = rank_rows(jnp.concatenate([s[0] for s in sets]), order)
    weight = jnp.concatenate([jnp.broadcast_to(s[1], (PLANE,) + s[1].shape[1:]) for s in sets])

    def halves(array):
        array = array.reshape(len(sets), PLANE, 2, 1, half * tok_rows)
        return array.transpose(0, 2, 1, 3, 4)

    home_rank, held_rank, back_rank = halves(rank)
    home_weight, held_weight, back_weight = halves(weight)

    groups = [[i * PLANE + j for j in range(PLANE)] for i in range(layers)]

    def sent_back(rows):
        rows = rows.reshape(PLANE, 2 * row_count, width)
        return lax.all_to_all(
            rows, "expert", split_axis=0, concat_axis=0, axis_index_groups=groups, tiled=True
        )

    def spread(back, weighted, flag):
        numbers = jnp.arange(row_count, dtype=jnp.int32)[None, None, :, None]
        chosen = (back_rank.transpose(1, 0, 2, 3) == numbers) & flag
        rows = back.reshape(PLANE, 2, row_count, width)
        if weighted:
            weights = back_weight.transpose(1, 0, 2, 3)
            scale = jnp.sum(jnp.where(chosen, weights, 0.0), axis=3, keepdims=True)
            rows = (scale * rows.astype(jnp.float32)).astype(jnp.bfloat16)
        same = jnp.eye(2, dtype=bool)[None, :, None, :, None]
        one_hot = (chosen[:, :, :, None, :] & same).astype(jnp.bfloat16)
        one_hot = one_hot.reshape(2 * PLANE * row_count, layers * tok_rows)
        rows = rows.reshape(2 * PLANE * row_count, width)
        return dot_f32(one_hot, rows, CONTRACT_ROWS).astype(jnp.bfloat16)

    hidden, *pre = forward(place, home_rank, token_sides, w_gate, w_up, row_count)
    got_hidden = crossed(hidden, "expert", pair)
    cot_sides = [plane_gather(side, [hidden]) for side in (near_cots, far_cots)]
    out_rows = dot_f32(hidden, w_down[0]).astype(jnp.bfloat16)
    out_back = sent_back(out_rows)
    earlier = [out_rows, got_hidden]
    gate_grad, up_grad = backward(
        place, home_rank, home_weight, cot_sides, w_down, *pre, row_count, earlier
    )
    got_gate_grad = crossed(gate_grad, "expert", pair)
    held_cots = pick_cots(place, held_rank, held_weight, cot_sides, row_count, [out_rows])
    held_rows = pick_tokens(place, held_rank, token_sides, row_count, [held_cots])

    def product(left, right, part):
        share = left.shape[1] // dp_count
        columns = lax.dynamic_slice_in_dim(left, part * share, share, axis=1)
        return dot_f32(columns, right, CONTRACT_ROWS)

    def dp_share(left, right):
        return product(left, right, (my_dp + 1) % dp_count).astype(jnp.bfloat16)

    def dp_sum(left, right, got):
        return ((product(left, right, my_dp) + got.astype(jnp.float32)) * (1.0 / dp_count))[None]

    held_hidden = jnp.where(moved, got_hidden, hidden)
    sent_down = dp_share(held_hidden, held_cots)
    got_down = crossed(sent_down, "dp", 1)
    out_spread = spread(out_back, True, there(True, gate_grad))
    out_in = layer_send(out_spread, tok_rows, layers)

    grad_rows = dot_f32(gate_grad, w_gate[0], CONTRACT_LAST)
    grad_rows = grad_rows + dot_f32(up_grad, w_up[0], CONTRACT_LAST)
    grad_rows = when(there(True, sent_down, out_spread), grad_rows).astype(jnp.bfloat16)
    grad_spread = spread(sent_back(grad_rows), False, True)
    grad_in = layer_send(grad_spread, tok_rows, layers)
    sent_up_grad = when(there(True, got_gate_grad, got_down), up_grad)
    got_up_grad = crossed(sent_up_grad, "expert", pair)
    mixed = layer_reduce(out_spread, out_in, tok_rows, layers, there(True, got_gate_grad))
    input_grad = layer_reduce(grad_spread, grad_in, tok_rows, layers, there(True, got_up_grad))

    grad_down = dp_sum(held_hidden, held_cots, got_down)
    held_gate = jnp.where(moved, got_gate_grad, gate_grad)
    held_up = jnp.where(moved, got_up_grad, up_grad)
    grad_gate, grad_up = [
        dp_sum(held_rows, held, crossed(dp_share(held_rows, held), "dp", 1))
        for held in (held_gate, held_up)
    ]
    return mixed, input_grad, grad_gate, grad_up, grad_down


def solution(mesh):
    tokens = P(("dp", "expert"), None)
    slots = P("expert", None, None)
    grads = P("expert", "dp", None)
    return jax.shard_map(
        body,
        mesh=mesh,
        in_specs=(tokens, tokens, tokens, tokens, P(), P(), slots, slots, slots),
        out_specs=(tokens, tokens, grads, grads, grads),
        check_vma=False,
    )
```

```python
import jax
import jax.numpy as jnp
from jax import lax
from jax.experimental import pallas as pl
from jax.experimental.pallas import tpu as pltpu
from jax.sharding import PartitionSpec as P

CONTRACT_ROWS = (((0,), (0,)), ((), ()))
CONTRACT_LAST = (((1,), (1,)), ((), ()))
PLANE = 4
FF_TILE = 256
VMEM_BYTES = 48 * 1024 * 1024


def dot_f32(a, b, dims=(((1,), (0,)), ((), ()))):
    return lax.dot_general(a, b, dims, preferred_element_type=jnp.float32)


def crossed(array, axis, flip):
    return lax.ppermute(array, axis, [(i, i ^ flip) for i in range(lax.axis_size(axis))])


def along(array, pairs):
    return lax.ppermute(array, "expert", pairs)


def line_pairs(owner_count):
    inner = [i for i in range(owner_count) if i // PLANE in (1, 2)]
    middle = [(i, i ^ 3 * PLANE) for i in inner]
    outward = [(i, i ^ PLANE) for i in inner]
    inward = [(i ^ PLANE, i) for i in inner]
    return middle, outward, inward


def there(flag, *arrays):
    for array in arrays:
        corner = array[tuple(slice(0, 1) for _ in array.shape)].reshape(())
        flag = flag & (corner == corner)
    return flag


def when(flag, array):
    return jnp.where(flag, array, jnp.zeros((), array.dtype))


def layer_gather(block, inner, layers):
    if layers != 4:
        got = [block] + [crossed(block, "expert", j * PLANE) for j in range(1, layers)]
        return jnp.concatenate(got[: layers // 2]), jnp.concatenate(got[layers // 2 :])
    middle, outward, _ = line_pairs(layers * PLANE)
    near = crossed(block, "expert", PLANE)
    far = [along(block, middle), along(near, middle)]
    relayed = [along(array, outward) for array in far]
    far_half = jnp.where(inner, jnp.concatenate(far), jnp.concatenate(relayed))
    return jnp.concatenate([block, near]), far_half


def plane_gather(half):
    mine = jnp.stack([half, crossed(half, "expert", 2)])
    return mine, crossed(mine, "expert", 1)


def layer_send(spread, tok_rows, layers):
    if layers != 4:
        blocks = [spread[j * tok_rows : (j + 1) * tok_rows] for j in range(1, layers)]
        return [crossed(block, "expert", j * PLANE) for j, block in enumerate(blocks, 1)]
    return [along(spread[tok_rows:], line_pairs(layers * PLANE)[2])]


def layer_reduce(spread, got, tok_rows, layers, flag):
    def total(parts):
        return sum(part.astype(jnp.float32) for part in parts).astype(jnp.bfloat16)

    if layers != 4:
        return total([spread[:tok_rows]] + got)
    middle, outward, _ = line_pairs(layers * PLANE)
    near_in, far_in = got[0][:tok_rows], got[0][tok_rows:]
    far_sum = total([spread[2 * tok_rows :], far_in])
    crossing = along(when(flag, far_sum), middle)
    near_sum = total([spread[tok_rows : 2 * tok_rows], crossing[tok_rows:]])
    near_out = along(near_sum, outward)
    return total([spread[:tok_rows], near_in, crossing[:tok_rows], near_out])


def rank_rows(hit, order):
    half = order.shape[0] // 2
    tok_rows = hit.shape[2]
    earlier = jnp.arange(tok_rows)[:, None] < jnp.arange(tok_rows)[None, :]
    within = jnp.einsum(
        "slt,tu->slu",
        hit.astype(jnp.bfloat16),
        earlier.astype(jnp.bfloat16),
        preferred_element_type=jnp.float32,
    ).astype(jnp.int32)
    count = jnp.sum(hit.astype(jnp.int32), axis=2)
    ahead = (order[:, None] < order[None, :]) & (order[:, None] // half == order[None, :] // half)
    before = jnp.sum(jnp.where(ahead[None], count[:, :, None], 0), axis=1)
    return jnp.where(hit, within + before[:, :, None], -1)


def pick_rows(rank, source, row_count):
    place = lax.broadcasted_iota(jnp.int32, (row_count, rank.shape[1]), 0)
    chosen = place == rank
    one_hot = jnp.where(chosen, 1.0, 0.0).astype(jnp.bfloat16)
    return chosen, dot_f32(one_hot, source)


def source_xor(step):
    return (step % PLANE) // 2 + 2 * (step % 2)


def run(kernel, grid, in_specs, out_specs, out_shape, scratch, flops, args, earlier=()):
    moved = sum(a.size * a.dtype.itemsize for a in args)
    count = len(in_specs) + 1
    in_specs = in_specs + [pl.BlockSpec(memory_space=pl.ANY)] * len(earlier)
    if earlier:
        inner_kernel = kernel

        def kernel(*refs):
            inner_kernel(*refs[:count], *refs[count + len(earlier) :])

    return pl.pallas_call(
        kernel,
        grid_spec=pltpu.PrefetchScalarGridSpec(
            num_scalar_prefetch=1,
            grid=(grid,),
            in_specs=in_specs,
            out_specs=out_specs,
            scratch_shapes=scratch,
        ),
        out_shape=out_shape,
        compiler_params=pltpu.CompilerParams(vmem_limit_bytes=VMEM_BYTES),
        cost_estimate=pl.CostEstimate(flops=flops, bytes_accessed=moved, transcendentals=0),
    )(*args, *earlier)


def row_block(side, source):
    return source * 2 + side


def token_specs(sides):
    _, tokens, width = sides[0][0].shape

    def line_at(i, p):
        i = jnp.minimum(i, 2 * PLANE - 1)
        return i // PLANE, source_xor(i), 0, 0

    def source(first):
        return pl.BlockSpec((1, tokens, width), lambda i, p: (jnp.clip(i - first, 0, 1), 0, 0))

    return [pl.BlockSpec((1, 1, 1, tokens), line_at)] + [source(2 * i) for i in range(PLANE)]


def each_source(step, rank_ref, source_refs, store, row_count):
    for i, source_ref in enumerate(source_refs):

        @pl.when(step // 2 == i)
        def _():
            store(pick_rows(rank_ref[0, 0], source_ref[0], row_count)[1].astype(jnp.bfloat16))


def pick_tokens(place, rank, sides, row_count, earlier):
    _, tokens, width = sides[0][0].shape

    def kernel(place_ref, rank_ref, *refs):
        def store(rows):
            refs[PLANE][...] = rows

        each_source(pl.program_id(0), rank_ref, refs[:PLANE], store, row_count)

    def out_at(i, p):
        return row_block((i // PLANE) ^ p[2], p[0] ^ source_xor(i)), 0

    return run(
        kernel,
        2 * PLANE,
        token_specs(sides),
        pl.BlockSpec((row_count, width), out_at),
        jax.ShapeDtypeStruct((2 * PLANE * row_count, width), jnp.bfloat16),
        [],
        4 * PLANE * row_count * tokens * width,
        [place, rank, *sides[0], *sides[1]],
        earlier,
    )


def scaled_each(step, rank_ref, weight_ref, source_refs, store, row_count):
    for i, source_ref in enumerate(source_refs):

        @pl.when(step // 2 == i)
        def _():
            chosen, rows = pick_rows(rank_ref[0, 0], source_ref[0], row_count)
            scale = jnp.sum(jnp.where(chosen, weight_ref[0, 0], 0.0), axis=1, keepdims=True)
            store((scale * rows).astype(jnp.bfloat16))


def pick_cots(place, rank, weight, sides, row_count, earlier):
    _, tokens, width = sides[0][0].shape

    def kernel(place_ref, rank_ref, weight_ref, *refs):
        def store(rows):
            refs[PLANE][...] = rows

        scaled_each(pl.program_id(0), rank_ref, weight_ref, refs[:PLANE], store, row_count)

    def out_at(i, p):
        return row_block((i // PLANE) ^ p[2], p[0] ^ source_xor(i)), 0

    specs = token_specs(sides)
    return run(
        kernel,
        2 * PLANE,
        specs[:1] + specs,
        pl.BlockSpec((row_count, width), out_at),
        jax.ShapeDtypeStruct((2 * PLANE * row_count, width), jnp.bfloat16),
        [],
        4 * PLANE * row_count * tokens * width,
        [place, rank, weight, *sides[0], *sides[1]],
        earlier,
    )


def tile_at(step):
    return jnp.maximum(step - 2 * PLANE, 0)


def store_rows(block, rows, rows_ref, row_count):
    rows_ref[pl.ds(pl.multiple_of(block * row_count, row_count), row_count), :] = rows


def forward(place, rank, sides, w_gate, w_up, row_count):
    _, tokens, width = sides[0][0].shape
    ff = w_gate.shape[2]
    rows = 2 * PLANE * row_count

    def kernel(place_ref, rank_ref, *refs):
        gate_ref, up_ref, hidden_ref, gate_pre_ref, up_pre_ref, rows_ref = refs[PLANE:]
        step = pl.program_id(0)

        @pl.when(step < 2 * PLANE)
        def _():
            def store(rows):
                block = row_block(step // PLANE, place_ref[0] ^ source_xor(step))
                store_rows(block, rows, rows_ref, row_count)

            each_source(step, rank_ref, refs[:PLANE], store, row_count)

        @pl.when(step >= 2 * PLANE)
        def _():
            gate_pre = dot_f32(rows_ref[...], gate_ref[0])
            up_pre = dot_f32(rows_ref[...], up_ref[0])
            gate_pre_ref[...] = gate_pre
            up_pre_ref[...] = up_pre
            hidden_ref[...] = (gate_pre * jax.nn.sigmoid(gate_pre) * up_pre).astype(jnp.bfloat16)

    weight_spec = pl.BlockSpec((1, width, FF_TILE), lambda i, p: (0, 0, tile_at(i)))
    out_spec = pl.BlockSpec((rows, FF_TILE), lambda i, p: (0, tile_at(i)))
    return run(
        kernel,
        2 * PLANE + ff // FF_TILE,
        token_specs(sides) + [weight_spec] * 2,
        [out_spec] * 3,
        [jax.ShapeDtypeStruct((rows, ff), t) for t in (jnp.bfloat16, jnp.float32, jnp.float32)],
        [pltpu.VMEM((rows, width), jnp.bfloat16)],
        4 * rows * width * ff,
        [place, rank, *sides[0], *sides[1], w_gate, w_up],
    )


def backward(place, rank, weight, sides, w_down, gate_pre, up_pre, row_count, earlier):
    _, tokens, width = sides[0][0].shape
    ff = w_down.shape[1]
    rows = 2 * PLANE * row_count

    def kernel(place_ref, rank_ref, weight_ref, *refs):
        down_ref, gate_pre_ref, up_pre_ref, gate_grad_ref, up_grad_ref, rows_ref = refs[PLANE:]
        step = pl.program_id(0)

        @pl.when(step < 2 * PLANE)
        def _():
            def store(rows):
                block = row_block(step // PLANE, place_ref[0] ^ source_xor(step))
                store_rows(block, rows, rows_ref, row_count)

            scaled_each(step, rank_ref, weight_ref, refs[:PLANE], store, row_count)

        @pl.when(step >= 2 * PLANE)
        def _():
            hidden_grad = dot_f32(rows_ref[...], down_ref[0], CONTRACT_LAST)
            gate_pre = gate_pre_ref[...]
            sigma = jax.nn.sigmoid(gate_pre)
            slope = sigma * (1.0 + gate_pre * (1.0 - sigma))
            gate_grad_ref[...] = (hidden_grad * up_pre_ref[...] * slope).astype(jnp.bfloat16)
            up_grad_ref[...] = (hidden_grad * gate_pre * sigma).astype(jnp.bfloat16)

    specs = token_specs(sides)
    down_spec = pl.BlockSpec((1, FF_TILE, width), lambda i, p: (0, tile_at(i), 0))
    tile_spec = pl.BlockSpec((rows, FF_TILE), lambda i, p: (0, tile_at(i)))
    return run(
        kernel,
        2 * PLANE + ff // FF_TILE,
        specs[:1] + specs + [down_spec] + [tile_spec] * 2,
        [tile_spec] * 2,
        [jax.ShapeDtypeStruct((rows, ff), jnp.bfloat16)] * 2,
        [pltpu.VMEM((rows, width), jnp.bfloat16)],
        2 * rows * width * ff,
        [place, rank, weight, *sides[0], *sides[1], w_down, gate_pre, up_pre],
        earlier,
    )


def body(tokens, cotangent, expert_ids, combine, placement, moves, w_gate, w_up, w_down):
    owner_count = lax.axis_size("expert")
    dp_count = lax.axis_size("dp")
    my_index = lax.axis_index("expert")
    my_dp = lax.axis_index("dp")
    tok_rows, width = tokens.shape
    choose_count = expert_ids.shape[1]
    layers = owner_count // PLANE
    half = layers // 2
    row_count = 3 * tok_rows * choose_count // (4 * PLANE)
    pair = owner_count // 2
    own_layer, my_place = my_index // PLANE, my_index % PLANE
    inner = (own_layer == 1) | (own_layer == 2)
    layer_ids = jnp.arange(layers, dtype=jnp.int32)
    order = own_layer ^ layer_ids
    if layers == 4:
        order = jnp.where(inner, jnp.stack([order[j] for j in (0, 1, 3, 2)]), order)
    routing = jnp.concatenate([expert_ids.astype(jnp.float32), combine], axis=1)
    lines = [routing] + [crossed(routing, "expert", j * PLANE) for j in range(1, layers)]
    if layers == 4:
        lines = lines[:2] + [jnp.where(inner, a, b) for a, b in (lines[:1:-1], lines[2:])]
    routing = jnp.stack(lines).transpose(2, 0, 1)
    routings = [routing] + [crossed(routing, "expert", k) for k in range(1, PLANE)]
    routing = jnp.stack(routings)
    routed = there(inner, *routings)
    token_sides = [plane_gather(side) for side in layer_gather(tokens, routed, layers)]
    cot_sides = [plane_gather(side) for side in layer_gather(cotangent, inner, layers)]
    ids, weights = routing[:, :choose_count], routing[:, choose_count:]

    slot_ids = jnp.arange(owner_count, dtype=jnp.int32)
    held = jnp.where(moves == 1, jnp.roll(placement, pair), placement)
    mine = slot_ids == my_index
    home_expert = jnp.sum(jnp.where(mine, placement, 0))
    held_expert = jnp.sum(jnp.where(mine, held, 0))
    my_move = jnp.sum(jnp.where(mine, moves, 0))
    moved = my_move == 1
    place = jnp.stack([my_place, own_layer // half, my_move]).astype(jnp.int32)
    plane_slots = own_layer * PLANE + jnp.arange(PLANE, dtype=jnp.int32)
    near = slot_ids[None, :] == plane_slots[:, None]
    plane_experts = jnp.sum(jnp.where(near, placement[None], 0), axis=1)

    def named(expert, source_ids, source_weights):
        match = source_ids == expert.astype(jnp.float32)
        return jnp.any(match, axis=1), jnp.sum(jnp.where(match, source_weights, 0.0), axis=1)

    sets = [
        named(home_expert, ids, weights),
        named(held_expert, ids, weights),
        named(plane_experts[:, None, None, None], ids[:1], weights[:1]),
    ]
    rank = rank_rows(jnp.concatenate([s[0] for s in sets]), order)
    weight = jnp.concatenate([jnp.broadcast_to(s[1], (PLANE,) + s[1].shape[1:]) for s in sets])

    def halves(array):
        array = array.reshape(len(sets), PLANE, 2, 1, half * tok_rows)
        return array.transpose(0, 2, 1, 3, 4)

    home_rank, held_rank, back_rank = halves(rank)
    home_weight, held_weight, back_weight = halves(weight)

    groups = [[i * PLANE + j for j in range(PLANE)] for i in range(layers)]

    def sent_back(rows):
        rows = rows.reshape(PLANE, 2 * row_count, width)
        return lax.all_to_all(
            rows, "expert", split_axis=0, concat_axis=0, axis_index_groups=groups, tiled=True
        )

    def spread(back, weighted, flag):
        numbers = jnp.arange(row_count, dtype=jnp.int32)[None, None, :, None]
        chosen = (back_rank.transpose(1, 0, 2, 3) == numbers) & flag
        rows = back.reshape(PLANE, 2, row_count, width)
        if weighted:
            weights = back_weight.transpose(1, 0, 2, 3)
            scale = jnp.sum(jnp.where(chosen, weights, 0.0), axis=3, keepdims=True)
            rows = (scale * rows.astype(jnp.float32)).astype(jnp.bfloat16)
        same = jnp.eye(2, dtype=bool)[None, :, None, :, None]
        one_hot = (chosen[:, :, :, None, :] & same).astype(jnp.bfloat16)
        one_hot = one_hot.reshape(2 * PLANE * row_count, layers * tok_rows)
        rows = rows.reshape(2 * PLANE * row_count, width)
        return dot_f32(one_hot, rows, CONTRACT_ROWS).astype(jnp.bfloat16)

    hidden, *pre = forward(place, home_rank, token_sides, w_gate, w_up, row_count)
    got_hidden = crossed(hidden, "expert", pair)
    out_rows = dot_f32(hidden, w_down[0]).astype(jnp.bfloat16)
    out_back = sent_back(out_rows)
    gate_grad, up_grad = backward(
        place, home_rank, home_weight, cot_sides, w_down, *pre, row_count, [out_rows]
    )
    got_gate_grad = crossed(when(there(True, got_hidden), gate_grad), "expert", pair)
    held_cots = pick_cots(place, held_rank, held_weight, cot_sides, row_count, [out_rows])
    held_rows = pick_tokens(place, held_rank, token_sides, row_count, [held_cots])

    def product(left, right, part):
        share = left.shape[1] // dp_count
        columns = lax.dynamic_slice_in_dim(left, part * share, share, axis=1)
        return dot_f32(columns, right, CONTRACT_ROWS)

    def dp_share(left, right):
        return product(left, right, (my_dp + 1) % dp_count).astype(jnp.bfloat16)

    def dp_sum(left, right, got):
        return ((product(left, right, my_dp) + got.astype(jnp.float32)) * (1.0 / dp_count))[None]

    held_hidden = jnp.where(moved, got_hidden, hidden)
    got_down = crossed(dp_share(held_hidden, held_cots), "dp", 1)
    grad_rows = dot_f32(gate_grad, w_gate[0], CONTRACT_LAST)
    grad_rows = grad_rows + dot_f32(up_grad, w_up[0], CONTRACT_LAST)
    grad_rows = when(there(True, got_hidden), grad_rows).astype(jnp.bfloat16)

    sent_up_grad = when(there(True, got_gate_grad, got_down), up_grad)
    got_up_grad = crossed(sent_up_grad, "expert", pair)
    out_spread = spread(out_back, True, there(True, gate_grad))
    out_in = layer_send(out_spread, tok_rows, layers)
    grad_spread = spread(sent_back(grad_rows), False, True)
    grad_in = layer_send(grad_spread, tok_rows, layers)
    mixed = layer_reduce(out_spread, out_in, tok_rows, layers, there(True, got_gate_grad))
    input_grad = layer_reduce(grad_spread, grad_in, tok_rows, layers, there(True, got_up_grad))

    grad_down = dp_sum(held_hidden, held_cots, got_down)
    held_gate = jnp.where(moved, got_gate_grad, gate_grad)
    held_up = jnp.where(moved, got_up_grad, up_grad)
    grad_gate, grad_up = [
        dp_sum(held_rows, held, crossed(dp_share(held_rows, held), "dp", 1))
        for held in (held_gate, held_up)
    ]
    return mixed, input_grad, grad_gate, grad_up, grad_down


def solution(mesh):
    tokens = P(("dp", "expert"), None)
    slots = P("expert", None, None)
    grads = P("expert", "dp", None)
    return jax.shard_map(
        body,
        mesh=mesh,
        in_specs=(tokens, tokens, tokens, tokens, P(), P(), slots, slots, slots),
        out_specs=(tokens, tokens, grads, grads, grads),
        check_vma=False,
    )
```

```python
import jax
import jax.numpy as jnp
from jax import lax
from jax.experimental import pallas as pl
from jax.experimental.pallas import tpu as pltpu
from jax.sharding import PartitionSpec as P

CONTRACT_ROWS = (((0,), (0,)), ((), ()))
CONTRACT_LAST = (((1,), (1,)), ((), ()))
PLANE = 4
FF_TILE = 256
VMEM_BYTES = 48 * 1024 * 1024


def dot_f32(a, b, dims=(((1,), (0,)), ((), ()))):
    return lax.dot_general(a, b, dims, preferred_element_type=jnp.float32)


def crossed(array, axis, flip):
    return lax.ppermute(array, axis, [(i, i ^ flip) for i in range(lax.axis_size(axis))])


def along(array, pairs):
    return lax.ppermute(array, "expert", pairs)


def line_pairs(owner_count):
    inner = [i for i in range(owner_count) if i // PLANE in (1, 2)]
    middle = [(i, i ^ 3 * PLANE) for i in inner]
    outward = [(i, i ^ PLANE) for i in inner]
    inward = [(i ^ PLANE, i) for i in inner]
    return middle, outward, inward


def there(flag, *arrays):
    for array in arrays:
        corner = array[tuple(slice(0, 1) for _ in array.shape)].reshape(())
        flag = flag & (corner == corner)
    return flag


def when(flag, array):
    return jnp.where(flag, array, jnp.zeros((), array.dtype))


def layer_gather(block, inner, layers):
    if layers != 4:
        got = [block] + [crossed(block, "expert", j * PLANE) for j in range(1, layers)]
        return jnp.concatenate(got[: layers // 2]), jnp.concatenate(got[layers // 2 :])
    middle, outward, _ = line_pairs(layers * PLANE)
    near = crossed(block, "expert", PLANE)
    far = [along(block, middle), along(near, middle)]
    relayed = [along(array, outward) for array in far]
    far_half = jnp.where(inner, jnp.concatenate(far), jnp.concatenate(relayed))
    return jnp.concatenate([block, near]), far_half


def plane_gather(half, earlier=()):
    mine = when(there(True, *earlier), jnp.stack([half, crossed(half, "expert", 2)]))
    return mine, crossed(mine, "expert", 1)


def layer_send(spread, tok_rows, layers):
    if layers != 4:
        blocks = [spread[j * tok_rows : (j + 1) * tok_rows] for j in range(1, layers)]
        return [crossed(block, "expert", j * PLANE) for j, block in enumerate(blocks, 1)]
    return [along(spread[tok_rows:], line_pairs(layers * PLANE)[2])]


def layer_reduce(spread, got, tok_rows, layers, flag):
    def total(parts):
        return sum(part.astype(jnp.float32) for part in parts).astype(jnp.bfloat16)

    if layers != 4:
        return total([spread[:tok_rows]] + got)
    middle, outward, _ = line_pairs(layers * PLANE)
    near_in, far_in = got[0][:tok_rows], got[0][tok_rows:]
    far_sum = total([spread[2 * tok_rows :], far_in])
    crossing = along(when(flag, far_sum), middle)
    near_sum = total([spread[tok_rows : 2 * tok_rows], crossing[tok_rows:]])
    near_out = along(near_sum, outward)
    return total([spread[:tok_rows], near_in, crossing[:tok_rows], near_out])


def rank_rows(hit, order):
    half = order.shape[0] // 2
    tok_rows = hit.shape[2]
    earlier = jnp.arange(tok_rows)[:, None] < jnp.arange(tok_rows)[None, :]
    within = jnp.einsum(
        "slt,tu->slu",
        hit.astype(jnp.bfloat16),
        earlier.astype(jnp.bfloat16),
        preferred_element_type=jnp.float32,
    ).astype(jnp.int32)
    count = jnp.sum(hit.astype(jnp.int32), axis=2)
    ahead = (order[:, None] < order[None, :]) & (order[:, None] // half == order[None, :] // half)
    before = jnp.sum(jnp.where(ahead[None], count[:, :, None], 0), axis=1)
    return jnp.where(hit, within + before[:, :, None], -1)


def pick_rows(rank, source, row_count):
    place = lax.broadcasted_iota(jnp.int32, (row_count, rank.shape[1]), 0)
    chosen = place == rank
    one_hot = jnp.where(chosen, 1.0, 0.0).astype(jnp.bfloat16)
    return chosen, dot_f32(one_hot, source)


def source_xor(step):
    return (step % PLANE) // 2 + 2 * (step % 2)


def run(kernel, grid, in_specs, out_specs, out_shape, scratch, flops, args, earlier=()):
    moved = sum(a.size * a.dtype.itemsize for a in args)
    count = len(in_specs) + 1
    in_specs = in_specs + [pl.BlockSpec(memory_space=pl.ANY)] * len(earlier)
    if earlier:
        inner_kernel = kernel

        def kernel(*refs):
            inner_kernel(*refs[:count], *refs[count + len(earlier) :])

    return pl.pallas_call(
        kernel,
        grid_spec=pltpu.PrefetchScalarGridSpec(
            num_scalar_prefetch=1,
            grid=(grid,),
            in_specs=in_specs,
            out_specs=out_specs,
            scratch_shapes=scratch,
        ),
        out_shape=out_shape,
        compiler_params=pltpu.CompilerParams(vmem_limit_bytes=VMEM_BYTES),
        cost_estimate=pl.CostEstimate(flops=flops, bytes_accessed=moved, transcendentals=0),
    )(*args, *earlier)


def row_block(side, source):
    return source * 2 + side


def token_specs(sides):
    _, tokens, width = sides[0][0].shape

    def line_at(i, p):
        i = jnp.minimum(i, 2 * PLANE - 1)
        return i // PLANE, source_xor(i), 0, 0

    def source(first):
        return pl.BlockSpec((1, tokens, width), lambda i, p: (jnp.clip(i - first, 0, 1), 0, 0))

    return [pl.BlockSpec((1, 1, 1, tokens), line_at)] + [source(2 * i) for i in range(PLANE)]


def each_source(step, rank_ref, source_refs, store, row_count):
    for i, source_ref in enumerate(source_refs):

        @pl.when(step // 2 == i)
        def _():
            store(pick_rows(rank_ref[0, 0], source_ref[0], row_count)[1].astype(jnp.bfloat16))


def pick_tokens(place, rank, sides, row_count, earlier):
    _, tokens, width = sides[0][0].shape

    def kernel(place_ref, rank_ref, *refs):
        def store(rows):
            refs[PLANE][...] = rows

        each_source(pl.program_id(0), rank_ref, refs[:PLANE], store, row_count)

    def out_at(i, p):
        return row_block((i // PLANE) ^ p[2], p[0] ^ source_xor(i)), 0

    return run(
        kernel,
        2 * PLANE,
        token_specs(sides),
        pl.BlockSpec((row_count, width), out_at),
        jax.ShapeDtypeStruct((2 * PLANE * row_count, width), jnp.bfloat16),
        [],
        4 * PLANE * row_count * tokens * width,
        [place, rank, *sides[0], *sides[1]],
        earlier,
    )


def scaled_each(step, rank_ref, weight_ref, source_refs, store, row_count):
    for i, source_ref in enumerate(source_refs):

        @pl.when(step // 2 == i)
        def _():
            chosen, rows = pick_rows(rank_ref[0, 0], source_ref[0], row_count)
            scale = jnp.sum(jnp.where(chosen, weight_ref[0, 0], 0.0), axis=1, keepdims=True)
            store((scale * rows).astype(jnp.bfloat16))


def pick_cots(place, rank, weight, sides, row_count, earlier):
    _, tokens, width = sides[0][0].shape

    def kernel(place_ref, rank_ref, weight_ref, *refs):
        def store(rows):
            refs[PLANE][...] = rows

        scaled_each(pl.program_id(0), rank_ref, weight_ref, refs[:PLANE], store, row_count)

    def out_at(i, p):
        return row_block((i // PLANE) ^ p[2], p[0] ^ source_xor(i)), 0

    specs = token_specs(sides)
    return run(
        kernel,
        2 * PLANE,
        specs[:1] + specs,
        pl.BlockSpec((row_count, width), out_at),
        jax.ShapeDtypeStruct((2 * PLANE * row_count, width), jnp.bfloat16),
        [],
        4 * PLANE * row_count * tokens * width,
        [place, rank, weight, *sides[0], *sides[1]],
        earlier,
    )


def tile_at(step):
    return jnp.maximum(step - 2 * PLANE, 0)


def store_rows(block, rows, rows_ref, row_count):
    rows_ref[pl.ds(pl.multiple_of(block * row_count, row_count), row_count), :] = rows


def forward(place, rank, sides, w_gate, w_up, row_count):
    _, tokens, width = sides[0][0].shape
    ff = w_gate.shape[2]
    rows = 2 * PLANE * row_count

    def kernel(place_ref, rank_ref, *refs):
        gate_ref, up_ref, hidden_ref, gate_pre_ref, up_pre_ref, rows_ref = refs[PLANE:]
        step = pl.program_id(0)

        @pl.when(step < 2 * PLANE)
        def _():
            def store(rows):
                block = row_block(step // PLANE, place_ref[0] ^ source_xor(step))
                store_rows(block, rows, rows_ref, row_count)

            each_source(step, rank_ref, refs[:PLANE], store, row_count)

        @pl.when(step >= 2 * PLANE)
        def _():
            gate_pre = dot_f32(rows_ref[...], gate_ref[0])
            up_pre = dot_f32(rows_ref[...], up_ref[0])
            gate_pre_ref[...] = gate_pre
            up_pre_ref[...] = up_pre
            hidden_ref[...] = (gate_pre * jax.nn.sigmoid(gate_pre) * up_pre).astype(jnp.bfloat16)

    weight_spec = pl.BlockSpec((1, width, FF_TILE), lambda i, p: (0, 0, tile_at(i)))
    out_spec = pl.BlockSpec((rows, FF_TILE), lambda i, p: (0, tile_at(i)))
    return run(
        kernel,
        2 * PLANE + ff // FF_TILE,
        token_specs(sides) + [weight_spec] * 2,
        [out_spec] * 3,
        [jax.ShapeDtypeStruct((rows, ff), t) for t in (jnp.bfloat16, jnp.float32, jnp.float32)],
        [pltpu.VMEM((rows, width), jnp.bfloat16)],
        4 * rows * width * ff,
        [place, rank, *sides[0], *sides[1], w_gate, w_up],
    )


def backward(place, rank, weight, sides, w_down, gate_pre, up_pre, row_count, earlier):
    _, tokens, width = sides[0][0].shape
    ff = w_down.shape[1]
    rows = 2 * PLANE * row_count

    def kernel(place_ref, rank_ref, weight_ref, *refs):
        down_ref, gate_pre_ref, up_pre_ref, gate_grad_ref, up_grad_ref, rows_ref = refs[PLANE:]
        step = pl.program_id(0)

        @pl.when(step < 2 * PLANE)
        def _():
            def store(rows):
                block = row_block(step // PLANE, place_ref[0] ^ source_xor(step))
                store_rows(block, rows, rows_ref, row_count)

            scaled_each(step, rank_ref, weight_ref, refs[:PLANE], store, row_count)

        @pl.when(step >= 2 * PLANE)
        def _():
            hidden_grad = dot_f32(rows_ref[...], down_ref[0], CONTRACT_LAST)
            gate_pre = gate_pre_ref[...]
            sigma = jax.nn.sigmoid(gate_pre)
            slope = sigma * (1.0 + gate_pre * (1.0 - sigma))
            gate_grad_ref[...] = (hidden_grad * up_pre_ref[...] * slope).astype(jnp.bfloat16)
            up_grad_ref[...] = (hidden_grad * gate_pre * sigma).astype(jnp.bfloat16)

    specs = token_specs(sides)
    down_spec = pl.BlockSpec((1, FF_TILE, width), lambda i, p: (0, tile_at(i), 0))
    tile_spec = pl.BlockSpec((rows, FF_TILE), lambda i, p: (0, tile_at(i)))
    return run(
        kernel,
        2 * PLANE + ff // FF_TILE,
        specs[:1] + specs + [down_spec] + [tile_spec] * 2,
        [tile_spec] * 2,
        [jax.ShapeDtypeStruct((rows, ff), jnp.bfloat16)] * 2,
        [pltpu.VMEM((rows, width), jnp.bfloat16)],
        2 * rows * width * ff,
        [place, rank, weight, *sides[0], *sides[1], w_down, gate_pre, up_pre],
        earlier,
    )


def body(tokens, cotangent, expert_ids, combine, placement, moves, w_gate, w_up, w_down):
    owner_count = lax.axis_size("expert")
    dp_count = lax.axis_size("dp")
    my_index = lax.axis_index("expert")
    my_dp = lax.axis_index("dp")
    tok_rows, width = tokens.shape
    choose_count = expert_ids.shape[1]
    layers = owner_count // PLANE
    half = layers // 2
    row_count = 3 * tok_rows * choose_count // (4 * PLANE)
    pair = owner_count // 2
    own_layer, my_place = my_index // PLANE, my_index % PLANE
    inner = (own_layer == 1) | (own_layer == 2)
    layer_ids = jnp.arange(layers, dtype=jnp.int32)
    order = own_layer ^ layer_ids
    if layers == 4:
        order = jnp.where(inner, jnp.stack([order[j] for j in (0, 1, 3, 2)]), order)
    routing = jnp.concatenate([expert_ids.astype(jnp.float32), combine], axis=1)
    lines = [routing] + [crossed(routing, "expert", j * PLANE) for j in range(1, layers)]
    if layers == 4:
        lines = lines[:2] + [jnp.where(inner, a, b) for a, b in (lines[:1:-1], lines[2:])]
    routing = jnp.stack(lines).transpose(2, 0, 1)
    routings = [routing] + [crossed(routing, "expert", k) for k in range(1, PLANE)]
    routing = jnp.stack(routings)
    routed = there(inner, *routings)
    token_sides = [plane_gather(side) for side in layer_gather(tokens, routed, layers)]
    ids, weights = routing[:, :choose_count], routing[:, choose_count:]

    slot_ids = jnp.arange(owner_count, dtype=jnp.int32)
    held = jnp.where(moves == 1, jnp.roll(placement, pair), placement)
    mine = slot_ids == my_index
    home_expert = jnp.sum(jnp.where(mine, placement, 0))
    held_expert = jnp.sum(jnp.where(mine, held, 0))
    my_move = jnp.sum(jnp.where(mine, moves, 0))
    moved = my_move == 1
    place = jnp.stack([my_place, own_layer // half, my_move]).astype(jnp.int32)
    plane_slots = own_layer * PLANE + jnp.arange(PLANE, dtype=jnp.int32)
    near = slot_ids[None, :] == plane_slots[:, None]
    plane_experts = jnp.sum(jnp.where(near, placement[None], 0), axis=1)

    def named(expert, source_ids, source_weights):
        match = source_ids == expert.astype(jnp.float32)
        return jnp.any(match, axis=1), jnp.sum(jnp.where(match, source_weights, 0.0), axis=1)

    sets = [
        named(home_expert, ids, weights),
        named(held_expert, ids, weights),
        named(plane_experts[:, None, None, None], ids[:1], weights[:1]),
    ]
    rank = rank_rows(jnp.concatenate([s[0] for s in sets]), order)
    weight = jnp.concatenate([jnp.broadcast_to(s[1], (PLANE,) + s[1].shape[1:]) for s in sets])

    def halves(array):
        array = array.reshape(len(sets), PLANE, 2, 1, half * tok_rows)
        return array.transpose(0, 2, 1, 3, 4)

    home_rank, held_rank, back_rank = halves(rank)
    home_weight, held_weight, back_weight = halves(weight)

    groups = [[i * PLANE + j for j in range(PLANE)] for i in range(layers)]

    def sent_back(rows):
        rows = rows.reshape(PLANE, 2 * row_count, width)
        return lax.all_to_all(
            rows, "expert", split_axis=0, concat_axis=0, axis_index_groups=groups, tiled=True
        )

    def spread(back, weighted, flag):
        numbers = jnp.arange(row_count, dtype=jnp.int32)[None, None, :, None]
        chosen = (back_rank.transpose(1, 0, 2, 3) == numbers) & flag
        rows = back.reshape(PLANE, 2, row_count, width)
        if weighted:
            weights = back_weight.transpose(1, 0, 2, 3)
            scale = jnp.sum(jnp.where(chosen, weights, 0.0), axis=3, keepdims=True)
            rows = (scale * rows.astype(jnp.float32)).astype(jnp.bfloat16)
        same = jnp.eye(2, dtype=bool)[None, :, None, :, None]
        one_hot = (chosen[:, :, :, None, :] & same).astype(jnp.bfloat16)
        one_hot = one_hot.reshape(2 * PLANE * row_count, layers * tok_rows)
        rows = rows.reshape(2 * PLANE * row_count, width)
        return dot_f32(one_hot, rows, CONTRACT_ROWS).astype(jnp.bfloat16)

    hidden, *pre = forward(place, home_rank, token_sides, w_gate, w_up, row_count)
    got_hidden = crossed(hidden, "expert", pair)
    near_cots, far_cots = layer_gather(cotangent, there(inner, hidden), layers)
    cot_sides = [plane_gather(near_cots, [hidden]), plane_gather(far_cots)]
    out_rows = dot_f32(hidden, w_down[0]).astype(jnp.bfloat16)
    out_back = sent_back(out_rows)
    gate_grad, up_grad = backward(
        place, home_rank, home_weight, cot_sides, w_down, *pre, row_count, [out_rows]
    )
    got_gate_grad = crossed(gate_grad, "expert", pair)
    held_cots = pick_cots(place, held_rank, held_weight, cot_sides, row_count, [out_rows])
    held_rows = pick_tokens(place, held_rank, token_sides, row_count, [held_cots])

    def product(left, right, part):
        share = left.shape[1] // dp_count
        columns = lax.dynamic_slice_in_dim(left, part * share, share, axis=1)
        return dot_f32(columns, right, CONTRACT_ROWS)

    def dp_share(left, right):
        return product(left, right, (my_dp + 1) % dp_count).astype(jnp.bfloat16)

    def dp_sum(left, right, got):
        return ((product(left, right, my_dp) + got.astype(jnp.float32)) * (1.0 / dp_count))[None]

    held_hidden = jnp.where(moved, got_hidden, hidden)
    got_down = crossed(dp_share(held_hidden, held_cots), "dp", 1)
    grad_rows = dot_f32(gate_grad, w_gate[0], CONTRACT_LAST)
    grad_rows = grad_rows + dot_f32(up_grad, w_up[0], CONTRACT_LAST)
    grad_rows = when(there(True, got_hidden), grad_rows).astype(jnp.bfloat16)

    sent_up_grad = when(there(True, got_gate_grad, got_down), up_grad)
    got_up_grad = crossed(sent_up_grad, "expert", pair)
    out_spread = spread(out_back, True, there(True, gate_grad))
    out_in = layer_send(out_spread, tok_rows, layers)
    grad_spread = spread(sent_back(grad_rows), False, True)
    grad_in = layer_send(grad_spread, tok_rows, layers)
    mixed = layer_reduce(out_spread, out_in, tok_rows, layers, there(True, got_gate_grad))
    input_grad = layer_reduce(grad_spread, grad_in, tok_rows, layers, there(True, got_up_grad))

    grad_down = dp_sum(held_hidden, held_cots, got_down)
    held_gate = jnp.where(moved, got_gate_grad, gate_grad)
    held_up = jnp.where(moved, got_up_grad, up_grad)
    grad_gate, grad_up = [
        dp_sum(held_rows, held, crossed(dp_share(held_rows, held), "dp", 1))
        for held in (held_gate, held_up)
    ]
    return mixed, input_grad, grad_gate, grad_up, grad_down


def solution(mesh):
    tokens = P(("dp", "expert"), None)
    slots = P("expert", None, None)
    grads = P("expert", "dp", None)
    return jax.shard_map(
        body,
        mesh=mesh,
        in_specs=(tokens, tokens, tokens, tokens, P(), P(), slots, slots, slots),
        out_specs=(tokens, tokens, grads, grads, grads),
        check_vma=False,
    )
```

```python
import jax
import jax.numpy as jnp
from jax import lax
from jax.experimental import pallas as pl
from jax.experimental.pallas import tpu as pltpu
from jax.sharding import PartitionSpec as P

CONTRACT_ROWS = (((0,), (0,)), ((), ()))
CONTRACT_LAST = (((1,), (1,)), ((), ()))
PLANE = 4
FF_TILE = 256
VMEM_BYTES = 48 * 1024 * 1024


def dot_f32(a, b, dims=(((1,), (0,)), ((), ()))):
    return lax.dot_general(a, b, dims, preferred_element_type=jnp.float32)


def crossed(array, axis, flip):
    return lax.ppermute(array, axis, [(i, i ^ flip) for i in range(lax.axis_size(axis))])


def along(array, pairs):
    return lax.ppermute(array, "expert", pairs)


def line_pairs(owner_count):
    inner = [i for i in range(owner_count) if i // PLANE in (1, 2)]
    middle = [(i, i ^ 3 * PLANE) for i in inner]
    outward = [(i, i ^ PLANE) for i in inner]
    inward = [(i ^ PLANE, i) for i in inner]
    return middle, outward, inward


def there(flag, *arrays):
    for array in arrays:
        corner = array[tuple(slice(0, 1) for _ in array.shape)].reshape(())
        flag = flag & (corner == corner)
    return flag


def when(flag, array):
    return jnp.where(flag, array, jnp.zeros((), array.dtype))


def layer_gather(block, layers):
    return [block] + [crossed(block, "expert", j * PLANE) for j in range(1, layers)]


def plane_gather(blocks):
    crossing = [crossed(block, "expert", 2) for block in blocks]
    mine = jnp.stack([jnp.concatenate(blocks), jnp.concatenate(crossing)])
    return mine, crossed(mine, "expert", 1)


def layer_send(spread, tok_rows, layers):
    if layers != 4:
        blocks = [spread[j * tok_rows : (j + 1) * tok_rows] for j in range(1, layers)]
        return [crossed(block, "expert", j * PLANE) for j, block in enumerate(blocks, 1)]
    return [along(spread[tok_rows:], line_pairs(layers * PLANE)[2])]


def layer_reduce(spread, got, tok_rows, layers, flag):
    def total(parts):
        return sum(part.astype(jnp.float32) for part in parts).astype(jnp.bfloat16)

    if layers != 4:
        return total([spread[:tok_rows]] + got)
    middle, outward, _ = line_pairs(layers * PLANE)
    near_in, far_in = got[0][:tok_rows], got[0][tok_rows:]
    far_in = jnp.concatenate([far_in[tok_rows:], far_in[:tok_rows]])
    far_sum = total([spread[2 * tok_rows :], far_in])
    crossing = along(when(flag, far_sum), middle)
    near_sum = total([spread[tok_rows : 2 * tok_rows], crossing[:tok_rows]])
    near_out = along(near_sum, outward)
    return total([spread[:tok_rows], near_in, crossing[tok_rows:], near_out])


def rank_rows(hit, order):
    half = order.shape[0] // 2
    tok_rows = hit.shape[2]
    earlier = jnp.arange(tok_rows)[:, None] < jnp.arange(tok_rows)[None, :]
    within = jnp.einsum(
        "slt,tu->slu",
        hit.astype(jnp.bfloat16),
        earlier.astype(jnp.bfloat16),
        preferred_element_type=jnp.float32,
    ).astype(jnp.int32)
    count = jnp.sum(hit.astype(jnp.int32), axis=2)
    ahead = (order[:, None] < order[None, :]) & (order[:, None] // half == order[None, :] // half)
    before = jnp.sum(jnp.where(ahead[None], count[:, :, None], 0), axis=1)
    return jnp.where(hit, within + before[:, :, None], -1)


def pick_rows(rank, source, row_count):
    place = lax.broadcasted_iota(jnp.int32, (row_count, rank.shape[1]), 0)
    chosen = place == rank
    one_hot = jnp.where(chosen, 1.0, 0.0).astype(jnp.bfloat16)
    return chosen, dot_f32(one_hot, source)


def source_xor(step):
    return (step % PLANE) // 2 + 2 * (step % 2)


def run(kernel, grid, in_specs, out_specs, out_shape, scratch, flops, args, earlier=()):
    moved = sum(a.size * a.dtype.itemsize for a in args)
    count = len(in_specs) + 1
    in_specs = in_specs + [pl.BlockSpec(memory_space=pl.ANY)] * len(earlier)
    if earlier:
        inner_kernel = kernel

        def kernel(*refs):
            inner_kernel(*refs[:count], *refs[count + len(earlier) :])

    return pl.pallas_call(
        kernel,
        grid_spec=pltpu.PrefetchScalarGridSpec(
            num_scalar_prefetch=1,
            grid=(grid,),
            in_specs=in_specs,
            out_specs=out_specs,
            scratch_shapes=scratch,
        ),
        out_shape=out_shape,
        compiler_params=pltpu.CompilerParams(vmem_limit_bytes=VMEM_BYTES),
        cost_estimate=pl.CostEstimate(flops=flops, bytes_accessed=moved, transcendentals=0),
    )(*args, *earlier)


def row_block(side, source):
    return source * 2 + side


def token_specs(sides):
    _, tokens, width = sides[0][0].shape

    def line_at(i, p):
        i = jnp.minimum(i, 2 * PLANE - 1)
        return i // PLANE, source_xor(i), 0, 0

    def source(first):
        return pl.BlockSpec((1, tokens, width), lambda i, p: (jnp.clip(i - first, 0, 1), 0, 0))

    return [pl.BlockSpec((1, 1, 1, tokens), line_at)] + [source(2 * i) for i in range(PLANE)]


def each_source(step, rank_ref, source_refs, store, row_count):
    for i, source_ref in enumerate(source_refs):

        @pl.when(step // 2 == i)
        def _():
            store(pick_rows(rank_ref[0, 0], source_ref[0], row_count)[1].astype(jnp.bfloat16))


def pick_tokens(place, rank, sides, row_count, earlier):
    _, tokens, width = sides[0][0].shape

    def kernel(place_ref, rank_ref, *refs):
        def store(rows):
            refs[PLANE][...] = rows

        each_source(pl.program_id(0), rank_ref, refs[:PLANE], store, row_count)

    def out_at(i, p):
        return row_block((i // PLANE) ^ p[2], p[0] ^ source_xor(i)), 0

    return run(
        kernel,
        2 * PLANE,
        token_specs(sides),
        pl.BlockSpec((row_count, width), out_at),
        jax.ShapeDtypeStruct((2 * PLANE * row_count, width), jnp.bfloat16),
        [],
        4 * PLANE * row_count * tokens * width,
        [place, rank, *sides[0], *sides[1]],
        earlier,
    )


def cot_specs(cots):
    layers, _, tok_rows, width = cots.shape
    tokens = layers // 2 * tok_rows

    def line_at(i, p):
        i = jnp.minimum(i, 2 * PLANE - 1)
        return i // PLANE, (i % PLANE) ^ p[0], 0, 0

    def block_at(i, p):
        i = jnp.minimum(i, 2 * PLANE - 1)
        return (i // PLANE) ^ p[1], i % PLANE, 0, 0

    line = pl.BlockSpec((1, 1, 1, tokens), line_at)
    return [line, line, pl.BlockSpec((layers // 2, 1, tok_rows, width), block_at)]


def scaled_rows(rank_ref, weight_ref, cots_ref, row_count):
    source = cots_ref[...].reshape(-1, cots_ref.shape[-1])
    chosen, rows = pick_rows(rank_ref[0, 0], source, row_count)
    scale = jnp.sum(jnp.where(chosen, weight_ref[0, 0], 0.0), axis=1, keepdims=True)
    return (scale * rows).astype(jnp.bfloat16)


def pick_cots(place, rank, weight, cots, row_count, earlier):
    width = cots.shape[3]

    def kernel(place_ref, rank_ref, weight_ref, cots_ref, rows_ref):
        rows_ref[...] = scaled_rows(rank_ref, weight_ref, cots_ref, row_count)

    def out_at(i, p):
        return row_block((i // PLANE) ^ p[2], i % PLANE), 0

    return run(
        kernel,
        2 * PLANE,
        cot_specs(cots),
        pl.BlockSpec((row_count, width), out_at),
        jax.ShapeDtypeStruct((2 * PLANE * row_count, width), jnp.bfloat16),
        [],
        2 * row_count * cots.size,
        [place, rank, weight, cots],
        earlier,
    )


def tile_at(step):
    return jnp.maximum(step - 2 * PLANE, 0)


def store_rows(block, rows, rows_ref, row_count):
    rows_ref[pl.ds(pl.multiple_of(block * row_count, row_count), row_count), :] = rows


def forward(place, rank, sides, w_gate, w_up, row_count):
    _, tokens, width = sides[0][0].shape
    ff = w_gate.shape[2]
    rows = 2 * PLANE * row_count

    def kernel(place_ref, rank_ref, *refs):
        gate_ref, up_ref, hidden_ref, gate_pre_ref, up_pre_ref, rows_ref = refs[PLANE:]
        step = pl.program_id(0)

        @pl.when(step < 2 * PLANE)
        def _():
            def store(rows):
                block = row_block(step // PLANE, place_ref[0] ^ source_xor(step))
                store_rows(block, rows, rows_ref, row_count)

            each_source(step, rank_ref, refs[:PLANE], store, row_count)

        @pl.when(step >= 2 * PLANE)
        def _():
            gate_pre = dot_f32(rows_ref[...], gate_ref[0])
            up_pre = dot_f32(rows_ref[...], up_ref[0])
            gate_pre_ref[...] = gate_pre
            up_pre_ref[...] = up_pre
            hidden_ref[...] = (gate_pre * jax.nn.sigmoid(gate_pre) * up_pre).astype(jnp.bfloat16)

    weight_spec = pl.BlockSpec((1, width, FF_TILE), lambda i, p: (0, 0, tile_at(i)))
    out_spec = pl.BlockSpec((rows, FF_TILE), lambda i, p: (0, tile_at(i)))
    return run(
        kernel,
        2 * PLANE + ff // FF_TILE,
        token_specs(sides) + [weight_spec] * 2,
        [out_spec] * 3,
        [jax.ShapeDtypeStruct((rows, ff), t) for t in (jnp.bfloat16, jnp.float32, jnp.float32)],
        [pltpu.VMEM((rows, width), jnp.bfloat16)],
        4 * rows * width * ff,
        [place, rank, *sides[0], *sides[1], w_gate, w_up],
    )


def backward(place, rank, weight, cots, w_down, gate_pre, up_pre, row_count, earlier):
    width = cots.shape[3]
    ff = w_down.shape[1]
    rows = 2 * PLANE * row_count

    def kernel(place_ref, rank_ref, weight_ref, cots_ref, down_ref, *refs):
        gate_pre_ref, up_pre_ref, gate_grad_ref, up_grad_ref, rows_ref = refs
        step = pl.program_id(0)

        @pl.when(step < 2 * PLANE)
        def _():
            block = row_block(step // PLANE, step % PLANE)
            rows = scaled_rows(rank_ref, weight_ref, cots_ref, row_count)
            store_rows(block, rows, rows_ref, row_count)

        @pl.when(step >= 2 * PLANE)
        def _():
            hidden_grad = dot_f32(rows_ref[...], down_ref[0], CONTRACT_LAST)
            gate_pre = gate_pre_ref[...]
            sigma = jax.nn.sigmoid(gate_pre)
            slope = sigma * (1.0 + gate_pre * (1.0 - sigma))
            gate_grad_ref[...] = (hidden_grad * up_pre_ref[...] * slope).astype(jnp.bfloat16)
            up_grad_ref[...] = (hidden_grad * gate_pre * sigma).astype(jnp.bfloat16)

    down_spec = pl.BlockSpec((1, FF_TILE, width), lambda i, p: (0, tile_at(i), 0))
    tile_spec = pl.BlockSpec((rows, FF_TILE), lambda i, p: (0, tile_at(i)))
    return run(
        kernel,
        2 * PLANE + ff // FF_TILE,
        cot_specs(cots) + [down_spec] + [tile_spec] * 2,
        [tile_spec] * 2,
        [jax.ShapeDtypeStruct((rows, ff), jnp.bfloat16)] * 2,
        [pltpu.VMEM((rows, width), jnp.bfloat16)],
        2 * rows * width * ff,
        [place, rank, weight, cots, w_down, gate_pre, up_pre],
        earlier,
    )


def body(tokens, cotangent, expert_ids, combine, placement, moves, w_gate, w_up, w_down):
    owner_count = lax.axis_size("expert")
    dp_count = lax.axis_size("dp")
    my_index = lax.axis_index("expert")
    my_dp = lax.axis_index("dp")
    tok_rows, width = tokens.shape
    choose_count = expert_ids.shape[1]
    layers = owner_count // PLANE
    half = layers // 2
    row_count = 3 * tok_rows * choose_count // (4 * PLANE)
    pair = owner_count // 2
    own_layer, my_place = my_index // PLANE, my_index % PLANE
    gathered = layer_gather(tokens, layers)

    layer_ids = jnp.arange(layers, dtype=jnp.int32)
    order = own_layer ^ layer_ids
    routing = jnp.concatenate([expert_ids.astype(jnp.float32), combine], axis=1)
    routing = jnp.stack(layer_gather(routing, layers)).transpose(2, 0, 1)
    routings = [routing] + [crossed(routing, "expert", k) for k in range(1, PLANE)]
    routing = jnp.stack(routings)
    ids, weights = routing[:, :choose_count], routing[:, choose_count:]

    slot_ids = jnp.arange(owner_count, dtype=jnp.int32)
    held = jnp.where(moves == 1, jnp.roll(placement, pair), placement)
    mine = slot_ids == my_index
    home_expert = jnp.sum(jnp.where(mine, placement, 0))
    held_expert = jnp.sum(jnp.where(mine, held, 0))
    my_move = jnp.sum(jnp.where(mine, moves, 0))
    moved = my_move == 1
    place = jnp.stack([my_place, own_layer // half, my_move]).astype(jnp.int32)
    plane_slots = own_layer * PLANE + jnp.arange(PLANE, dtype=jnp.int32)
    near = slot_ids[None, :] == plane_slots[:, None]
    plane_experts = jnp.sum(jnp.where(near, placement[None], 0), axis=1)

    def named(expert, source_ids, source_weights):
        match = source_ids == expert.astype(jnp.float32)
        return jnp.any(match, axis=1), jnp.sum(jnp.where(match, source_weights, 0.0), axis=1)

    sets = [
        named(home_expert, ids, weights),
        named(held_expert, ids, weights),
        named(plane_experts[:, None, None, None], ids[:1], weights[:1]),
    ]
    rank = rank_rows(jnp.concatenate([s[0] for s in sets]), order)
    weight = jnp.concatenate([jnp.broadcast_to(s[1], (PLANE,) + s[1].shape[1:]) for s in sets])

    def halves(array):
        array = array.reshape(len(sets), PLANE, 2, 1, half * tok_rows)
        return array.transpose(0, 2, 1, 3, 4)

    home_rank, held_rank, back_rank = halves(rank)
    back_weight = halves(weight)[2]

    def by_layer(array):
        array = array.reshape(len(sets), PLANE, 2, half, tok_rows)
        return halves(array[:, :, :, layer_ids[:half] ^ (own_layer % half)])

    cot_rank, cot_weight = by_layer(rank), by_layer(weight)

    groups = [[i * PLANE + j for j in range(PLANE)] for i in range(layers)]

    def sent_back(rows):
        rows = rows.reshape(PLANE, 2 * row_count, width)
        return lax.all_to_all(
            rows, "expert", split_axis=0, concat_axis=0, axis_index_groups=groups, tiled=True
        )

    def spread(back, weighted, flag):
        numbers = jnp.arange(row_count, dtype=jnp.int32)[None, None, :, None]
        chosen = (back_rank.transpose(1, 0, 2, 3) == numbers) & flag
        rows = back.reshape(PLANE, 2, row_count, width)
        if weighted:
            weights = back_weight.transpose(1, 0, 2, 3)
            scale = jnp.sum(jnp.where(chosen, weights, 0.0), axis=3, keepdims=True)
            rows = (scale * rows.astype(jnp.float32)).astype(jnp.bfloat16)
        same = jnp.eye(2, dtype=bool)[None, :, None, :, None]
        one_hot = (chosen[:, :, :, None, :] & same).astype(jnp.bfloat16)
        one_hot = one_hot.reshape(2 * PLANE * row_count, layers * tok_rows)
        rows = rows.reshape(2 * PLANE * row_count, width)
        return dot_f32(one_hot, rows, CONTRACT_ROWS).astype(jnp.bfloat16)

    far_tokens = [when(there(True, *routings), block) for block in gathered[half:]]
    token_sides = [plane_gather(gathered[:half]), plane_gather(far_tokens)]
    cots = when(there(True, *[mine[1:] for mine, _ in token_sides]), cotangent)
    cots = lax.all_gather(cots, "expert", axis=0, tiled=True)
    cots = cots.reshape(layers, PLANE, tok_rows, width)
    hidden, *pre = forward(place, home_rank, token_sides, w_gate, w_up, row_count)
    got_hidden = crossed(hidden, "expert", pair)
    out_rows = dot_f32(hidden, w_down[0]).astype(jnp.bfloat16)
    out_back = sent_back(out_rows)
    gate_grad, up_grad = backward(
        place, cot_rank[0], cot_weight[0], cots, w_down, *pre, row_count, [out_rows, got_hidden]
    )
    got_gate_grad = crossed(gate_grad, "expert", pair)
    got_up_grad = crossed(when(there(True, got_gate_grad), up_grad), "expert", pair)
    grad_rows = (
        dot_f32(gate_grad, w_gate[0], CONTRACT_LAST) + dot_f32(up_grad, w_up[0], CONTRACT_LAST)
    ).astype(jnp.bfloat16)
    grad_back = sent_back(grad_rows)
    held_grads = pick_cots(place, cot_rank[1], cot_weight[1], cots, row_count, [grad_rows])
    held_rows = pick_tokens(place, held_rank, token_sides, row_count, [held_grads])

    out_spread = spread(out_back, True, there(True, grad_rows))
    grad_spread = spread(grad_back, False, True)
    out_in, grad_in = [layer_send(a, tok_rows, layers) for a in (out_spread, grad_spread)]
    mixed = layer_reduce(out_spread, out_in, tok_rows, layers, there(True, got_gate_grad))
    input_grad = layer_reduce(grad_spread, grad_in, tok_rows, layers, there(True, got_up_grad))

    def weight_grad(left, own, got, transposed, earlier):
        right = jnp.where(moved & there(True, *earlier), got, own)
        if transposed:
            left, right = right, left
        share = left.shape[1] // dp_count

        def product(part):
            columns = lax.dynamic_slice_in_dim(left, part * share, share, axis=1)
            return dot_f32(columns, right, CONTRACT_ROWS)

        sent = product((my_dp + 1) % dp_count).astype(jnp.bfloat16)
        got = crossed(sent, "dp", 1)
        return got, ((product(my_dp) + got.astype(jnp.float32)) * (1.0 / dp_count))[None]

    _, grad_down = weight_grad(held_grads, hidden, got_hidden, True, [])
    _, grad_gate = weight_grad(held_rows, gate_grad, got_gate_grad, False, [])
    _, grad_up = weight_grad(held_rows, up_grad, got_up_grad, False, [])
    return mixed, input_grad, grad_gate, grad_up, grad_down


def solution(mesh):
    tokens = P(("dp", "expert"), None)
    slots = P("expert", None, None)
    grads = P("expert", "dp", None)
    return jax.shard_map(
        body,
        mesh=mesh,
        in_specs=(tokens, tokens, tokens, tokens, P(), P(), slots, slots, slots),
        out_specs=(tokens, tokens, grads, grads, grads),
        check_vma=False,
    )
```

```python
import jax
import jax.numpy as jnp
from jax import lax
from jax.experimental import pallas as pl
from jax.experimental.pallas import tpu as pltpu
from jax.sharding import PartitionSpec as P

CONTRACT_ROWS = (((0,), (0,)), ((), ()))
CONTRACT_LAST = (((1,), (1,)), ((), ()))
PLANE = 4
FF_TILE = 256
VMEM_BYTES = 48 * 1024 * 1024


def dot_f32(a, b, dims=(((1,), (0,)), ((), ()))):
    return lax.dot_general(a, b, dims, preferred_element_type=jnp.float32)


def crossed(array, axis, flip):
    return lax.ppermute(array, axis, [(i, i ^ flip) for i in range(lax.axis_size(axis))])


def along(array, pairs):
    return lax.ppermute(array, "expert", pairs)


def line_pairs(owner_count):
    inner = [i for i in range(owner_count) if i // PLANE in (1, 2)]
    middle = [(i, i ^ 3 * PLANE) for i in inner]
    outward = [(i, i ^ PLANE) for i in inner]
    inward = [(i ^ PLANE, i) for i in inner]
    return middle, outward, inward


def there(flag, *arrays):
    for array in arrays:
        corner = array[tuple(slice(0, 1) for _ in array.shape)].reshape(())
        flag = flag & (corner == corner)
    return flag


def when(flag, array):
    return jnp.where(flag, array, jnp.zeros((), array.dtype))


def layer_gather(block, layers):
    return [block] + [crossed(block, "expert", j * PLANE) for j in range(1, layers)]


def plane_gather(blocks):
    crossing = [crossed(block, "expert", 2) for block in blocks]
    mine = jnp.stack([jnp.concatenate(blocks), jnp.concatenate(crossing)])
    return mine, crossed(mine, "expert", 1)


def layer_send(spread, tok_rows, layers):
    if layers != 4:
        blocks = [spread[j * tok_rows : (j + 1) * tok_rows] for j in range(1, layers)]
        return [crossed(block, "expert", j * PLANE) for j, block in enumerate(blocks, 1)]
    return [along(spread[tok_rows:], line_pairs(layers * PLANE)[2])]


def layer_reduce(spread, got, tok_rows, layers, flag):
    def total(parts):
        return sum(part.astype(jnp.float32) for part in parts).astype(jnp.bfloat16)

    if layers != 4:
        return total([spread[:tok_rows]] + got)
    middle, outward, _ = line_pairs(layers * PLANE)
    near_in, far_in = got[0][:tok_rows], got[0][tok_rows:]
    far_in = jnp.concatenate([far_in[tok_rows:], far_in[:tok_rows]])
    far_sum = total([spread[2 * tok_rows :], far_in])
    crossing = along(when(flag, far_sum), middle)
    near_sum = total([spread[tok_rows : 2 * tok_rows], crossing[:tok_rows]])
    near_out = along(near_sum, outward)
    return total([spread[:tok_rows], near_in, crossing[tok_rows:], near_out])


def rank_rows(hit, order):
    half = order.shape[0] // 2
    tok_rows = hit.shape[2]
    earlier = jnp.arange(tok_rows)[:, None] < jnp.arange(tok_rows)[None, :]
    within = jnp.einsum(
        "slt,tu->slu",
        hit.astype(jnp.bfloat16),
        earlier.astype(jnp.bfloat16),
        preferred_element_type=jnp.float32,
    ).astype(jnp.int32)
    count = jnp.sum(hit.astype(jnp.int32), axis=2)
    ahead = (order[:, None] < order[None, :]) & (order[:, None] // half == order[None, :] // half)
    before = jnp.sum(jnp.where(ahead[None], count[:, :, None], 0), axis=1)
    return jnp.where(hit, within + before[:, :, None], -1)


def pick_rows(rank, source, row_count):
    place = lax.broadcasted_iota(jnp.int32, (row_count, rank.shape[1]), 0)
    chosen = place == rank
    one_hot = jnp.where(chosen, 1.0, 0.0).astype(jnp.bfloat16)
    return chosen, dot_f32(one_hot, source)


def source_xor(step):
    return (step % PLANE) // 2 + 2 * (step % 2)


def run(kernel, grid, in_specs, out_specs, out_shape, scratch, flops, args, earlier=()):
    moved = sum(a.size * a.dtype.itemsize for a in args)
    count = len(in_specs) + 1
    in_specs = in_specs + [pl.BlockSpec(memory_space=pl.ANY)] * len(earlier)
    if earlier:
        inner_kernel = kernel

        def kernel(*refs):
            inner_kernel(*refs[:count], *refs[count + len(earlier) :])

    return pl.pallas_call(
        kernel,
        grid_spec=pltpu.PrefetchScalarGridSpec(
            num_scalar_prefetch=1,
            grid=(grid,),
            in_specs=in_specs,
            out_specs=out_specs,
            scratch_shapes=scratch,
        ),
        out_shape=out_shape,
        compiler_params=pltpu.CompilerParams(vmem_limit_bytes=VMEM_BYTES),
        cost_estimate=pl.CostEstimate(flops=flops, bytes_accessed=moved, transcendentals=0),
    )(*args, *earlier)


def row_block(side, source):
    return source * 2 + side


def token_specs(sides):
    _, tokens, width = sides[0][0].shape

    def line_at(i, p):
        i = jnp.minimum(i, 2 * PLANE - 1)
        return i // PLANE, source_xor(i), 0, 0

    def source(first):
        return pl.BlockSpec((1, tokens, width), lambda i, p: (jnp.clip(i - first, 0, 1), 0, 0))

    return [pl.BlockSpec((1, 1, 1, tokens), line_at)] + [source(2 * i) for i in range(PLANE)]


def each_source(step, rank_ref, source_refs, store, row_count):
    for i, source_ref in enumerate(source_refs):

        @pl.when(step // 2 == i)
        def _():
            store(pick_rows(rank_ref[0, 0], source_ref[0], row_count)[1].astype(jnp.bfloat16))


def pick_tokens(place, rank, sides, row_count, earlier):
    _, tokens, width = sides[0][0].shape

    def kernel(place_ref, rank_ref, *refs):
        def store(rows):
            refs[PLANE][...] = rows

        each_source(pl.program_id(0), rank_ref, refs[:PLANE], store, row_count)

    def out_at(i, p):
        return row_block((i // PLANE) ^ p[2], p[0] ^ source_xor(i)), 0

    return run(
        kernel,
        2 * PLANE,
        token_specs(sides),
        pl.BlockSpec((row_count, width), out_at),
        jax.ShapeDtypeStruct((2 * PLANE * row_count, width), jnp.bfloat16),
        [],
        4 * PLANE * row_count * tokens * width,
        [place, rank, *sides[0], *sides[1]],
        earlier,
    )


def cot_specs(cots):
    layers, _, tok_rows, width = cots.shape
    tokens = layers // 2 * tok_rows

    def line_at(i, p):
        i = jnp.minimum(i, 2 * PLANE - 1)
        return i // PLANE, (i % PLANE) ^ p[0], 0, 0

    def block_at(i, p):
        i = jnp.minimum(i, 2 * PLANE - 1)
        return (i // PLANE) ^ p[1], i % PLANE, 0, 0

    line = pl.BlockSpec((1, 1, 1, tokens), line_at)
    return [line, line, pl.BlockSpec((layers // 2, 1, tok_rows, width), block_at)]


def scaled_rows(rank_ref, weight_ref, cots_ref, row_count):
    source = cots_ref[...].reshape(-1, cots_ref.shape[-1])
    chosen, rows = pick_rows(rank_ref[0, 0], source, row_count)
    scale = jnp.sum(jnp.where(chosen, weight_ref[0, 0], 0.0), axis=1, keepdims=True)
    return (scale * rows).astype(jnp.bfloat16)


def pick_cots(place, rank, weight, cots, row_count, earlier):
    width = cots.shape[3]

    def kernel(place_ref, rank_ref, weight_ref, cots_ref, rows_ref):
        rows_ref[...] = scaled_rows(rank_ref, weight_ref, cots_ref, row_count)

    def out_at(i, p):
        return row_block((i // PLANE) ^ p[2], i % PLANE), 0

    return run(
        kernel,
        2 * PLANE,
        cot_specs(cots),
        pl.BlockSpec((row_count, width), out_at),
        jax.ShapeDtypeStruct((2 * PLANE * row_count, width), jnp.bfloat16),
        [],
        2 * row_count * cots.size,
        [place, rank, weight, cots],
        earlier,
    )


def tile_at(step):
    return jnp.maximum(step - 2 * PLANE, 0)


def store_rows(block, rows, rows_ref, row_count):
    rows_ref[pl.ds(pl.multiple_of(block * row_count, row_count), row_count), :] = rows


def forward(place, rank, sides, w_gate, w_up, row_count):
    _, tokens, width = sides[0][0].shape
    ff = w_gate.shape[2]
    rows = 2 * PLANE * row_count

    def kernel(place_ref, rank_ref, *refs):
        gate_ref, up_ref, hidden_ref, gate_pre_ref, up_pre_ref, rows_ref = refs[PLANE:]
        step = pl.program_id(0)

        @pl.when(step < 2 * PLANE)
        def _():
            def store(rows):
                block = row_block(step // PLANE, place_ref[0] ^ source_xor(step))
                store_rows(block, rows, rows_ref, row_count)

            each_source(step, rank_ref, refs[:PLANE], store, row_count)

        @pl.when(step >= 2 * PLANE)
        def _():
            gate_pre = dot_f32(rows_ref[...], gate_ref[0])
            up_pre = dot_f32(rows_ref[...], up_ref[0])
            gate_pre_ref[...] = gate_pre
            up_pre_ref[...] = up_pre
            hidden_ref[...] = (gate_pre * jax.nn.sigmoid(gate_pre) * up_pre).astype(jnp.bfloat16)

    weight_spec = pl.BlockSpec((1, width, FF_TILE), lambda i, p: (0, 0, tile_at(i)))
    out_spec = pl.BlockSpec((rows, FF_TILE), lambda i, p: (0, tile_at(i)))
    return run(
        kernel,
        2 * PLANE + ff // FF_TILE,
        token_specs(sides) + [weight_spec] * 2,
        [out_spec] * 3,
        [jax.ShapeDtypeStruct((rows, ff), t) for t in (jnp.bfloat16, jnp.float32, jnp.float32)],
        [pltpu.VMEM((rows, width), jnp.bfloat16)],
        4 * rows * width * ff,
        [place, rank, *sides[0], *sides[1], w_gate, w_up],
    )


def backward(place, rank, weight, cots, w_down, gate_pre, up_pre, row_count, earlier):
    width = cots.shape[3]
    ff = w_down.shape[1]
    rows = 2 * PLANE * row_count

    def kernel(place_ref, rank_ref, weight_ref, cots_ref, down_ref, *refs):
        gate_pre_ref, up_pre_ref, gate_grad_ref, up_grad_ref, rows_ref = refs
        step = pl.program_id(0)

        @pl.when(step < 2 * PLANE)
        def _():
            block = row_block(step // PLANE, step % PLANE)
            rows = scaled_rows(rank_ref, weight_ref, cots_ref, row_count)
            store_rows(block, rows, rows_ref, row_count)

        @pl.when(step >= 2 * PLANE)
        def _():
            hidden_grad = dot_f32(rows_ref[...], down_ref[0], CONTRACT_LAST)
            gate_pre = gate_pre_ref[...]
            sigma = jax.nn.sigmoid(gate_pre)
            slope = sigma * (1.0 + gate_pre * (1.0 - sigma))
            gate_grad_ref[...] = (hidden_grad * up_pre_ref[...] * slope).astype(jnp.bfloat16)
            up_grad_ref[...] = (hidden_grad * gate_pre * sigma).astype(jnp.bfloat16)

    down_spec = pl.BlockSpec((1, FF_TILE, width), lambda i, p: (0, tile_at(i), 0))
    tile_spec = pl.BlockSpec((rows, FF_TILE), lambda i, p: (0, tile_at(i)))
    return run(
        kernel,
        2 * PLANE + ff // FF_TILE,
        cot_specs(cots) + [down_spec] + [tile_spec] * 2,
        [tile_spec] * 2,
        [jax.ShapeDtypeStruct((rows, ff), jnp.bfloat16)] * 2,
        [pltpu.VMEM((rows, width), jnp.bfloat16)],
        2 * rows * width * ff,
        [place, rank, weight, cots, w_down, gate_pre, up_pre],
        earlier,
    )


def body(tokens, cotangent, expert_ids, combine, placement, moves, w_gate, w_up, w_down):
    owner_count = lax.axis_size("expert")
    dp_count = lax.axis_size("dp")
    my_index = lax.axis_index("expert")
    my_dp = lax.axis_index("dp")
    tok_rows, width = tokens.shape
    choose_count = expert_ids.shape[1]
    layers = owner_count // PLANE
    half = layers // 2
    row_count = 3 * tok_rows * choose_count // (4 * PLANE)
    pair = owner_count // 2
    own_layer, my_place = my_index // PLANE, my_index % PLANE
    gathered = layer_gather(tokens, layers)
    cots = lax.all_gather(cotangent, "expert", axis=0, tiled=True)
    cots = cots.reshape(layers, PLANE, tok_rows, width)

    layer_ids = jnp.arange(layers, dtype=jnp.int32)
    order = own_layer ^ layer_ids
    routing = jnp.concatenate([expert_ids.astype(jnp.float32), combine], axis=1)
    routing = jnp.stack(layer_gather(routing, layers)).transpose(2, 0, 1)
    routings = [routing] + [crossed(routing, "expert", k) for k in range(1, PLANE)]
    routing = jnp.stack(routings)
    ids, weights = routing[:, :choose_count], routing[:, choose_count:]

    slot_ids = jnp.arange(owner_count, dtype=jnp.int32)
    held = jnp.where(moves == 1, jnp.roll(placement, pair), placement)
    mine = slot_ids == my_index
    home_expert = jnp.sum(jnp.where(mine, placement, 0))
    held_expert = jnp.sum(jnp.where(mine, held, 0))
    my_move = jnp.sum(jnp.where(mine, moves, 0))
    moved = my_move == 1
    place = jnp.stack([my_place, own_layer // half, my_move]).astype(jnp.int32)
    plane_slots = own_layer * PLANE + jnp.arange(PLANE, dtype=jnp.int32)
    near = slot_ids[None, :] == plane_slots[:, None]
    plane_experts = jnp.sum(jnp.where(near, placement[None], 0), axis=1)

    def named(expert, source_ids, source_weights):
        match = source_ids == expert.astype(jnp.float32)
        return jnp.any(match, axis=1), jnp.sum(jnp.where(match, source_weights, 0.0), axis=1)

    sets = [
        named(home_expert, ids, weights),
        named(held_expert, ids, weights),
        named(plane_experts[:, None, None, None], ids[:1], weights[:1]),
    ]
    rank = rank_rows(jnp.concatenate([s[0] for s in sets]), order)
    weight = jnp.concatenate([jnp.broadcast_to(s[1], (PLANE,) + s[1].shape[1:]) for s in sets])

    def halves(array):
        array = array.reshape(len(sets), PLANE, 2, 1, half * tok_rows)
        return array.transpose(0, 2, 1, 3, 4)

    home_rank, held_rank, back_rank = halves(rank)
    back_weight = halves(weight)[2]

    def by_layer(array):
        array = array.reshape(len(sets), PLANE, 2, half, tok_rows)
        return halves(array[:, :, :, layer_ids[:half] ^ (own_layer % half)])

    cot_rank, cot_weight = by_layer(rank), by_layer(weight)

    groups = [[i * PLANE + j for j in range(PLANE)] for i in range(layers)]

    def sent_back(rows):
        rows = rows.reshape(PLANE, 2 * row_count, width)
        return lax.all_to_all(
            rows, "expert", split_axis=0, concat_axis=0, axis_index_groups=groups, tiled=True
        )

    def spread(back, weighted, flag):
        numbers = jnp.arange(row_count, dtype=jnp.int32)[None, None, :, None]
        chosen = (back_rank.transpose(1, 0, 2, 3) == numbers) & flag
        rows = back.reshape(PLANE, 2, row_count, width)
        if weighted:
            weights = back_weight.transpose(1, 0, 2, 3)
            scale = jnp.sum(jnp.where(chosen, weights, 0.0), axis=3, keepdims=True)
            rows = (scale * rows.astype(jnp.float32)).astype(jnp.bfloat16)
        same = jnp.eye(2, dtype=bool)[None, :, None, :, None]
        one_hot = (chosen[:, :, :, None, :] & same).astype(jnp.bfloat16)
        one_hot = one_hot.reshape(2 * PLANE * row_count, layers * tok_rows)
        rows = rows.reshape(2 * PLANE * row_count, width)
        return dot_f32(one_hot, rows, CONTRACT_ROWS).astype(jnp.bfloat16)

    far_tokens = [when(there(True, *routings), block) for block in gathered[half:]]
    token_sides = [plane_gather(gathered[:half]), plane_gather(far_tokens)]
    hidden, *pre = forward(place, home_rank, token_sides, w_gate, w_up, row_count)
    got_hidden = crossed(hidden, "expert", pair)
    out_rows = dot_f32(hidden, w_down[0]).astype(jnp.bfloat16)
    out_back = sent_back(out_rows)
    gate_grad, up_grad = backward(
        place, cot_rank[0], cot_weight[0], cots, w_down, *pre, row_count, [out_rows, got_hidden]
    )
    got_gate_grad = crossed(gate_grad, "expert", pair)
    got_up_grad = crossed(when(there(True, got_gate_grad), up_grad), "expert", pair)
    grad_rows = (
        dot_f32(gate_grad, w_gate[0], CONTRACT_LAST) + dot_f32(up_grad, w_up[0], CONTRACT_LAST)
    ).astype(jnp.bfloat16)
    grad_back = sent_back(grad_rows)
    held_grads = pick_cots(place, cot_rank[1], cot_weight[1], cots, row_count, [grad_rows])
    held_rows = pick_tokens(place, held_rank, token_sides, row_count, [held_grads])

    out_spread = spread(out_back, True, there(True, grad_rows))
    grad_spread = spread(grad_back, False, True)
    out_in, grad_in = [layer_send(a, tok_rows, layers) for a in (out_spread, grad_spread)]
    mixed = layer_reduce(out_spread, out_in, tok_rows, layers, there(True, got_gate_grad))
    input_grad = layer_reduce(grad_spread, grad_in, tok_rows, layers, there(True, got_up_grad))

    def weight_grad(left, own, got, transposed, earlier):
        right = jnp.where(moved & there(True, *earlier), got, own)
        if transposed:
            left, right = right, left
        share = left.shape[1] // dp_count

        def product(part):
            columns = lax.dynamic_slice_in_dim(left, part * share, share, axis=1)
            return dot_f32(columns, right, CONTRACT_ROWS)

        sent = product((my_dp + 1) % dp_count).astype(jnp.bfloat16)
        got = crossed(sent, "dp", 1)
        return got, ((product(my_dp) + got.astype(jnp.float32)) * (1.0 / dp_count))[None]

    _, grad_down = weight_grad(held_grads, hidden, got_hidden, True, [])
    _, grad_gate = weight_grad(held_rows, gate_grad, got_gate_grad, False, [])
    _, grad_up = weight_grad(held_rows, up_grad, got_up_grad, False, [])
    return mixed, input_grad, grad_gate, grad_up, grad_down


def solution(mesh):
    tokens = P(("dp", "expert"), None)
    slots = P("expert", None, None)
    grads = P("expert", "dp", None)
    return jax.shard_map(
        body,
        mesh=mesh,
        in_specs=(tokens, tokens, tokens, tokens, P(), P(), slots, slots, slots),
        out_specs=(tokens, tokens, grads, grads, grads),
        check_vma=False,
    )
```
